128 devices in a mesh: row: 4 (over x), col: 8 (over z, core), depth: 4 (over y).
Axes of the slice: x: 4, y: 4, z: 4, core: 2. Of those that a mesh axis runs over, the one named last changes fastest.
Arguments:
- x_in: bfloat16 [4096, 4096], P('row', ('col', 'depth')), may hold values from -1.5 to 1.5
- patterns: int32 [7, 32, 32], replicated, may hold values from 0 to 1, as said below
Outputs:
- sign_matrix: bfloat16 [4096, 4096], P('row', ('col', 'depth'))
The draws below stay inside these ranges and needn't reach their ends.
Inputs may be any that keep to these rules, and one draw needn't show every extreme that they name: `patterns`: block (i, j) of every pattern is 1 where i and j are at most one apart, cyclically over 32 blocks.
All inputs are finite; a program needn't handle non-finite values.
Results may differ from the reference program's by a relative error of at most 0.0038.
The reference program's roundings to bfloat16 on the way (of `current` and `squared`) count: a program that leaves them out, or rounds other values in their place, can miss the bound.
Values may be sent and summed in bfloat16 or wider, within the bound.
No kernel may reach another device: no remote copies, remote signals or barrier semaphores. Data moves between devices by JAX's collectives and lax.ppermute only.
A program may use at most 64 MiB of HBM per device.

```python
import jax
import jax.numpy as jnp
from jax import lax

BLOCK = 128
ITERS = 3
NB = 32
PATS = 7


def draw_patterns(key, part):
    key = jax.random.fold_in(key, 11)
    key_level, key_roll = jax.random.split(key)
    indices = jnp.arange(NB)
    spread = jnp.abs(indices[:, None] - indices[None, :])
    cyclic = jnp.minimum(spread, NB - spread)
    levels = jax.random.randint(key_level, (PATS, NB, 1), 0, 4)
    rolled = jax.random.randint(key_roll, (PATS, NB, NB), 0, 8)
    chosen = (cyclic <= 1)[None, :, :] | (rolled < levels)
    return jnp.where(chosen, 1, 0).astype(jnp.int32)


def draw_x_in(key, part):
    key = jax.random.fold_in(key, 23)
    key_off, key_mag, key_sign = jax.random.split(key, 3)
    order = NB * BLOCK
    factor = 1.2 * float(order) ** (-0.5)
    off_part = jnp.clip(jax.random.normal(key_off, (order, order), jnp.float32), -4.0, 4.0)
    magnitude = jax.random.uniform(key_mag, (order,), jnp.float32, 0.4, 1.0)
    signs = jnp.where(jax.random.normal(key_sign, (order,), jnp.float32) < 0.0, -1.0, 1.0)
    indices = jnp.arange(order)
    diagonal_mask = indices[:, None] == indices[None, :]
    values = jnp.where(diagonal_mask, (signs * magnitude)[:, None], off_part * factor)
    return values.astype(jnp.bfloat16)


def setup_inputs(seed: int = 0) -> dict:
    key_of = jax.random.split(jax.random.key(seed), 3)
    x_in = draw_x_in(jax.random.fold_in(key_of[2], 71), 0)
    patterns = draw_patterns(jax.random.fold_in(key_of[2], 71), 0)
    return dict(x_in=x_in, patterns=patterns)


def expand(pattern, values):
    blocks = pattern.shape[0]
    order = values.shape[0]
    width = order // blocks
    shaped = values.reshape(blocks, width, blocks, width).astype(jnp.float32)
    return (shaped * pattern.astype(jnp.float32)[:, None, :, None]).reshape(order, order)


def multiply(left_side, right_side):
    return jnp.dot(left_side.astype(jnp.float32), right_side.astype(jnp.float32), precision=lax.Precision.HIGHEST)


def reference(x_in, patterns):
    current = expand(patterns[0], x_in).astype(jnp.bfloat16)
    for iteration in range(ITERS):
        squared = expand(patterns[2 * iteration + 1], multiply(current, current)).astype(jnp.bfloat16)
        cubed_terms = multiply(current, squared)
        update = 1.5 * current.astype(jnp.float32) - 0.5 * cubed_terms
        current = expand(patterns[2 * iteration + 2], update).astype(jnp.bfloat16)
    return current
```

```python
import functools

import jax
import jax.numpy as jnp
from jax import lax
from jax.experimental import pallas as pl
from jax.experimental.pallas import tpu as pltpu
from jax.sharding import PartitionSpec as P

BLOCK = 128
ITERS = 3
NB = 32
AXES = ("row", "col", "depth")

GROUP_CAP = 28
GROUPS = 16
CAP = 400
ZERO = GROUPS * GROUP_CAP
DUMMY = ZERO + 1
TILE = DUMMY + 1
S_BASE = TILE + 8
X_BASE = S_BASE + CAP
SLOTS = X_BASE + CAP
TERMS = 16
POSITIONS = 512
ROWS = 1032
CLASSES = ((1, 16), (2, 8), (3, 5), (4, 4), (8, 2))
STEPS = 2 * ITERS


def pack_kernel(pick_ref, in_ref, out_ref):
    for p in range(GROUP_CAP):
        out_ref[p] = in_ref[pick_ref[p]]


def product_kernel(ent_ref, ox_ref, ord_ref, body_ref, start_ref, out_ref, blocks, sem):
    for z in range(4):
        for d in range(4):
            g = z * 4 + d
            for r in range(4):
                for k in range(2):
                    pltpu.make_async_copy(
                        start_ref.at[r, z, k, d],
                        blocks.at[pl.ds(g * GROUP_CAP, GROUP_CAP), r * 2 + k],
                        sem,
                    ).start()
    blocks[ZERO] = jnp.zeros(blocks.shape[1:], blocks.dtype)
    for b in range(8):
        blocks[TILE + b] = jnp.zeros(blocks.shape[1:], blocks.dtype)
    whole = blocks.at[pl.ds(0, ZERO)]
    pltpu.make_async_copy(whole, whole, sem).wait()

    def load(slot):
        return blocks[slot].reshape(BLOCK, BLOCK)

    def step(t, carry):
        is_update = (t & 1) == 1
        keep = jnp.where(is_update, 1.5, 0.0).astype(jnp.float32)
        scale = jnp.where(is_update, -0.5, 1.0).astype(jnp.float32)
        for index, (pairs, width) in enumerate(CLASSES):
            first = body_ref[t * 16 + index * 2]
            count = body_ref[t * 16 + index * 2 + 1]

            def body(it, carry, pairs=pairs, width=width, first=first):
                results = []
                for u in range(width):
                    entry = ord_ref[t * POSITIONS + first + it * width + u]
                    at = (t * ROWS + entry) * TERMS
                    total = None
                    for q in range(pairs):
                        w1 = ent_ref[at + 2 * q]
                        w2 = ent_ref[at + 2 * q + 1]
                        left = jnp.concatenate([load(w1 & 0xFFFF), load(w2 & 0xFFFF)], axis=1)
                        right = jnp.concatenate([load(w1 >> 16), load(w2 >> 16)], axis=0)
                        term = jnp.dot(left, right, preferred_element_type=jnp.float32)
                        total = term if total is None else total + term
                    ox = ox_ref[t * ROWS + entry]
                    old = load(ox >> 16).astype(jnp.float32)
                    results.append((ox & 0xFFFF, (keep * old + scale * total).astype(jnp.bfloat16)))
                for slot, value in results:
                    blocks[slot] = value.reshape(blocks.shape[1:])
                return carry

            lax.fori_loop(0, count, body, 0)
        return carry

    lax.fori_loop(0, STEPS, step, 0)
    copy = pltpu.make_async_copy(blocks.at[pl.ds(TILE, 8)], out_ref, sem)
    copy.start()
    copy.wait()


def ranks(mask):
    n = mask.shape[-1]
    before = (lax.iota(jnp.int32, n)[:, None] < lax.iota(jnp.int32, n)[None, :]).astype(jnp.bfloat16)
    flat = mask.reshape(-1, n).astype(jnp.bfloat16)
    return jnp.dot(flat, before, preferred_element_type=jnp.float32).astype(jnp.int32).reshape(mask.shape)


def group_order(pattern):
    return pattern.reshape(4, 8, 4, 2, 4).transpose(2, 4, 0, 3, 1).reshape(GROUPS, 64)


def fits(patterns):
    groups = group_order(patterns[0]).sum(-1).max()
    counts = patterns[1 : 2 * ITERS - 1].sum((1, 2)).max()
    f = patterns.astype(jnp.bfloat16)
    left = f[0 : 2 * ITERS].at[1::2].set(f[0 : 2 * ITERS : 2])
    right = f[0 : 2 * ITERS]
    terms = jnp.einsum("tik,tkj->tij", left, right, preferred_element_type=jnp.float32)
    most = (terms * patterns[1:].astype(jnp.float32)).max()
    return (groups <= GROUP_CAP) & (counts <= CAP) & (most <= TERMS)


def tables(patterns):
    row, col, depth = (lax.axis_index(a) for a in AXES)
    me_col = col * 4 + depth
    i = lax.iota(jnp.int32, NB)[:, None]
    j = lax.iota(jnp.int32, NB)[None, :]
    mine = (j == me_col).astype(jnp.int32)
    tile = mine * ((i // 8) == row).astype(jnp.int32)
    outs = jnp.concatenate([patterns[1:5], patterns[5:6] * mine, patterns[6:7] * tile])

    order = group_order(patterns[0])
    in_group = ranks(order)
    slot0 = lax.iota(jnp.int32, GROUPS)[:, None] * GROUP_CAP + in_group
    slot0 = slot0.reshape(4, 4, 4, 2, 8).transpose(2, 4, 0, 3, 1).reshape(NB, NB)
    slot0 = jnp.where(patterns[0] > 0, slot0, ZERO)
    linear = ranks(outs.reshape(STEPS, NB * NB)).reshape(STEPS, NB, NB)
    base = jnp.array([S_BASE, X_BASE, S_BASE, 0, S_BASE, 0], jnp.int32)[:, None, None]
    out_slot = linear + base
    out_slot = jnp.concatenate([out_slot[:5], jnp.broadcast_to(TILE + i - 8 * row, (1, NB, NB))])
    read_slot = jnp.where(outs > 0, out_slot, ZERO)
    x_slot = jnp.stack([slot0, read_slot[1], read_slot[3]])
    left = jnp.repeat(x_slot, 2, axis=0)
    right = jnp.stack([slot0, read_slot[0], read_slot[1], read_slot[2], read_slot[3], read_slot[4]])
    old = jnp.where((lax.iota(jnp.int32, STEPS) % 2 == 1)[:, None, None], left, ZERO)
    left_on = left != ZERO
    right_on = right != ZERO

    on = (outs > 0)[:, :, :, None] & left_on[:, :, None, :] & right_on.transpose(0, 2, 1)[:, None, :, :]
    place = ranks(on.astype(jnp.int32))
    word = left[:, :, None, :] + right.transpose(0, 2, 1)[:, None, :, :] * 65536
    blank = ZERO + ZERO * 65536
    place = jnp.where(on, place, TERMS)
    hit = place[..., None, :] == lax.iota(jnp.int32, TERMS)[:, None]
    ent = jnp.where(hit, word[..., None, :] - blank, 0).sum(-1) + blank
    ent = ent.reshape(STEPS, NB * NB, TERMS)
    ent = jnp.pad(ent, ((0, 0), (0, ROWS - NB * NB), (0, 0)), constant_values=blank)

    ox = (out_slot + old * 65536).reshape(STEPS, NB * NB)
    ox = jnp.pad(ox, ((0, 0), (0, ROWS - NB * NB)), constant_values=DUMMY + ZERO * 65536)

    count = on.astype(jnp.int32).sum(-1).reshape(STEPS, NB * NB)
    pairs = jnp.maximum((count + 1) // 2, 1)
    live = outs.reshape(STEPS, NB * NB) > 0
    low = 0
    members = []
    for limit, _ in CLASSES:
        members.append(live & (pairs > low) & (pairs <= limit))
        low = limit
    member = jnp.stack(members, 1).astype(jnp.int32)
    rank = ranks(member)
    total = member.sum(-1)
    widths = jnp.array([w for _, w in CLASSES], jnp.int32)
    bodies = (total + widths - 1) // widths
    firsts = jnp.cumsum(bodies * widths, axis=1) - bodies * widths
    position = jnp.where(member > 0, rank + firsts[:, :, None], 0).sum(1)
    position = jnp.where(live, position, POSITIONS)
    match = position[:, None, :] == lax.iota(jnp.int32, POSITIONS)[None, :, None]
    entry = jnp.where(match, lax.iota(jnp.int32, NB * NB) - NB * NB, 0).sum(-1) + NB * NB
    body = jnp.stack([firsts, bodies], -1).reshape(STEPS, 2 * len(CLASSES))
    body = jnp.pad(body, ((0, 0), (0, 16 - 2 * len(CLASSES))))
    return ent.reshape(-1), ox.reshape(-1), entry.reshape(-1), body.reshape(-1)


def sparse_path(slices, patterns):
    _, col, depth = (lax.axis_index(a) for a in AXES)
    order = lax.dynamic_index_in_dim(group_order(patterns[0]), (col // 2) * 4 + depth, 0, keepdims=False)
    place = jnp.where(order > 0, ranks(order[None])[0], GROUP_CAP)
    hit = place[None, :] == lax.iota(jnp.int32, GROUP_CAP)[:, None]
    pick = jnp.where(hit, lax.iota(jnp.int32, 64)[None, :], 0).sum(-1)
    packed = pl.pallas_call(
        pack_kernel,
        out_shape=jax.ShapeDtypeStruct((GROUP_CAP, 16, BLOCK), jnp.bfloat16),
        in_specs=[pl.BlockSpec(memory_space=pltpu.SMEM), pl.BlockSpec(memory_space=pltpu.VMEM)],
        out_specs=pl.BlockSpec(memory_space=pltpu.VMEM),
        name="pack_blocks",
    )(pick, slices)
    start = lax.all_gather(packed, AXES, axis=0, tiled=True)
    start = start.reshape(4, 4, 2, 4, GROUP_CAP, 16, BLOCK)
    ent, ox, entry, body = tables(patterns)
    smem = pl.BlockSpec(memory_space=pltpu.SMEM)
    out = pl.pallas_call(
        product_kernel,
        out_shape=jax.ShapeDtypeStruct((8, 8, 16, BLOCK), jnp.bfloat16),
        in_specs=[smem, smem, smem, smem, pl.BlockSpec(memory_space=pl.ANY)],
        out_specs=pl.BlockSpec(memory_space=pl.ANY),
        scratch_shapes=[pltpu.VMEM((SLOTS, 8, 16, BLOCK), jnp.bfloat16), pltpu.SemaphoreType.DMA(())],
        compiler_params=pltpu.CompilerParams(vmem_limit_bytes=56 * 2**20),
        name="block_products",
    )(ent, ox, entry, body, start)
    return out.reshape(8 * BLOCK, BLOCK)


def tile_mask(pattern, row_first, col_first, tile_rows, tile_cols):
    blocks = pattern.shape[0]
    slab = lax.dynamic_slice_in_dim(pattern, row_first // BLOCK, tile_rows // BLOCK, 0).astype(jnp.float32)
    col_block = (col_first + lax.iota(jnp.int32, tile_cols)) // BLOCK
    onehot = (col_block[None, :] == lax.iota(jnp.int32, blocks)[:, None]).astype(jnp.float32)
    coarse = jnp.dot(slab, onehot)
    spread_rows = jnp.broadcast_to(coarse[:, None, :], (tile_rows // BLOCK, BLOCK, tile_cols))
    return spread_rows.reshape(tile_rows, tile_cols)


def dense_path(x_in, patterns):
    tile_rows, tile_width = x_in.shape
    row_first = lax.axis_index("row") * tile_rows
    col_first = (lax.axis_index("col") * lax.axis_size("depth") + lax.axis_index("depth")) * tile_width
    masks = [tile_mask(patterns[p], row_first, col_first, tile_rows, tile_width) for p in range(2 * ITERS + 1)]
    matrix = (x_in * masks[0]).astype(jnp.bfloat16)
    for iteration in range(ITERS):
        panel = lax.all_gather(matrix, ("col", "depth"), axis=1, tiled=True)

        def product(right):
            column = lax.all_gather(right, "row", axis=0, tiled=True)
            return jnp.dot(panel, column, preferred_element_type=jnp.float32)

        squared = (masks[2 * iteration + 1] * product(matrix)).astype(jnp.bfloat16)
        update = 1.5 * matrix.astype(jnp.float32) - 0.5 * product(squared)
        matrix = (masks[2 * iteration + 2] * update).astype(jnp.bfloat16)
    return matrix


def on_device(x_in, patterns):
    groups = [[r * 8 + z * 2 + k for r in range(4) for k in range(2)] for z in range(4)]
    by_slice = x_in.reshape(8, 8, 16, BLOCK).transpose(1, 0, 2, 3)
    slices = lax.all_to_all(by_slice, ("row", "col"), 0, 0, axis_index_groups=groups, tiled=True)
    slices = slices.reshape(64, 16, BLOCK)
    return lax.cond(
        fits(patterns),
        lambda: sparse_path(slices, patterns),
        lambda: dense_path(x_in, patterns),
    )


def solution(mesh):
    placed = (P("row", ("col", "depth")), P())
    return jax.shard_map(
        on_device, mesh=mesh, in_specs=placed, out_specs=P("row", ("col", "depth")), check_vma=False
    )
```

```python
import functools

import jax
import jax.numpy as jnp
from jax import lax
from jax.experimental import pallas as pl
from jax.experimental.pallas import tpu as pltpu
from jax.sharding import PartitionSpec as P

BLOCK = 128
ITERS = 3
NB = 32
AXES = ("row", "col", "depth")

GROUP_CAP = 28
GROUPS = 16
CAP = 400
ZERO = GROUPS * GROUP_CAP
DUMMY = ZERO + 1
TILE = DUMMY + 1
S_BASE = TILE + 8
X_BASE = S_BASE + CAP
SLOTS = X_BASE + CAP
TERMS = 16
POSITIONS = 512
ROWS = 1152
BODY_WORDS = 24
CLASSES = ((16, 2), (8, 8), (6, 10), (5, 12), (4, 16), (3, 20), (2, 32), (1, 32), (0, 16))
STEPS = 2 * ITERS


def pack_kernel(pick_ref, in_ref, out_ref):
    for p in range(GROUP_CAP):
        out_ref[p] = in_ref[pick_ref[p]]


def product_kernel(ent_ref, ox_ref, ord_ref, body_ref, start_ref, out_ref, blocks, sem):
    for z in range(4):
        for d in range(4):
            g = z * 4 + d
            for r in range(4):
                for k in range(2):
                    pltpu.make_async_copy(
                        start_ref.at[r, z, k, d],
                        blocks.at[pl.ds(g * GROUP_CAP, GROUP_CAP), r * 2 + k],
                        sem,
                    ).start()
    blocks[ZERO] = jnp.zeros(blocks.shape[1:], blocks.dtype)
    for b in range(8):
        blocks[TILE + b] = jnp.zeros(blocks.shape[1:], blocks.dtype)
    whole = blocks.at[pl.ds(0, ZERO)]
    pltpu.make_async_copy(whole, whole, sem).wait()

    def load(slot):
        return blocks[slot].reshape(BLOCK, BLOCK)

    def step(t, carry):
        is_update = (t & 1) == 1
        keep = jnp.where(is_update, 1.5, 0.0).astype(jnp.float32)
        scale = jnp.where(is_update, -0.5, 1.0).astype(jnp.float32)
        for index, (terms, width) in enumerate(CLASSES):
            first = body_ref[t * BODY_WORDS + index * 2]
            count = body_ref[t * BODY_WORDS + index * 2 + 1]

            def body(it, carry, terms=terms, width=width, first=first):
                results = []
                for u in range(width):
                    entry = ord_ref[t * POSITIONS + first + it * width + u]
                    at = t * (TERMS * ROWS) + entry
                    words = [ent_ref[at + q * ROWS] for q in range(terms)]
                    lefts = [load(w & 0xFFFF) for w in words]
                    rights = [load(w >> 16) for w in words]
                    total = jnp.zeros((BLOCK, BLOCK), jnp.float32)
                    if terms == 1:
                        total = jnp.dot(lefts[0], rights[0], preferred_element_type=jnp.float32)
                    elif terms > 1:
                        left = jnp.concatenate(lefts, axis=1)
                        right = jnp.concatenate(rights, axis=0)
                        total = jnp.dot(left, right, preferred_element_type=jnp.float32)
                    ox = ox_ref[t * ROWS + entry]
                    old = load(ox >> 16).astype(jnp.float32)
                    results.append((ox & 0xFFFF, (keep * old + scale * total).astype(jnp.bfloat16)))
                for slot, value in results:
                    blocks[slot] = value.reshape(blocks.shape[1:])
                return carry

            lax.fori_loop(0, count, body, 0)
        return carry

    lax.fori_loop(0, STEPS, step, 0)
    copy = pltpu.make_async_copy(blocks.at[pl.ds(TILE, 8)], out_ref, sem)
    copy.start()
    copy.wait()


def ranks(mask):
    n = mask.shape[-1]
    before = (lax.iota(jnp.int32, n)[:, None] < lax.iota(jnp.int32, n)[None, :]).astype(jnp.bfloat16)
    flat = mask.reshape(-1, n).astype(jnp.bfloat16)
    return jnp.dot(flat, before, preferred_element_type=jnp.float32).astype(jnp.int32).reshape(mask.shape)


def group_order(pattern):
    return pattern.reshape(4, 8, 4, 2, 4).transpose(2, 4, 0, 3, 1).reshape(GROUPS, 64)


def fits(patterns):
    groups = group_order(patterns[0]).sum(-1).max()
    counts = patterns[1 : 2 * ITERS - 1].sum((1, 2)).max()
    f = patterns.astype(jnp.bfloat16)
    left = f[0 : 2 * ITERS].at[1::2].set(f[0 : 2 * ITERS : 2])
    right = f[0 : 2 * ITERS]
    terms = jnp.einsum("tik,tkj->tij", left, right, preferred_element_type=jnp.float32)
    most = (terms * patterns[1:].astype(jnp.float32)).max()
    return (groups <= GROUP_CAP) & (counts <= CAP) & (most <= TERMS)


def tables(patterns):
    row, col, depth = (lax.axis_index(a) for a in AXES)
    me_col = col * 4 + depth
    i = lax.iota(jnp.int32, NB)[:, None]
    j = lax.iota(jnp.int32, NB)[None, :]
    mine = (j == me_col).astype(jnp.int32)
    tile = mine * ((i // 8) == row).astype(jnp.int32)
    outs = jnp.concatenate([patterns[1:5], patterns[5:6] * mine, patterns[6:7] * tile])

    in_group = ranks(group_order(patterns[0]))
    slot0 = lax.iota(jnp.int32, GROUPS)[:, None] * GROUP_CAP + in_group
    slot0 = slot0.reshape(4, 4, 4, 2, 8).transpose(2, 4, 0, 3, 1).reshape(NB, NB)
    slot0 = jnp.where(patterns[0] > 0, slot0, ZERO)
    base = jnp.array([S_BASE, X_BASE, S_BASE, 0, S_BASE, 0], jnp.int32)[:, None]
    live = outs.reshape(STEPS, NB * NB) > 0
    out_slot = ranks(outs.reshape(STEPS, NB * NB)) + base
    in_tile = jnp.broadcast_to(TILE + i - 8 * row, (NB, NB)).reshape(1, NB * NB)
    out_slot = jnp.concatenate([out_slot[:5], in_tile])
    read_slot = jnp.where(live, out_slot, ZERO).reshape(STEPS, NB, NB)
    x_slot = jnp.stack([slot0, read_slot[1], read_slot[3]])
    left = jnp.repeat(x_slot, 2, axis=0)
    right = jnp.stack([slot0, read_slot[0], read_slot[1], read_slot[2], read_slot[3], read_slot[4]])
    old = jnp.where((lax.iota(jnp.int32, STEPS) % 2 == 1)[:, None, None], left, ZERO)

    o = lax.iota(jnp.int32, NB * NB)[None, :]
    of_row = (o // NB == i).astype(jnp.float32)
    of_col = (o % NB == i).astype(jnp.float32)
    spread = functools.partial(jnp.dot, precision=lax.Precision.HIGHEST, preferred_element_type=jnp.float32)
    wide_left = spread(left.transpose(0, 2, 1).astype(jnp.float32), of_row).astype(jnp.int32)
    wide_right = spread(right.astype(jnp.float32), of_col).astype(jnp.int32)
    on = live[:, None, :] & (wide_left != ZERO) & (wide_right != ZERO)
    before = (i > j).astype(jnp.bfloat16)
    place = jnp.einsum("kl,tlo->tko", before, on.astype(jnp.bfloat16), preferred_element_type=jnp.float32)
    blank = ZERO + ZERO * 65536
    word = jnp.where(on, wide_left + wide_right * 65536 - blank, 0)
    place = jnp.where(on, place.astype(jnp.int32), TERMS)
    hit = place[:, None] == lax.iota(jnp.int32, TERMS)[None, :, None, None]
    ent = jnp.where(hit, word[:, None], 0).sum(2) + blank
    ent = jnp.pad(ent, ((0, 0), (0, 0), (0, ROWS - NB * NB)), constant_values=blank)

    ox = out_slot + old.reshape(STEPS, NB * NB) * 65536
    ox = jnp.pad(ox, ((0, 0), (0, ROWS - NB * NB)), constant_values=DUMMY + ZERO * 65536)

    count = on.astype(jnp.int32).sum(1)
    members = []
    for (limit, _), low in zip(CLASSES, [limit for limit, _ in CLASSES[1:]] + [-1]):
        members.append(live & (count > low) & (count <= limit))
    member = jnp.stack(members, 1).astype(jnp.int32)
    rank = ranks(member)
    total = member.sum(-1)
    passed = [jnp.zeros((STEPS,), jnp.int32)]
    for index in range(len(CLASSES)):
        passed.append(passed[-1] + total[:, index])
    ahead = jnp.stack(passed[:-1], 1)
    position = jnp.where(member > 0, rank + ahead[:, :, None], 0).sum(1)
    position = jnp.where(live, position, POSITIONS)
    match = position[:, None, :] == lax.iota(jnp.int32, POSITIONS)[None, :, None]
    entry = jnp.where(match, o[None] - NB * NB, 0).sum(-1) + NB * NB
    end = jnp.zeros((STEPS,), jnp.int32)
    body = []
    for index, (_, width) in enumerate(CLASSES):
        bodies = jnp.maximum((passed[index + 1] - end + width - 1) // width, 0)
        body += [end, bodies]
        end = end + bodies * width
    body = jnp.stack(body + [end] * (BODY_WORDS - len(body)), 1)
    return ent.reshape(-1), ox.reshape(-1), entry.reshape(-1), body.reshape(-1)


def pick_places(patterns):
    _, col, depth = (lax.axis_index(a) for a in AXES)
    order = lax.dynamic_index_in_dim(group_order(patterns[0]), (col // 2) * 4 + depth, 0, keepdims=False)
    place = jnp.where(order > 0, ranks(order[None])[0], GROUP_CAP)
    hit = place[None, :] == lax.iota(jnp.int32, GROUP_CAP)[:, None]
    return jnp.where(hit, lax.iota(jnp.int32, 64)[None, :], 0).sum(-1)


def pack(pick, slices):
    return pl.pallas_call(
        pack_kernel,
        out_shape=jax.ShapeDtypeStruct((GROUP_CAP, 16, BLOCK), jnp.bfloat16),
        in_specs=[pl.BlockSpec(memory_space=pltpu.SMEM), pl.BlockSpec(memory_space=pltpu.VMEM)],
        out_specs=pl.BlockSpec(memory_space=pltpu.VMEM),
        name="pack_blocks",
    )(pick, slices)


def sparse_path(ent, ox, entry, body, start):
    smem = pl.BlockSpec(memory_space=pltpu.SMEM)
    out = pl.pallas_call(
        product_kernel,
        out_shape=jax.ShapeDtypeStruct((8, 8, 16, BLOCK), jnp.bfloat16),
        in_specs=[smem, smem, smem, smem, pl.BlockSpec(memory_space=pl.ANY)],
        out_specs=pl.BlockSpec(memory_space=pl.ANY),
        scratch_shapes=[pltpu.VMEM((SLOTS, 8, 16, BLOCK), jnp.bfloat16), pltpu.SemaphoreType.DMA(())],
        compiler_params=pltpu.CompilerParams(vmem_limit_bytes=56 * 2**20),
        name="block_products",
    )(ent, ox, entry, body, start)
    return out.reshape(8 * BLOCK, BLOCK)


def tile_mask(pattern, row_first, col_first, tile_rows, tile_cols):
    blocks = pattern.shape[0]
    slab = lax.dynamic_slice_in_dim(pattern, row_first // BLOCK, tile_rows // BLOCK, 0).astype(jnp.float32)
    col_block = (col_first + lax.iota(jnp.int32, tile_cols)) // BLOCK
    onehot = (col_block[None, :] == lax.iota(jnp.int32, blocks)[:, None]).astype(jnp.float32)
    coarse = jnp.dot(slab, onehot)
    spread_rows = jnp.broadcast_to(coarse[:, None, :], (tile_rows // BLOCK, BLOCK, tile_cols))
    return spread_rows.reshape(tile_rows, tile_cols)


def dense_path(x_in, patterns):
    tile_rows, tile_width = x_in.shape
    row_first = lax.axis_index("row") * tile_rows
    col_first = (lax.axis_index("col") * lax.axis_size("depth") + lax.axis_index("depth")) * tile_width
    masks = [tile_mask(patterns[p], row_first, col_first, tile_rows, tile_width) for p in range(2 * ITERS + 1)]
    matrix = (x_in * masks[0]).astype(jnp.bfloat16)
    for iteration in range(ITERS):
        panel = lax.all_gather(matrix, ("col", "depth"), axis=1, tiled=True)

        def product(right):
            column = lax.all_gather(right, "row", axis=0, tiled=True)
            return jnp.dot(panel, column, preferred_element_type=jnp.float32)

        squared = (masks[2 * iteration + 1] * product(matrix)).astype(jnp.bfloat16)
        update = 1.5 * matrix.astype(jnp.float32) - 0.5 * product(squared)
        matrix = (masks[2 * iteration + 2] * update).astype(jnp.bfloat16)
    return matrix


def on_device(x_in, patterns):
    groups = [[r * 8 + z * 2 + k for r in range(4) for k in range(2)] for z in range(4)]
    by_slice = x_in.reshape(8, 8, 16, BLOCK).transpose(1, 0, 2, 3)
    slices = lax.all_to_all(by_slice, ("row", "col"), 0, 0, axis_index_groups=groups, tiled=True)
    slices = slices.reshape(64, 16, BLOCK)
    packed = pack(pick_places(patterns), slices)
    start = lax.all_gather(packed, AXES, axis=0, tiled=True)
    start = start.reshape(4, 4, 2, 4, GROUP_CAP, 16, BLOCK)
    lists = tables(patterns)
    return lax.cond(
        fits(patterns),
        lambda: sparse_path(*lists, start),
        lambda: dense_path(x_in, patterns),
    )


def solution(mesh):
    placed = (P("row", ("col", "depth")), P())
    return jax.shard_map(
        on_device, mesh=mesh, in_specs=placed, out_specs=P("row", ("col", "depth")), check_vma=False
    )
```

```python
import functools

import jax
import jax.numpy as jnp
from jax import lax
from jax.experimental import pallas as pl
from jax.experimental.pallas import tpu as pltpu
from jax.sharding import PartitionSpec as P

BLOCK = 128
ITERS = 3
NB = 32
AXES = ("row", "col", "depth")

GROUP_CAP = 28
GROUPS = 16
CAP = 400
ZERO = GROUPS * GROUP_CAP
DUMMY = ZERO + 1
TILE = DUMMY + 1
S_BASE = TILE + 8
X_BASE = S_BASE + CAP
SLOTS = X_BASE + CAP
TERMS = 16
POSITIONS = 512
ROWS = 1152
BODY_WORDS = 24
CLASSES = ((16, 2), (8, 8), (6, 10), (5, 12), (4, 16), (3, 20), (2, 32), (1, 32), (0, 16))
STEPS = 2 * ITERS


def pack_kernel(pick_ref, in_ref, out_ref):
    for p in range(GROUP_CAP):
        out_ref[p] = in_ref[pick_ref[p]]


def product_kernel(ent_ref, ox_ref, ord_ref, body_ref, start_ref, out_ref, blocks, sem):
    for z in range(4):
        for d in range(4):
            g = z * 4 + d
            for r in range(4):
                for k in range(2):
                    pltpu.make_async_copy(
                        start_ref.at[r, z, k, d],
                        blocks.at[pl.ds(g * GROUP_CAP, GROUP_CAP), r * 2 + k],
                        sem,
                    ).start()
    blocks[ZERO] = jnp.zeros(blocks.shape[1:], blocks.dtype)
    for b in range(8):
        blocks[TILE + b] = jnp.zeros(blocks.shape[1:], blocks.dtype)
    whole = blocks.at[pl.ds(0, ZERO)]
    pltpu.make_async_copy(whole, whole, sem).wait()

    def load(slot):
        return blocks[slot].reshape(BLOCK, BLOCK)

    def step(t, carry):
        is_update = (t & 1) == 1
        keep = jnp.where(is_update, 1.5, 0.0).astype(jnp.float32)
        scale = jnp.where(is_update, -0.5, 1.0).astype(jnp.float32)
        for index, (terms, width) in enumerate(CLASSES):
            first = body_ref[t * BODY_WORDS + index * 2]
            count = body_ref[t * BODY_WORDS + index * 2 + 1]

            def body(it, carry, terms=terms, width=width, first=first):
                results = []
                for u in range(width):
                    entry = ord_ref[t * POSITIONS + first + it * width + u]
                    at = t * (TERMS * ROWS) + entry
                    words = [ent_ref[at + q * ROWS] for q in range(terms)]
                    lefts = [load(w & 0xFFFF) for w in words]
                    rights = [load(w >> 16) for w in words]
                    total = jnp.zeros((BLOCK, BLOCK), jnp.float32)
                    if terms == 1:
                        total = jnp.dot(lefts[0], rights[0], preferred_element_type=jnp.float32)
                    elif terms > 1:
                        left = jnp.concatenate(lefts, axis=1)
                        right = jnp.concatenate(rights, axis=0)
                        total = jnp.dot(left, right, preferred_element_type=jnp.float32)
                    ox = ox_ref[t * ROWS + entry]
                    old = load(ox >> 16).astype(jnp.float32)
                    results.append((ox & 0xFFFF, (keep * old + scale * total).astype(jnp.bfloat16)))
                for slot, value in results:
                    blocks[slot] = value.reshape(blocks.shape[1:])
                return carry

            lax.fori_loop(0, count, body, 0)
        return carry

    lax.fori_loop(0, STEPS, step, 0)
    copy = pltpu.make_async_copy(blocks.at[pl.ds(TILE, 8)], out_ref, sem)
    copy.start()
    copy.wait()


def ranks(mask):
    n = mask.shape[-1]
    before = (lax.iota(jnp.int32, n)[:, None] < lax.iota(jnp.int32, n)[None, :]).astype(jnp.bfloat16)
    flat = mask.reshape(-1, n).astype(jnp.bfloat16)
    return jnp.dot(flat, before, preferred_element_type=jnp.float32).astype(jnp.int32).reshape(mask.shape)


def group_order(pattern):
    return pattern.reshape(4, 8, 4, 2, 4).transpose(2, 4, 0, 3, 1).reshape(GROUPS, 64)


def fits(patterns):
    groups = group_order(patterns[0]).sum(-1).max()
    counts = patterns[1 : 2 * ITERS - 1].sum((1, 2)).max()
    f = patterns.astype(jnp.bfloat16)
    left = f[0 : 2 * ITERS].at[1::2].set(f[0 : 2 * ITERS : 2])
    right = f[0 : 2 * ITERS]
    terms = jnp.einsum("tik,tkj->tij", left, right, preferred_element_type=jnp.float32)
    most = (terms * patterns[1:].astype(jnp.float32)).max()
    return (groups <= GROUP_CAP) & (counts <= CAP) & (most <= TERMS)


def tables(patterns):
    row, col, depth = (lax.axis_index(a) for a in AXES)
    me_col = col * 4 + depth
    i = lax.iota(jnp.int32, NB)[:, None]
    j = lax.iota(jnp.int32, NB)[None, :]
    mine = (j == me_col).astype(jnp.int32)
    tile = mine * ((i // 8) == row).astype(jnp.int32)
    outs = jnp.concatenate([patterns[1:5], patterns[5:6] * mine, patterns[6:7] * tile])

    in_group = ranks(group_order(patterns[0]))
    slot0 = lax.iota(jnp.int32, GROUPS)[:, None] * GROUP_CAP + in_group
    slot0 = slot0.reshape(4, 4, 4, 2, 8).transpose(2, 4, 0, 3, 1).reshape(NB, NB)
    slot0 = jnp.where(patterns[0] > 0, slot0, ZERO)
    base = jnp.array([S_BASE, X_BASE, S_BASE, 0, S_BASE, 0], jnp.int32)[:, None]
    live = outs.reshape(STEPS, NB * NB) > 0
    out_slot = ranks(outs.reshape(STEPS, NB * NB)) + base
    in_tile = jnp.broadcast_to(TILE + i - 8 * row, (NB, NB)).reshape(1, NB * NB)
    out_slot = jnp.concatenate([out_slot[:5], in_tile])
    read_slot = jnp.where(live, out_slot, ZERO).reshape(STEPS, NB, NB)
    x_slot = jnp.stack([slot0, read_slot[1], read_slot[3]])
    left = jnp.repeat(x_slot, 2, axis=0)
    right = jnp.stack([slot0, read_slot[0], read_slot[1], read_slot[2], read_slot[3], read_slot[4]])
    old = jnp.where((lax.iota(jnp.int32, STEPS) % 2 == 1)[:, None, None], left, ZERO)

    o = lax.iota(jnp.int32, NB * NB)[None, :]
    of_row = (o // NB == i).astype(jnp.float32)
    of_col = (o % NB == i).astype(jnp.float32)
    spread = functools.partial(jnp.dot, precision=lax.Precision.HIGHEST, preferred_element_type=jnp.float32)
    wide_left = spread(left.transpose(0, 2, 1).astype(jnp.float32), of_row).astype(jnp.int32)
    wide_right = spread(right.astype(jnp.float32), of_col).astype(jnp.int32)
    on = live[:, None, :] & (wide_left != ZERO) & (wide_right != ZERO)
    before = (i > j).astype(jnp.bfloat16)
    place = jnp.einsum("kl,tlo->tko", before, on.astype(jnp.bfloat16), preferred_element_type=jnp.float32)
    blank = ZERO + ZERO * 65536
    word = jnp.where(on, wide_left + wide_right * 65536 - blank, 0)
    place = jnp.where(on, place.astype(jnp.int32), TERMS)
    hit = place[:, None] == lax.iota(jnp.int32, TERMS)[None, :, None, None]
    ent = jnp.where(hit, word[:, None], 0).sum(2) + blank
    ent = jnp.pad(ent, ((0, 0), (0, 0), (0, ROWS - NB * NB)), constant_values=blank)

    ox = out_slot + old.reshape(STEPS, NB * NB) * 65536
    ox = jnp.pad(ox, ((0, 0), (0, ROWS - NB * NB)), constant_values=DUMMY + ZERO * 65536)

    count = on.astype(jnp.int32).sum(1)
    members = []
    for (limit, _), low in zip(CLASSES, [limit for limit, _ in CLASSES[1:]] + [-1]):
        members.append(live & (count > low) & (count <= limit))
    member = jnp.stack(members, 1).astype(jnp.int32)
    rank = ranks(member)
    total = member.sum(-1)
    passed = [jnp.zeros((STEPS,), jnp.int32)]
    for index in range(len(CLASSES)):
        passed.append(passed[-1] + total[:, index])
    ahead = jnp.stack(passed[:-1], 1)
    position = jnp.where(member > 0, rank + ahead[:, :, None], 0).sum(1)
    position = jnp.where(live, position, POSITIONS)
    match = position[:, None, :] == lax.iota(jnp.int32, POSITIONS)[None, :, None]
    entry = jnp.where(match, o[None] - NB * NB, 0).sum(-1) + NB * NB
    end = jnp.zeros((STEPS,), jnp.int32)
    body = []
    for index, (_, width) in enumerate(CLASSES):
        bodies = jnp.maximum((passed[index + 1] - end + width - 1) // width, 0)
        body += [end, bodies]
        end = end + bodies * width
    body = jnp.stack(body + [end] * (BODY_WORDS - len(body)), 1)
    return ent.reshape(-1), ox.reshape(-1), entry.reshape(-1), body.reshape(-1)


def pick_places(patterns):
    _, col, depth = (lax.axis_index(a) for a in AXES)
    order = lax.dynamic_index_in_dim(group_order(patterns[0]), (col // 2) * 4 + depth, 0, keepdims=False)
    place = jnp.where(order > 0, ranks(order[None])[0], GROUP_CAP)
    hit = place[None, :] == lax.iota(jnp.int32, GROUP_CAP)[:, None]
    return jnp.where(hit, lax.iota(jnp.int32, 64)[None, :], 0).sum(-1)


def pack(pick, slices):
    return pl.pallas_call(
        pack_kernel,
        out_shape=jax.ShapeDtypeStruct((GROUP_CAP, 16, BLOCK), jnp.bfloat16),
        in_specs=[pl.BlockSpec(memory_space=pltpu.SMEM), pl.BlockSpec(memory_space=pltpu.VMEM)],
        out_specs=pl.BlockSpec(memory_space=pltpu.VMEM),
        name="pack_blocks",
    )(pick, slices)


def sparse_path(ent, ox, entry, body, start):
    smem = pl.BlockSpec(memory_space=pltpu.SMEM)
    out = pl.pallas_call(
        product_kernel,
        out_shape=jax.ShapeDtypeStruct((8, 8, 16, BLOCK), jnp.bfloat16),
        in_specs=[smem, smem, smem, smem, pl.BlockSpec(memory_space=pl.ANY)],
        out_specs=pl.BlockSpec(memory_space=pl.ANY),
        scratch_shapes=[pltpu.VMEM((SLOTS, 8, 16, BLOCK), jnp.bfloat16), pltpu.SemaphoreType.DMA(())],
        compiler_params=pltpu.CompilerParams(vmem_limit_bytes=56 * 2**20),
        name="block_products",
    )(ent, ox, entry, body, start)
    return out.reshape(8 * BLOCK, BLOCK)


def tile_mask(pattern, row_first, col_first, tile_rows, tile_cols):
    blocks = pattern.shape[0]
    slab = lax.dynamic_slice_in_dim(pattern, row_first // BLOCK, tile_rows // BLOCK, 0).astype(jnp.float32)
    col_block = (col_first + lax.iota(jnp.int32, tile_cols)) // BLOCK
    onehot = (col_block[None, :] == lax.iota(jnp.int32, blocks)[:, None]).astype(jnp.float32)
    coarse = jnp.dot(slab, onehot)
    spread_rows = jnp.broadcast_to(coarse[:, None, :], (tile_rows // BLOCK, BLOCK, tile_cols))
    return spread_rows.reshape(tile_rows, tile_cols)


def dense_path(x_in, patterns):
    tile_rows, tile_width = x_in.shape
    row_first = lax.axis_index("row") * tile_rows
    col_first = (lax.axis_index("col") * lax.axis_size("depth") + lax.axis_index("depth")) * tile_width
    masks = [tile_mask(patterns[p], row_first, col_first, tile_rows, tile_width) for p in range(2 * ITERS + 1)]
    matrix = (x_in * masks[0]).astype(jnp.bfloat16)
    for iteration in range(ITERS):
        panel = lax.all_gather(matrix, ("col", "depth"), axis=1, tiled=True)

        def product(right):
            column = lax.all_gather(right, "row", axis=0, tiled=True)
            return jnp.dot(panel, column, preferred_element_type=jnp.float32)

        squared = (masks[2 * iteration + 1] * product(matrix)).astype(jnp.bfloat16)
        update = 1.5 * matrix.astype(jnp.float32) - 0.5 * product(squared)
        matrix = (masks[2 * iteration + 2] * update).astype(jnp.bfloat16)
    return matrix


def on_device(x_in, patterns):
    groups = [[r * 8 + z * 2 + k for r in range(4) for k in range(2)] for z in range(4)]
    by_slice = x_in.reshape(8, 8, 16, BLOCK).transpose(1, 0, 2, 3)
    slices = lax.all_to_all(by_slice, ("row", "col"), 0, 0, axis_index_groups=groups, tiled=True)
    slices = slices.reshape(64, 16, BLOCK)
    packed = pack(pick_places(patterns), slices)
    start = lax.all_gather(packed, AXES, axis=0, tiled=True)
    start = start.reshape(4, 4, 2, 4, GROUP_CAP, 16, BLOCK)
    lists = lax.optimization_barrier(tables(patterns))
    return lax.cond(
        fits(patterns),
        lambda: sparse_path(*lists, start),
        lambda: dense_path(x_in, patterns),
    )


def solution(mesh):
    placed = (P("row", ("col", "depth")), P())
    return jax.shard_map(
        on_device, mesh=mesh, in_specs=placed, out_specs=P("row", ("col", "depth")), check_vma=False
    )
```

```python
import functools

import jax
import jax.numpy as jnp
from jax import lax
from jax.experimental import pallas as pl
from jax.experimental.pallas import tpu as pltpu
from jax.sharding import PartitionSpec as P

BLOCK = 128
ITERS = 3
NB = 32
AXES = ("row", "col", "depth")

COLUMN_CAP = 17
GROUP_CAP = 50
CAP = 400
ZERO = 8 * GROUP_CAP
DUMMY = ZERO + 1
TILE = DUMMY + 1
S_BASE = TILE + 8
X_BASE = S_BASE + CAP
SLOTS = X_BASE + CAP
TERMS = 16
POSITIONS = 512
ROWS = 1152
BODY_WORDS = 24
CLASSES = ((16, 2), (8, 8), (6, 10), (5, 12), (4, 16), (3, 20), (2, 32), (1, 32), (0, 16))
STEPS = 2 * ITERS


def pack_kernel(pick_ref, *refs):
    sources, out_ref, blocks, sem = refs[:4], refs[4], refs[5], refs[6]
    length = sources[0].shape[0]
    for index, source in enumerate(sources):
        pltpu.make_async_copy(source, blocks.at[pl.ds(index * length, length)], sem).start()
    pltpu.make_async_copy(blocks, blocks, sem).wait()
    for p in range(out_ref.shape[0]):
        out_ref[p] = blocks[pick_ref[p]]


def pack(pick, sources):
    slots = pick.shape[0]
    return pl.pallas_call(
        pack_kernel,
        out_shape=jax.ShapeDtypeStruct((slots, BLOCK, BLOCK), jnp.bfloat16),
        in_specs=[pl.BlockSpec(memory_space=pltpu.SMEM)] + [pl.BlockSpec(memory_space=pl.ANY)] * 4,
        out_specs=pl.BlockSpec(memory_space=pltpu.VMEM),
        scratch_shapes=[
            pltpu.VMEM((4 * sources[0].shape[0], BLOCK, BLOCK), jnp.bfloat16),
            pltpu.SemaphoreType.DMA(()),
        ],
        compiler_params=pltpu.CompilerParams(vmem_limit_bytes=16 * 2**20),
        name="pack_blocks",
    )(pick, *sources)


def product_kernel(ent_ref, ox_ref, ord_ref, body_ref, *refs):
    pieces, out_ref, blocks, sem = refs[:8], refs[8], refs[9], refs[10]
    for index, piece in enumerate(pieces):
        pltpu.make_async_copy(piece, blocks.at[pl.ds(index * GROUP_CAP, GROUP_CAP)], sem).start()
    blocks[ZERO] = jnp.zeros((BLOCK, BLOCK), blocks.dtype)
    for b in range(8):
        blocks[TILE + b] = jnp.zeros((BLOCK, BLOCK), blocks.dtype)
    whole = blocks.at[pl.ds(0, ZERO)]
    pltpu.make_async_copy(whole, whole, sem).wait()

    def load(slot):
        return blocks[slot]

    def step(t, carry):
        is_update = (t & 1) == 1
        keep = jnp.where(is_update, 1.5, 0.0).astype(jnp.float32)
        scale = jnp.where(is_update, -0.5, 1.0).astype(jnp.float32)
        for index, (terms, width) in enumerate(CLASSES):
            first = body_ref[t * BODY_WORDS + index * 2]
            count = body_ref[t * BODY_WORDS + index * 2 + 1]

            def body(it, carry, terms=terms, width=width, first=first):
                results = []
                for u in range(width):
                    entry = ord_ref[t * POSITIONS + first + it * width + u]
                    at = t * (TERMS * ROWS) + entry
                    words = [ent_ref[at + q * ROWS] for q in range(terms)]
                    lefts = [load(w & 0xFFFF) for w in words]
                    rights = [load(w >> 16) for w in words]
                    total = jnp.zeros((BLOCK, BLOCK), jnp.float32)
                    if terms == 1:
                        total = jnp.dot(lefts[0], rights[0], preferred_element_type=jnp.float32)
                    elif terms > 1:
                        left = jnp.concatenate(lefts, axis=1)
                        right = jnp.concatenate(rights, axis=0)
                        total = jnp.dot(left, right, preferred_element_type=jnp.float32)
                    ox = ox_ref[t * ROWS + entry]
                    old = load(ox >> 16).astype(jnp.float32)
                    results.append((ox & 0xFFFF, (keep * old + scale * total).astype(jnp.bfloat16)))
                for slot, value in results:
                    blocks[slot] = value
                return carry

            lax.fori_loop(0, count, body, 0)
        return carry

    lax.fori_loop(0, STEPS, step, 0)
    copy = pltpu.make_async_copy(blocks.at[pl.ds(TILE, 8)], out_ref, sem)
    copy.start()
    copy.wait()


def ranks(mask):
    n = mask.shape[-1]
    before = (lax.iota(jnp.int32, n)[:, None] < lax.iota(jnp.int32, n)[None, :]).astype(jnp.bfloat16)
    flat = mask.reshape(-1, n).astype(jnp.bfloat16)
    return jnp.dot(flat, before, preferred_element_type=jnp.float32).astype(jnp.int32).reshape(mask.shape)


def start_groups(pattern):
    by_place = pattern.reshape(NB, 4, 2, 4)
    return jnp.stack([by_place[:, :, 0].transpose(1, 2, 0), by_place[:, :, 1].transpose(2, 1, 0)])


def fits(patterns):
    groups = start_groups(patterns[0])
    columns = groups.sum(-1)
    fit = (columns.max() <= COLUMN_CAP) & (columns.sum(-1).max() <= GROUP_CAP)
    counts = patterns[1 : 2 * ITERS - 1].sum((1, 2)).max()
    f = patterns.astype(jnp.bfloat16)
    left = f[0 : 2 * ITERS].at[1::2].set(f[0 : 2 * ITERS : 2])
    right = f[0 : 2 * ITERS]
    terms = jnp.einsum("tik,tkj->tij", left, right, preferred_element_type=jnp.float32)
    most = (terms * patterns[1:].astype(jnp.float32)).max()
    return fit & (counts <= CAP) & (most <= TERMS)


def tables(patterns):
    row, col, depth = (lax.axis_index(a) for a in AXES)
    me_col = col * 4 + depth
    i = lax.iota(jnp.int32, NB)[:, None]
    j = lax.iota(jnp.int32, NB)[None, :]
    mine = (j == me_col).astype(jnp.int32)
    tile = mine * ((i // 8) == row).astype(jnp.int32)
    outs = jnp.concatenate([patterns[1:5], patterns[5:6] * mine, patterns[6:7] * tile])

    groups = start_groups(patterns[0])
    _, _, (my_core, my_z, my_y) = my_place()
    line = jnp.stack([my_z, my_y])[:, None]
    back = (line - lax.iota(jnp.int32, 4)[None, :]) % 4
    first = (lax.iota(jnp.int32, 2)[:, None] != my_core).astype(jnp.int32) * 4 + back
    slot = first[:, :, None] * GROUP_CAP + ranks(groups.reshape(2, 4, 4 * NB))
    slot = slot.reshape(2, 4, 4, NB)
    slot0 = jnp.stack([slot[0].transpose(2, 0, 1), slot[1].transpose(2, 1, 0)], axis=2).reshape(NB, NB)
    slot0 = jnp.where(patterns[0] > 0, slot0, ZERO)
    base = jnp.array([S_BASE, X_BASE, S_BASE, 0, S_BASE, 0], jnp.int32)[:, None]
    live = outs.reshape(STEPS, NB * NB) > 0
    out_slot = ranks(outs.reshape(STEPS, NB * NB)) + base
    in_tile = jnp.broadcast_to(TILE + i - 8 * row, (NB, NB)).reshape(1, NB * NB)
    out_slot = jnp.concatenate([out_slot[:5], in_tile])
    read_slot = jnp.where(live, out_slot, ZERO).reshape(STEPS, NB, NB)
    x_slot = jnp.stack([slot0, read_slot[1], read_slot[3]])
    left = jnp.repeat(x_slot, 2, axis=0)
    right = jnp.stack([slot0, read_slot[0], read_slot[1], read_slot[2], read_slot[3], read_slot[4]])
    old = jnp.where((lax.iota(jnp.int32, STEPS) % 2 == 1)[:, None, None], left, ZERO)

    o = lax.iota(jnp.int32, NB * NB)[None, :]
    of_row = (o // NB == i).astype(jnp.float32)
    of_col = (o % NB == i).astype(jnp.float32)
    spread = functools.partial(jnp.dot, precision=lax.Precision.HIGHEST, preferred_element_type=jnp.float32)
    wide_left = spread(left.transpose(0, 2, 1).astype(jnp.float32), of_row).astype(jnp.int32)
    wide_right = spread(right.astype(jnp.float32), of_col).astype(jnp.int32)
    on = live[:, None, :] & (wide_left != ZERO) & (wide_right != ZERO)
    before = (i > j).astype(jnp.bfloat16)
    place = jnp.einsum("kl,tlo->tko", before, on.astype(jnp.bfloat16), preferred_element_type=jnp.float32)
    blank = ZERO + ZERO * 65536
    word = jnp.where(on, wide_left + wide_right * 65536 - blank, 0)
    place = jnp.where(on, place.astype(jnp.int32), TERMS)
    hit = place[:, None] == lax.iota(jnp.int32, TERMS)[None, :, None, None]
    ent = jnp.where(hit, word[:, None], 0).sum(2) + blank
    ent = jnp.pad(ent, ((0, 0), (0, 0), (0, ROWS - NB * NB)), constant_values=blank)

    ox = out_slot + old.reshape(STEPS, NB * NB) * 65536
    ox = jnp.pad(ox, ((0, 0), (0, ROWS - NB * NB)), constant_values=DUMMY + ZERO * 65536)

    count = on.astype(jnp.int32).sum(1)
    members = []
    for (limit, _), low in zip(CLASSES, [limit for limit, _ in CLASSES[1:]] + [-1]):
        members.append(live & (count > low) & (count <= limit))
    member = jnp.stack(members, 1).astype(jnp.int32)
    rank = ranks(member)
    total = member.sum(-1)
    passed = [jnp.zeros((STEPS,), jnp.int32)]
    for index in range(len(CLASSES)):
        passed.append(passed[-1] + total[:, index])
    ahead = jnp.stack(passed[:-1], 1)
    position = jnp.where(member > 0, rank + ahead[:, :, None], 0).sum(1)
    position = jnp.where(live, position, POSITIONS)
    match = position[:, None, :] == lax.iota(jnp.int32, POSITIONS)[None, :, None]
    entry = jnp.where(match, o[None] - NB * NB, 0).sum(-1) + NB * NB
    end = jnp.zeros((STEPS,), jnp.int32)
    body = []
    for index, (_, width) in enumerate(CLASSES):
        bodies = jnp.maximum((passed[index + 1] - end + width - 1) // width, 0)
        body += [end, bodies]
        end = end + bodies * width
    body = jnp.stack(body + [end] * (BODY_WORDS - len(body)), 1)
    return ent.reshape(-1), ox.reshape(-1), entry.reshape(-1), body.reshape(-1)


def my_place():
    row, col, depth = (lax.axis_index(a) for a in AXES)
    return row, col * 4 + depth, (col % 2, col // 2, depth)


def picked(mask, value, slots):
    place = jnp.where(mask > 0, ranks(mask[None])[0], slots)
    hit = place[None, :] == lax.iota(jnp.int32, slots)[:, None]
    return jnp.where(hit, value[None, :], 0).sum(-1)


def picks(pattern):
    row, column, (core, z, y) = my_place()
    i = lax.iota(jnp.int32, NB)
    mine = lax.dynamic_index_in_dim(pattern, column, 1, keepdims=False)
    of_column = picked(mine, ((row - i // 8) % 4) * 8 + i % 8, COLUMN_CAP)
    line = core * 4 + jnp.where(core == 0, z, y)
    along = jnp.where(core == 0, y, z)
    group = lax.dynamic_index_in_dim(start_groups(pattern).reshape(8, 4, NB), line, 0, keepdims=False)
    source = (along - lax.iota(jnp.int32, 4)) % 4
    value = source[:, None] * COLUMN_CAP + jnp.minimum(ranks(group), COLUMN_CAP - 1)
    of_group = picked(group.reshape(4 * NB), value.reshape(4 * NB), GROUP_CAP)
    return of_column, of_group


def hops(axes, shift):
    pairs = []
    for x in range(4):
        for z in range(4):
            for c in range(2):
                for y in range(4):
                    to = {"x": x, "y": y, "z": z}
                    to[axes[c]] = (to[axes[c]] + shift) % 4
                    pairs.append((((x * 4 + z) * 2 + c) * 4 + y, ((to["x"] * 4 + to["z"]) * 2 + c) * 4 + to["y"]))
    return pairs


def gather(mine, axes):
    far = {shift: lax.ppermute(mine, AXES, hops(axes, shift)) for shift in (1, 3, 2)}
    return [mine, far[1], far[2], far[3]]


def sparse_path(ent, ox, entry, body, pieces):
    smem = pl.BlockSpec(memory_space=pltpu.SMEM)
    out = pl.pallas_call(
        product_kernel,
        out_shape=jax.ShapeDtypeStruct((8, BLOCK, BLOCK), jnp.bfloat16),
        in_specs=[smem] * 4 + [pl.BlockSpec(memory_space=pl.ANY)] * 8,
        out_specs=pl.BlockSpec(memory_space=pl.ANY),
        scratch_shapes=[pltpu.VMEM((SLOTS, BLOCK, BLOCK), jnp.bfloat16), pltpu.SemaphoreType.DMA(())],
        compiler_params=pltpu.CompilerParams(vmem_limit_bytes=56 * 2**20),
        name="block_products",
    )(ent, ox, entry, body, *pieces)
    return out.reshape(8 * BLOCK, BLOCK)


def tile_mask(pattern, row_first, col_first, tile_rows, tile_cols):
    blocks = pattern.shape[0]
    slab = lax.dynamic_slice_in_dim(pattern, row_first // BLOCK, tile_rows // BLOCK, 0).astype(jnp.float32)
    col_block = (col_first + lax.iota(jnp.int32, tile_cols)) // BLOCK
    onehot = (col_block[None, :] == lax.iota(jnp.int32, blocks)[:, None]).astype(jnp.float32)
    coarse = jnp.dot(slab, onehot)
    spread_rows = jnp.broadcast_to(coarse[:, None, :], (tile_rows // BLOCK, BLOCK, tile_cols))
    return spread_rows.reshape(tile_rows, tile_cols)


def dense_path(x_in, patterns):
    tile_rows, tile_width = x_in.shape
    row_first = lax.axis_index("row") * tile_rows
    col_first = (lax.axis_index("col") * lax.axis_size("depth") + lax.axis_index("depth")) * tile_width
    masks = [tile_mask(patterns[p], row_first, col_first, tile_rows, tile_width) for p in range(2 * ITERS + 1)]
    matrix = (x_in * masks[0]).astype(jnp.bfloat16)
    for iteration in range(ITERS):
        panel = lax.all_gather(matrix, ("col", "depth"), axis=1, tiled=True)

        def product(right):
            column = lax.all_gather(right, "row", axis=0, tiled=True)
            return jnp.dot(panel, column, preferred_element_type=jnp.float32)

        squared = (masks[2 * iteration + 1] * product(matrix)).astype(jnp.bfloat16)
        update = 1.5 * matrix.astype(jnp.float32) - 0.5 * product(squared)
        matrix = (masks[2 * iteration + 2] * update).astype(jnp.bfloat16)
    return matrix


def on_device(x_in, patterns):
    of_column, of_group = picks(patterns[0])
    column = pack(of_column, gather(x_in.reshape(8, BLOCK, BLOCK), "xx"))
    group = pack(of_group, gather(column, "yz"))
    group, patterns = lax.optimization_barrier((group, patterns))
    pieces = gather(group, "zy")
    pieces += [lax.ppermute(piece, "col", [(c, c ^ 1) for c in range(8)]) for piece in pieces]
    lists = lax.optimization_barrier(tables(patterns))
    return lax.cond(
        fits(patterns),
        lambda: sparse_path(*lists, pieces),
        lambda: dense_path(x_in, patterns),
    )


def solution(mesh):
    placed = (P("row", ("col", "depth")), P())
    return jax.shard_map(
        on_device, mesh=mesh, in_specs=placed, out_specs=P("row", ("col", "depth")), check_vma=False
    )
```

```python
import functools

import jax
import jax.numpy as jnp
from jax import lax
from jax.experimental import pallas as pl
from jax.experimental.pallas import tpu as pltpu
from jax.sharding import PartitionSpec as P

BLOCK = 128
ITERS = 3
NB = 32
AXES = ("row", "col", "depth")

COLUMN_CAP = 17
GROUP_CAP = 50
CAP = 400
ZERO = 8 * GROUP_CAP
DUMMY = ZERO + 1
TILE = DUMMY + 1
S_BASE = TILE + 8
X_BASE = S_BASE + CAP
SLOTS = X_BASE + CAP
TERMS = 16
POSITIONS = 512
ROWS = 1152
BODY_WORDS = 24
CLASSES = ((16, 2), (8, 8), (6, 10), (5, 12), (4, 16), (3, 20), (2, 32), (1, 32), (0, 16))
STEPS = 2 * ITERS


def pack_kernel(pick_ref, *refs):
    sources, out_ref, blocks, sem = refs[:4], refs[4], refs[5], refs[6]
    length = sources[0].shape[0]
    for index, source in enumerate(sources):
        pltpu.make_async_copy(source, blocks.at[pl.ds(index * length, length)], sem).start()
    pltpu.make_async_copy(blocks, blocks, sem).wait()
    for p in range(out_ref.shape[0]):
        out_ref[p] = blocks[pick_ref[p]]


def pack(pick, sources):
    slots = pick.shape[0]
    return pl.pallas_call(
        pack_kernel,
        out_shape=jax.ShapeDtypeStruct((slots, BLOCK, BLOCK), jnp.bfloat16),
        in_specs=[pl.BlockSpec(memory_space=pltpu.SMEM)] + [pl.BlockSpec(memory_space=pl.ANY)] * 4,
        out_specs=pl.BlockSpec(memory_space=pltpu.VMEM),
        scratch_shapes=[
            pltpu.VMEM((4 * sources[0].shape[0], BLOCK, BLOCK), jnp.bfloat16),
            pltpu.SemaphoreType.DMA(()),
        ],
        compiler_params=pltpu.CompilerParams(vmem_limit_bytes=16 * 2**20),
        name="pack_blocks",
    )(pick, *sources)


def product_kernel(ent_ref, ox_ref, ord_ref, body_ref, *refs):
    pieces, out_ref, blocks, sem = refs[:8], refs[8], refs[9], refs[10]
    for index, piece in enumerate(pieces):
        pltpu.make_async_copy(piece, blocks.at[pl.ds(index * GROUP_CAP, GROUP_CAP)], sem).start()
    blocks[ZERO] = jnp.zeros((BLOCK, BLOCK), blocks.dtype)
    for b in range(8):
        blocks[TILE + b] = jnp.zeros((BLOCK, BLOCK), blocks.dtype)
    whole = blocks.at[pl.ds(0, ZERO)]
    pltpu.make_async_copy(whole, whole, sem).wait()

    def load(slot):
        return blocks[slot]

    def step(t, carry):
        is_update = (t & 1) == 1
        keep = jnp.where(is_update, 1.5, 0.0).astype(jnp.float32)
        scale = jnp.where(is_update, -0.5, 1.0).astype(jnp.float32)
        for index, (terms, width) in enumerate(CLASSES):
            first = body_ref[t * BODY_WORDS + index * 2]
            count = body_ref[t * BODY_WORDS + index * 2 + 1]

            def body(it, carry, terms=terms, width=width, first=first):
                results = []
                for u in range(width):
                    entry = ord_ref[t * POSITIONS + first + it * width + u]
                    at = t * (TERMS * ROWS) + entry
                    words = [ent_ref[at + q * ROWS] for q in range(terms)]
                    lefts = [load(w & 0xFFFF) for w in words]
                    rights = [load(w >> 16) for w in words]
                    total = jnp.zeros((BLOCK, BLOCK), jnp.float32)
                    if terms == 1:
                        total = jnp.dot(lefts[0], rights[0], preferred_element_type=jnp.float32)
                    elif terms > 1:
                        left = jnp.concatenate(lefts, axis=1)
                        right = jnp.concatenate(rights, axis=0)
                        total = jnp.dot(left, right, preferred_element_type=jnp.float32)
                    ox = ox_ref[t * ROWS + entry]
                    old = load(ox >> 16).astype(jnp.float32)
                    results.append((ox & 0xFFFF, (keep * old + scale * total).astype(jnp.bfloat16)))
                for slot, value in results:
                    blocks[slot] = value
                return carry

            lax.fori_loop(0, count, body, 0)
        return carry

    lax.fori_loop(0, STEPS, step, 0)
    copy = pltpu.make_async_copy(blocks.at[pl.ds(TILE, 8)], out_ref, sem)
    copy.start()
    copy.wait()


def ranks(mask):
    n = mask.shape[-1]
    before = (lax.iota(jnp.int32, n)[:, None] < lax.iota(jnp.int32, n)[None, :]).astype(jnp.bfloat16)
    flat = mask.reshape(-1, n).astype(jnp.bfloat16)
    return jnp.dot(flat, before, preferred_element_type=jnp.float32).astype(jnp.int32).reshape(mask.shape)


def start_groups(pattern):
    by_place = pattern.reshape(NB, 4, 2, 4)
    return jnp.stack([by_place[:, :, 0].transpose(1, 2, 0), by_place[:, :, 1].transpose(2, 1, 0)])


def fits(patterns):
    groups = start_groups(patterns[0])
    columns = groups.sum(-1)
    fit = (columns.max() <= COLUMN_CAP) & (columns.sum(-1).max() <= GROUP_CAP)
    counts = patterns[1 : 2 * ITERS - 1].sum((1, 2)).max()
    f = patterns.astype(jnp.bfloat16)
    left = f[0 : 2 * ITERS].at[1::2].set(f[0 : 2 * ITERS : 2])
    right = f[0 : 2 * ITERS]
    terms = jnp.einsum("tik,tkj->tij", left, right, preferred_element_type=jnp.float32)
    most = (terms * patterns[1:].astype(jnp.float32)).max()
    return fit & (counts <= CAP) & (most <= TERMS)


def slots(patterns):
    row, col, depth = (lax.axis_index(a) for a in AXES)
    me_col = col * 4 + depth
    i = lax.iota(jnp.int32, NB)[:, None]
    j = lax.iota(jnp.int32, NB)[None, :]
    mine = (j == me_col).astype(jnp.int32)
    tile = mine * ((i // 8) == row).astype(jnp.int32)
    outs = jnp.concatenate([patterns[1:5], patterns[5:6] * mine, patterns[6:7] * tile])

    groups = start_groups(patterns[0])
    _, _, (my_core, my_z, my_y) = my_place()
    line = jnp.stack([my_z, my_y])[:, None]
    back = (line - lax.iota(jnp.int32, 4)[None, :]) % 4
    first = (lax.iota(jnp.int32, 2)[:, None] != my_core).astype(jnp.int32) * 4 + back
    slot = first[:, :, None] * GROUP_CAP + ranks(groups.reshape(2, 4, 4 * NB))
    slot = slot.reshape(2, 4, 4, NB)
    slot0 = jnp.stack([slot[0].transpose(2, 0, 1), slot[1].transpose(2, 1, 0)], axis=2).reshape(NB, NB)
    slot0 = jnp.where(patterns[0] > 0, slot0, ZERO)
    base = jnp.array([S_BASE, X_BASE, S_BASE, 0, S_BASE, 0], jnp.int32)[:, None]
    live = outs.reshape(STEPS, NB * NB) > 0
    out_slot = ranks(outs.reshape(STEPS, NB * NB)) + base
    in_tile = jnp.broadcast_to(TILE + i - 8 * row, (NB, NB)).reshape(1, NB * NB)
    out_slot = jnp.concatenate([out_slot[:5], in_tile])
    read_slot = jnp.where(live, out_slot, ZERO).reshape(STEPS, NB, NB)
    x_slot = jnp.stack([slot0, read_slot[1], read_slot[3]])
    left = jnp.repeat(x_slot, 2, axis=0)
    right = jnp.stack([slot0, read_slot[0], read_slot[1], read_slot[2], read_slot[3], read_slot[4]])
    old = jnp.where((lax.iota(jnp.int32, STEPS) % 2 == 1)[:, None, None], left, ZERO)

    return live, out_slot, left, right, old


def tables(live, out_slot, left, right, old):
    i = lax.iota(jnp.int32, NB)[:, None]
    j = lax.iota(jnp.int32, NB)[None, :]

    o = lax.iota(jnp.int32, NB * NB)[None, :]
    of_row = (o // NB == i).astype(jnp.float32)
    of_col = (o % NB == i).astype(jnp.float32)
    spread = functools.partial(jnp.dot, precision=lax.Precision.HIGHEST, preferred_element_type=jnp.float32)
    wide_left = spread(left.transpose(0, 2, 1).astype(jnp.float32), of_row).astype(jnp.int32)
    wide_right = spread(right.astype(jnp.float32), of_col).astype(jnp.int32)
    on = live[:, None, :] & (wide_left != ZERO) & (wide_right != ZERO)
    before = (i > j).astype(jnp.bfloat16)
    place = jnp.einsum("kl,tlo->tko", before, on.astype(jnp.bfloat16), preferred_element_type=jnp.float32)
    blank = ZERO + ZERO * 65536
    word = jnp.where(on, wide_left + wide_right * 65536 - blank, 0)
    place = jnp.where(on, place.astype(jnp.int32), TERMS)
    hit = place[:, None] == lax.iota(jnp.int32, TERMS)[None, :, None, None]
    ent = jnp.where(hit, word[:, None], 0).sum(2) + blank
    ent = jnp.pad(ent, ((0, 0), (0, 0), (0, ROWS - NB * NB)), constant_values=blank)

    ox = out_slot + old.reshape(STEPS, NB * NB) * 65536
    ox = jnp.pad(ox, ((0, 0), (0, ROWS - NB * NB)), constant_values=DUMMY + ZERO * 65536)

    count = on.astype(jnp.int32).sum(1)
    members = []
    for (limit, _), low in zip(CLASSES, [limit for limit, _ in CLASSES[1:]] + [-1]):
        members.append(live & (count > low) & (count <= limit))
    member = jnp.stack(members, 1).astype(jnp.int32)
    rank = ranks(member)
    total = member.sum(-1)
    ahead = jnp.stack([total[:, :index].sum(1) for index in range(len(CLASSES) + 1)], 1)
    passed = [ahead[:, index : index + 1] for index in range(len(CLASSES) + 1)]
    ahead = ahead[:, : len(CLASSES)]
    position = jnp.where(member > 0, rank + ahead[:, :, None], 0).sum(1)
    position = jnp.where(live, position, POSITIONS)
    match = position[:, None, :] == lax.iota(jnp.int32, POSITIONS)[None, :, None]
    entry = jnp.where(match, o[None] - NB * NB, 0).sum(-1) + NB * NB
    end = jnp.zeros((STEPS, 1), jnp.int32)
    lane = lax.iota(jnp.int32, BODY_WORDS)[None, :]
    body = jnp.zeros((STEPS, BODY_WORDS), jnp.int32)
    for index, (_, width) in enumerate(CLASSES):
        bodies = jnp.maximum((passed[index + 1] - end + width - 1) // width, 0)
        body = jnp.where(lane == 2 * index, end, jnp.where(lane == 2 * index + 1, bodies, body))
        end = end + bodies * width
    return ent.reshape(-1), ox.reshape(-1), entry.reshape(-1), body.reshape(-1)


def my_place():
    row, col, depth = (lax.axis_index(a) for a in AXES)
    return row, col * 4 + depth, (col % 2, col // 2, depth)


def picked(mask, value, slots):
    place = jnp.where(mask > 0, ranks(mask[None])[0], slots)
    hit = place[None, :] == lax.iota(jnp.int32, slots)[:, None]
    return jnp.where(hit, value[None, :], 0).sum(-1)


def picks(pattern):
    row, column, (core, z, y) = my_place()
    i = lax.iota(jnp.int32, NB)
    mine = lax.dynamic_index_in_dim(pattern, column, 1, keepdims=False)
    of_column = picked(mine, ((row - i // 8) % 4) * 8 + i % 8, COLUMN_CAP)
    line = core * 4 + jnp.where(core == 0, z, y)
    along = jnp.where(core == 0, y, z)
    group = lax.dynamic_index_in_dim(start_groups(pattern).reshape(8, 4, NB), line, 0, keepdims=False)
    source = (along - lax.iota(jnp.int32, 4)) % 4
    value = source[:, None] * COLUMN_CAP + jnp.minimum(ranks(group), COLUMN_CAP - 1)
    of_group = picked(group.reshape(4 * NB), value.reshape(4 * NB), GROUP_CAP)
    return of_column, of_group


def hops(axes, shift):
    pairs = []
    for x in range(4):
        for z in range(4):
            for c in range(2):
                for y in range(4):
                    to = {"x": x, "y": y, "z": z}
                    to[axes[c]] = (to[axes[c]] + shift) % 4
                    pairs.append((((x * 4 + z) * 2 + c) * 4 + y, ((to["x"] * 4 + to["z"]) * 2 + c) * 4 + to["y"]))
    return pairs


def gather(mine, axes):
    far = {shift: lax.ppermute(mine, AXES, hops(axes, shift)) for shift in (1, 3, 2)}
    return [mine, far[1], far[2], far[3]]


def sparse_path(ent, ox, entry, body, pieces):
    smem = pl.BlockSpec(memory_space=pltpu.SMEM)
    out = pl.pallas_call(
        product_kernel,
        out_shape=jax.ShapeDtypeStruct((8, BLOCK, BLOCK), jnp.bfloat16),
        in_specs=[smem] * 4 + [pl.BlockSpec(memory_space=pl.ANY)] * 8,
        out_specs=pl.BlockSpec(memory_space=pl.ANY),
        scratch_shapes=[pltpu.VMEM((SLOTS, BLOCK, BLOCK), jnp.bfloat16), pltpu.SemaphoreType.DMA(())],
        compiler_params=pltpu.CompilerParams(vmem_limit_bytes=56 * 2**20),
        name="block_products",
    )(ent, ox, entry, body, *pieces)
    return out.reshape(8 * BLOCK, BLOCK)


def tile_mask(pattern, row_first, col_first, tile_rows, tile_cols):
    blocks = pattern.shape[0]
    slab = lax.dynamic_slice_in_dim(pattern, row_first // BLOCK, tile_rows // BLOCK, 0).astype(jnp.float32)
    col_block = (col_first + lax.iota(jnp.int32, tile_cols)) // BLOCK
    onehot = (col_block[None, :] == lax.iota(jnp.int32, blocks)[:, None]).astype(jnp.float32)
    coarse = jnp.dot(slab, onehot)
    spread_rows = jnp.broadcast_to(coarse[:, None, :], (tile_rows // BLOCK, BLOCK, tile_cols))
    return spread_rows.reshape(tile_rows, tile_cols)


def dense_path(x_in, patterns):
    tile_rows, tile_width = x_in.shape
    row_first = lax.axis_index("row") * tile_rows
    col_first = (lax.axis_index("col") * lax.axis_size("depth") + lax.axis_index("depth")) * tile_width
    masks = [tile_mask(patterns[p], row_first, col_first, tile_rows, tile_width) for p in range(2 * ITERS + 1)]
    matrix = (x_in * masks[0]).astype(jnp.bfloat16)
    for iteration in range(ITERS):
        panel = lax.all_gather(matrix, ("col", "depth"), axis=1, tiled=True)

        def product(right):
            column = lax.all_gather(right, "row", axis=0, tiled=True)
            return jnp.dot(panel, column, preferred_element_type=jnp.float32)

        squared = (masks[2 * iteration + 1] * product(matrix)).astype(jnp.bfloat16)
        update = 1.5 * matrix.astype(jnp.float32) - 0.5 * product(squared)
        matrix = (masks[2 * iteration + 2] * update).astype(jnp.bfloat16)
    return matrix


def on_device(x_in, patterns):
    of_column, of_group = picks(patterns[0])
    column = pack(of_column, gather(x_in.reshape(8, BLOCK, BLOCK), "xx"))
    columns = gather(column, "yz")
    columns[1], patterns = lax.optimization_barrier((columns[1], patterns))
    fit, where, of_group = lax.optimization_barrier((fits(patterns), slots(patterns), of_group))
    group = pack(of_group, columns)
    pieces = gather(group, "zy")
    pieces[1], where = lax.optimization_barrier((pieces[1], where))
    lists, pieces[2] = lax.optimization_barrier((tables(*where), pieces[2]))
    pieces += [lax.ppermute(piece, "col", [(c, c ^ 1) for c in range(8)]) for piece in pieces]
    return lax.cond(
        fit,
        lambda: sparse_path(*lists, pieces),
        lambda: dense_path(x_in, patterns),
    )


def solution(mesh):
    placed = (P("row", ("col", "depth")), P())
    return jax.shard_map(
        on_device, mesh=mesh, in_specs=placed, out_specs=P("row", ("col", "depth")), check_vma=False
    )
```

```python
import functools

import jax
import jax.numpy as jnp
from jax import lax
from jax.experimental import pallas as pl
from jax.experimental.pallas import tpu as pltpu
from jax.sharding import PartitionSpec as P

BLOCK = 128
ITERS = 3
NB = 32
AXES = ("row", "col", "depth")

COLUMN_CAP = 17
GROUP_CAP = 50
CAP = 400
ZERO = 8 * GROUP_CAP
DUMMY = ZERO + 1
TILE = DUMMY + 1
S_BASE = TILE + 8
X_BASE = S_BASE + CAP
SLOTS = X_BASE + CAP
TERMS = 16
POSITIONS = 512
ROWS = 1152
CLASSES = ((16, 2), (8, 8), (6, 10), (5, 12), (4, 16), (3, 20), (2, 32), (1, 32), (0, 16))
STEPS = 2 * ITERS


def pack_kernel(pick_ref, *refs):
    sources, out_ref, blocks, sem = refs[:4], refs[4], refs[5], refs[6]
    length = sources[0].shape[0]
    for index, source in enumerate(sources):
        pltpu.make_async_copy(source, blocks.at[pl.ds(index * length, length)], sem).start()
    pltpu.make_async_copy(blocks, blocks, sem).wait()
    for p in range(out_ref.shape[0]):
        out_ref[p] = blocks[pick_ref[p]]


def pack(pick, sources):
    slots = pick.shape[0]
    return pl.pallas_call(
        pack_kernel,
        out_shape=jax.ShapeDtypeStruct((slots, BLOCK, BLOCK), jnp.bfloat16),
        in_specs=[pl.BlockSpec(memory_space=pltpu.SMEM)] + [pl.BlockSpec(memory_space=pl.ANY)] * 4,
        out_specs=pl.BlockSpec(memory_space=pltpu.VMEM),
        scratch_shapes=[
            pltpu.VMEM((4 * sources[0].shape[0], BLOCK, BLOCK), jnp.bfloat16),
            pltpu.SemaphoreType.DMA(()),
        ],
        compiler_params=pltpu.CompilerParams(vmem_limit_bytes=16 * 2**20),
        name="pack_blocks",
    )(pick, *sources)


def product_kernel(ent_ref, ox_ref, ord_ref, body_ref, *refs):
    pieces, out_ref, blocks, sem = refs[:8], refs[8], refs[9], refs[10]
    for index, piece in enumerate(pieces):
        pltpu.make_async_copy(piece, blocks.at[pl.ds(index * GROUP_CAP, GROUP_CAP)], sem).start()
    blocks[ZERO] = jnp.zeros((BLOCK, BLOCK), blocks.dtype)
    for b in range(8):
        blocks[TILE + b] = jnp.zeros((BLOCK, BLOCK), blocks.dtype)
    whole = blocks.at[pl.ds(0, ZERO)]
    pltpu.make_async_copy(whole, whole, sem).wait()

    def load(slot):
        return blocks[slot]

    def step(t, carry):
        is_update = (t & 1) == 1
        keep = jnp.where(is_update, 1.5, 0.0).astype(jnp.float32)
        scale = jnp.where(is_update, -0.5, 1.0).astype(jnp.float32)
        for index, (terms, width) in enumerate(CLASSES):
            first = body_ref[t, index * 2]
            count = body_ref[t, index * 2 + 1]

            def body(it, carry, terms=terms, width=width, first=first):
                results = []
                for u in range(width):
                    entry = ord_ref[t, first + it * width + u]
                    words = [ent_ref[t * TERMS + q, entry] for q in range(terms)]
                    lefts = [load(w & 0xFFFF) for w in words]
                    rights = [load(w >> 16) for w in words]
                    total = jnp.zeros((BLOCK, BLOCK), jnp.float32)
                    if terms == 1:
                        total = jnp.dot(lefts[0], rights[0], preferred_element_type=jnp.float32)
                    elif terms > 1:
                        left = jnp.concatenate(lefts, axis=1)
                        right = jnp.concatenate(rights, axis=0)
                        total = jnp.dot(left, right, preferred_element_type=jnp.float32)
                    ox = ox_ref[t, entry]
                    old = load(ox >> 16).astype(jnp.float32)
                    results.append((ox & 0xFFFF, (keep * old + scale * total).astype(jnp.bfloat16)))
                for slot, value in results:
                    blocks[slot] = value
                return carry

            lax.fori_loop(0, count, body, 0)
        return carry

    lax.fori_loop(0, STEPS, step, 0)
    copy = pltpu.make_async_copy(blocks.at[pl.ds(TILE, 8)], out_ref, sem)
    copy.start()
    copy.wait()


def start_groups(pattern):
    by_place = pattern.reshape(NB, 4, 2, 4)
    return jnp.stack([by_place[:, :, 0].transpose(1, 2, 0), by_place[:, :, 1].transpose(2, 1, 0)])


def ranks(mask):
    n = mask.shape[-1]
    before = (lax.iota(jnp.int32, n)[:, None] < lax.iota(jnp.int32, n)[None, :]).astype(jnp.bfloat16)
    flat = mask.reshape(-1, n).astype(jnp.bfloat16)
    return jnp.dot(flat, before, preferred_element_type=jnp.float32).astype(jnp.int32).reshape(mask.shape)


def lists_kernel(pattern_ref, ent_ref, ox_ref, ord_ref, body_ref, member_ref):
    f32, bf16, i32 = jnp.float32, jnp.bfloat16, jnp.int32
    row, col, my_y = (lax.axis_index(a) for a in AXES)
    my_column, my_core, my_z = col * 4 + my_y, col & 1, col >> 1
    flat_size = NB * NB

    def iota(shape, axis):
        return lax.broadcasted_iota(i32, shape, axis)

    def dot(a, b):
        return jnp.dot(a.astype(bf16), b.astype(bf16), preferred_element_type=f32)

    def exact(a, b, contract):
        return lax.dot_general(a, b, (contract, ((), ())), precision=lax.Precision.HIGHEST, preferred_element_type=f32)

    i, j = iota((NB, NB), 0), iota((NB, NB), 1)
    below, above = (j < i).astype(f32), (i < j).astype(f32)
    o = iota((NB, flat_size), 1)
    of_row = ((o >> 5) == iota((NB, flat_size), 0)).astype(f32)
    of_col = ((o & 31) == iota((NB, flat_size), 0)).astype(f32)

    def flat(v):
        return (of_row * exact(v, of_col, ((1,), (0,)))).sum(0, keepdims=True)

    pattern = [pattern_ref[t].astype(f32) for t in range(2 * ITERS + 1)]
    start = pattern[0]

    y, c, z = j & 3, (j >> 2) & 1, j >> 3
    y1, c1, z1 = i & 3, (i >> 2) & 1, i >> 3
    line = jnp.where(c == 0, z, y)
    along = jnp.where(c == 0, y, z)
    line1 = jnp.where(c1 == 0, z1, y1)
    along1 = jnp.where(c1 == 0, y1, z1)
    same = (c1 == c) & (line1 == line)
    in_line = dot(start, (same & (along1 < along)).astype(f32)).sum(0, keepdims=True)
    of_line = dot(start, same.astype(f32)).sum(0, keepdims=True)
    back = (jnp.where(c == 0, my_z, my_y) - line) & 3
    piece = jnp.where(c == my_core, 0, 4) + back
    slot0 = piece.astype(f32) * GROUP_CAP + in_line + dot(below, start)
    slot0 = jnp.where(start > 0, slot0, float(ZERO))
    fit = jnp.where(start.sum(0, keepdims=True).max(1, keepdims=True) <= COLUMN_CAP, 1, 0)
    fit = fit * jnp.where(of_line.max(1, keepdims=True) <= GROUP_CAP, 1, 0)

    mine = jnp.where(j == my_column, 1.0, 0.0)
    tile = mine * jnp.where((i >> 3) == row, 1.0, 0.0)
    outs = pattern[1:5] + [pattern[5] * mine, pattern[6] * tile]
    out_slot = []
    read_slot = []
    for t, base in enumerate((S_BASE, X_BASE, S_BASE, 0, S_BASE)):
        rank = dot(below, outs[t]).sum(1, keepdims=True) + dot(outs[t], above)
        out_slot.append(rank + float(base))
        read_slot.append(jnp.where(outs[t] > 0, out_slot[t], float(ZERO)))
        if t < 4:
            total = outs[t].sum(1, keepdims=True).sum(0, keepdims=True)
            fit = fit * jnp.where(total <= CAP, 1, 0)
    out_slot.append((TILE + i - 8 * row).astype(f32))
    left = [slot0, slot0, read_slot[1], read_slot[1], read_slot[3], read_slot[3]]
    right = [slot0, read_slot[0], read_slot[1], read_slot[2], read_slot[3], read_slot[4]]

    blank = ZERO + ZERO * 65536
    low_limits = [limit for limit, _ in CLASSES[1:]] + [-1]
    count_classes = len(CLASSES)
    ent_ref[:, pl.ds(flat_size, ROWS - flat_size)] = jnp.full((STEPS * TERMS, ROWS - flat_size), blank, i32)
    ox_ref[:, pl.ds(flat_size, ROWS - flat_size)] = jnp.full((8, ROWS - flat_size), DUMMY + ZERO * 65536, i32)
    member_ref[...] = jnp.zeros(member_ref.shape, f32)
    lives = []
    for t in range(STEPS):
        terms = dot(pattern[t - t % 2], pattern[t]) * pattern[t + 1]
        most = terms.max(1, keepdims=True).max(0, keepdims=True)
        fit = fit * jnp.where(most <= TERMS, 1, 0)

        wide_left = exact(left[t], of_row, ((0,), (0,))).astype(i32)
        wide_right = exact(right[t], of_col, ((1,), (0,))).astype(i32)
        live = flat(outs[t])
        lives.append(live)
        on = jnp.where((wide_left != ZERO) & (wide_right != ZERO), live, 0.0)
        place = jnp.where(on > 0, dot(below, on).astype(i32), TERMS)
        word = wide_left + wide_right * 65536 - blank
        for s in range(TERMS):
            found = jnp.where(place == s, word, 0).sum(0, keepdims=True)
            ent_ref[pl.ds(t * TERMS + s, 1), pl.ds(0, flat_size)] = found + blank
        slot = flat(out_slot[t]).astype(i32)
        old = flat(left[t]).astype(i32) if t % 2 else jnp.full((1, flat_size), ZERO, i32)
        ox_ref[pl.ds(t, 1), pl.ds(0, flat_size)] = slot + old * 65536
        count = on.sum(0, keepdims=True)
        for index, ((limit, _), low) in enumerate(zip(CLASSES, low_limits)):
            inside = (live > 0) & (count > low) & (count <= limit)
            member_ref[pl.ds(t * count_classes + index, 1), :] = jnp.where(inside, 1.0, 0.0)

    member = member_ref[...]
    earlier = iota((flat_size, flat_size), 0) < iota((flat_size, flat_size), 1)
    rank = dot(member, jnp.where(earlier, 1.0, 0.0))
    total = member.sum(1, keepdims=True)
    o_row = iota((8, flat_size), 1)
    o_part = iota((8, flat_size), 0)
    number = jnp.where(o_part == 0, o_row >> 5, jnp.where(o_part == 1, o_row & 31, jnp.where(o_part == 2, 1, 0)))
    lane = iota((1, 128), 1)
    for t in range(STEPS):
        position = jnp.zeros((1, flat_size), f32)
        ahead = jnp.zeros((1, 1), f32)
        end = jnp.zeros((1, 1), i32)
        body = jnp.zeros((1, 128), i32)
        for index, (_, width) in enumerate(CLASSES):
            at = t * count_classes + index
            position = position + member[at : at + 1] * (rank[at : at + 1] + ahead)
            ahead = ahead + total[at : at + 1]
            left_over = jnp.maximum(ahead.astype(i32) - end + (width - 1), 0)
            bodies = (left_over * -(-65536 // width)) >> 16
            body = jnp.where(lane == 2 * index, end, jnp.where(lane == 2 * index + 1, bodies, body))
            end = end + bodies * width
        body_ref[pl.ds(t, 1), :] = body
        position = jnp.where(lives[t] > 0, position, float(POSITIONS)).astype(i32)
        match = jnp.where(iota((POSITIONS, flat_size), 0) == position, 1.0, 0.0).astype(bf16)
        found = lax.dot_general(
            number.astype(f32).astype(bf16), match, (((1,), (1,)), ((), ())), preferred_element_type=f32
        )
        entry = found[0:1] * float(NB) + found[1:2]
        ord_ref[pl.ds(t, 1), :] = jnp.where(found[2:3] > 0, entry, float(flat_size)).astype(i32)
    body_ref[pl.ds(STEPS, 1), :] = jnp.broadcast_to(fit, (1, 128))


def lists(patterns):
    return pl.pallas_call(
        lists_kernel,
        out_shape=[
            jax.ShapeDtypeStruct((STEPS * TERMS, ROWS), jnp.int32),
            jax.ShapeDtypeStruct((8, ROWS), jnp.int32),
            jax.ShapeDtypeStruct((8, POSITIONS), jnp.int32),
            jax.ShapeDtypeStruct((8, 128), jnp.int32),
        ],
        in_specs=[pl.BlockSpec(memory_space=pltpu.VMEM)],
        out_specs=[pl.BlockSpec(memory_space=pltpu.VMEM)] * 4,
        scratch_shapes=[pltpu.VMEM((STEPS * len(CLASSES) + 2, NB * NB), jnp.float32)],
        compiler_params=pltpu.CompilerParams(vmem_limit_bytes=24 * 2**20),
        name="build_lists",
    )(patterns)


def my_place():
    row, col, depth = (lax.axis_index(a) for a in AXES)
    return row, col * 4 + depth, (col % 2, col // 2, depth)


def picked(mask, value, slots):
    place = jnp.where(mask > 0, ranks(mask[None])[0], slots)
    hit = place[None, :] == lax.iota(jnp.int32, slots)[:, None]
    return jnp.where(hit, value[None, :], 0).sum(-1)


def picks(pattern):
    row, column, (core, z, y) = my_place()
    i = lax.iota(jnp.int32, NB)
    mine = lax.dynamic_index_in_dim(pattern, column, 1, keepdims=False)
    of_column = picked(mine, ((row - i // 8) % 4) * 8 + i % 8, COLUMN_CAP)
    line = core * 4 + jnp.where(core == 0, z, y)
    along = jnp.where(core == 0, y, z)
    group = lax.dynamic_index_in_dim(start_groups(pattern).reshape(8, 4, NB), line, 0, keepdims=False)
    source = (along - lax.iota(jnp.int32, 4)) % 4
    value = source[:, None] * COLUMN_CAP + jnp.minimum(ranks(group), COLUMN_CAP - 1)
    of_group = picked(group.reshape(4 * NB), value.reshape(4 * NB), GROUP_CAP)
    return of_column, of_group


def hops(axes, shift):
    pairs = []
    for x in range(4):
        for z in range(4):
            for c in range(2):
                for y in range(4):
                    to = {"x": x, "y": y, "z": z}
                    to[axes[c]] = (to[axes[c]] + shift) % 4
                    pairs.append((((x * 4 + z) * 2 + c) * 4 + y, ((to["x"] * 4 + to["z"]) * 2 + c) * 4 + to["y"]))
    return pairs


def gather(mine, axes):
    far = {shift: lax.ppermute(mine, AXES, hops(axes, shift)) for shift in (1, 3, 2)}
    return [mine, far[1], far[2], far[3]]


def sparse_path(ent, ox, entry, body, pieces):
    smem = pl.BlockSpec(memory_space=pltpu.SMEM)
    out = pl.pallas_call(
        product_kernel,
        out_shape=jax.ShapeDtypeStruct((8, BLOCK, BLOCK), jnp.bfloat16),
        in_specs=[smem] * 4 + [pl.BlockSpec(memory_space=pl.ANY)] * 8,
        out_specs=pl.BlockSpec(memory_space=pl.ANY),
        scratch_shapes=[pltpu.VMEM((SLOTS, BLOCK, BLOCK), jnp.bfloat16), pltpu.SemaphoreType.DMA(())],
        compiler_params=pltpu.CompilerParams(vmem_limit_bytes=56 * 2**20),
        name="block_products",
    )(ent, ox, entry, body, *pieces)
    return out.reshape(8 * BLOCK, BLOCK)


def tile_mask(pattern, row_first, col_first, tile_rows, tile_cols):
    blocks = pattern.shape[0]
    slab = lax.dynamic_slice_in_dim(pattern, row_first // BLOCK, tile_rows // BLOCK, 0).astype(jnp.float32)
    col_block = (col_first + lax.iota(jnp.int32, tile_cols)) // BLOCK
    onehot = (col_block[None, :] == lax.iota(jnp.int32, blocks)[:, None]).astype(jnp.float32)
    coarse = jnp.dot(slab, onehot)
    spread_rows = jnp.broadcast_to(coarse[:, None, :], (tile_rows // BLOCK, BLOCK, tile_cols))
    return spread_rows.reshape(tile_rows, tile_cols)


def dense_path(x_in, patterns):
    tile_rows, tile_width = x_in.shape
    row_first = lax.axis_index("row") * tile_rows
    col_first = (lax.axis_index("col") * lax.axis_size("depth") + lax.axis_index("depth")) * tile_width
    masks = [tile_mask(patterns[p], row_first, col_first, tile_rows, tile_width) for p in range(2 * ITERS + 1)]
    matrix = (x_in * masks[0]).astype(jnp.bfloat16)
    for iteration in range(ITERS):
        panel = lax.all_gather(matrix, ("col", "depth"), axis=1, tiled=True)

        def product(right):
            column = lax.all_gather(right, "row", axis=0, tiled=True)
            return jnp.dot(panel, column, preferred_element_type=jnp.float32)

        squared = (masks[2 * iteration + 1] * product(matrix)).astype(jnp.bfloat16)
        update = 1.5 * matrix.astype(jnp.float32) - 0.5 * product(squared)
        matrix = (masks[2 * iteration + 2] * update).astype(jnp.bfloat16)
    return matrix


def on_device(x_in, patterns):
    of_column, of_group = picks(patterns[0])
    column = pack(of_column, gather(x_in.reshape(8, BLOCK, BLOCK), "xx"))
    columns = gather(column, "yz")
    group = pack(of_group, columns)
    pieces = gather(group, "zy")
    pieces[1], patterns = lax.optimization_barrier((pieces[1], patterns))
    tables = lists(patterns)
    tables, pieces[2] = lax.optimization_barrier((tables, pieces[2]))
    pieces += [lax.ppermute(piece, "col", [(c, c ^ 1) for c in range(8)]) for piece in pieces]
    return lax.cond(
        tables[3][STEPS, 0] > 0,
        lambda: sparse_path(*tables, pieces),
        lambda: dense_path(x_in, patterns),
    )


def solution(mesh):
    placed = (P("row", ("col", "depth")), P())
    return jax.shard_map(
        on_device, mesh=mesh, in_specs=placed, out_specs=P("row", ("col", "depth")), check_vma=False
    )
```

```python
import functools

import jax
import jax.numpy as jnp
from jax import lax
from jax.experimental import pallas as pl
from jax.experimental.pallas import tpu as pltpu
from jax.sharding import PartitionSpec as P

BLOCK = 128
ITERS = 3
NB = 32
AXES = ("row", "col", "depth")

LINE_CAP = 19
GROUP_CAP = 50
HALF = GROUP_CAP // 2
CAP = 400
ZERO = 8 * GROUP_CAP
DUMMY = ZERO + 1
TILE = DUMMY + 1
S_BASE = TILE + 8
X_BASE = S_BASE + CAP
SLOTS = X_BASE + CAP
TERMS = 16
POSITIONS = 512
ROWS = 1152
CLASSES = ((16, 2), (8, 8), (6, 10), (5, 12), (4, 16), (3, 20), (2, 32), (1, 32), (0, 16))
STEPS = 2 * ITERS


def pack_kernel(pick_ref, *refs):
    sources, outs, blocks, sem = refs[:4], refs[4:-2], refs[-2], refs[-1]
    length = sources[0].shape[0]
    for index, source in enumerate(sources):
        pltpu.make_async_copy(source, blocks.at[pl.ds(index * length, length)], sem).start()
    pltpu.make_async_copy(blocks, blocks, sem).wait()
    first = 0
    for out_ref in outs:
        for p in range(out_ref.shape[0]):
            out_ref[p] = blocks[pick_ref[first + p]]
        first += out_ref.shape[0]


def pack(pick, sources, parts):
    return pl.pallas_call(
        pack_kernel,
        out_shape=[jax.ShapeDtypeStruct((pick.shape[0] // parts, BLOCK, BLOCK), jnp.bfloat16)] * parts,
        in_specs=[pl.BlockSpec(memory_space=pltpu.SMEM)] + [pl.BlockSpec(memory_space=pl.ANY)] * 4,
        out_specs=[pl.BlockSpec(memory_space=pltpu.VMEM)] * parts,
        scratch_shapes=[
            pltpu.VMEM((4 * sources[0].shape[0], BLOCK, BLOCK), jnp.bfloat16),
            pltpu.SemaphoreType.DMA(()),
        ],
        compiler_params=pltpu.CompilerParams(vmem_limit_bytes=16 * 2**20),
        name="pack_blocks",
    )(pick, *sources)


def product_kernel(ent_ref, ox_ref, ord_ref, body_ref, *refs):
    pieces, out_ref, blocks, sem = refs[:16], refs[16], refs[17], refs[18]
    for index, piece in enumerate(pieces):
        pltpu.make_async_copy(piece, blocks.at[pl.ds(index * HALF, HALF)], sem).start()
    blocks[ZERO] = jnp.zeros((BLOCK, BLOCK), blocks.dtype)
    for b in range(8):
        blocks[TILE + b] = jnp.zeros((BLOCK, BLOCK), blocks.dtype)
    whole = blocks.at[pl.ds(0, ZERO)]
    pltpu.make_async_copy(whole, whole, sem).wait()

    def load(slot):
        return blocks[slot]

    def step(t, carry):
        is_update = (t & 1) == 1
        keep = jnp.where(is_update, 1.5, 0.0).astype(jnp.float32)
        scale = jnp.where(is_update, -0.5, 1.0).astype(jnp.float32)
        for index, (terms, width) in enumerate(CLASSES):
            first = body_ref[t, index * 2]
            count = body_ref[t, index * 2 + 1]

            def body(it, carry, terms=terms, width=width, first=first):
                results = []
                for u in range(width):
                    entry = ord_ref[t, first + it * width + u]
                    words = [ent_ref[t * TERMS + q, entry] for q in range(terms)]
                    lefts = [load(w & 0xFFFF) for w in words]
                    rights = [load(w >> 16) for w in words]
                    total = jnp.zeros((BLOCK, BLOCK), jnp.float32)
                    if terms == 1:
                        total = jnp.dot(lefts[0], rights[0], preferred_element_type=jnp.float32)
                    elif terms > 1:
                        left = jnp.concatenate(lefts, axis=1)
                        right = jnp.concatenate(rights, axis=0)
                        total = jnp.dot(left, right, preferred_element_type=jnp.float32)
                    ox = ox_ref[t, entry]
                    old = load(ox >> 16).astype(jnp.float32)
                    results.append((ox & 0xFFFF, (keep * old + scale * total).astype(jnp.bfloat16)))
                for slot, value in results:
                    blocks[slot] = value
                return carry

            lax.fori_loop(0, count, body, 0)
        return carry

    lax.fori_loop(0, STEPS, step, 0)
    copy = pltpu.make_async_copy(blocks.at[pl.ds(TILE, 8)], out_ref, sem)
    copy.start()
    copy.wait()


def ranks(mask):
    n = mask.shape[-1]
    before = (lax.iota(jnp.int32, n)[:, None] < lax.iota(jnp.int32, n)[None, :]).astype(jnp.bfloat16)
    flat = mask.reshape(-1, n).astype(jnp.bfloat16)
    return jnp.dot(flat, before, preferred_element_type=jnp.float32).astype(jnp.int32).reshape(mask.shape)


def lists_kernel(pattern_ref, ent_ref, ox_ref, ord_ref, body_ref, member_ref):
    f32, bf16, i32 = jnp.float32, jnp.bfloat16, jnp.int32
    row, col, my_y = (lax.axis_index(a) for a in AXES)
    my_column, my_core, my_z = col * 4 + my_y, col & 1, col >> 1
    flat_size = NB * NB

    def iota(shape, axis):
        return lax.broadcasted_iota(i32, shape, axis)

    def dot(a, b):
        return jnp.dot(a.astype(bf16), b.astype(bf16), preferred_element_type=f32)

    def exact(a, b, contract):
        return lax.dot_general(a, b, (contract, ((), ())), precision=lax.Precision.HIGHEST, preferred_element_type=f32)

    i, j = iota((NB, NB), 0), iota((NB, NB), 1)
    below, above = (j < i).astype(f32), (i < j).astype(f32)
    o = iota((NB, flat_size), 1)
    of_row = ((o >> 5) == iota((NB, flat_size), 0)).astype(f32)
    of_col = ((o & 31) == iota((NB, flat_size), 0)).astype(f32)

    def flat(v):
        return (of_row * exact(v, of_col, ((1,), (0,)))).sum(0, keepdims=True)

    pattern = [pattern_ref[t].astype(f32) for t in range(2 * ITERS + 1)]
    start = pattern[0]

    y, c, z = j & 3, (j >> 2) & 1, j >> 3
    y1, c1, z1 = i & 3, (i >> 2) & 1, i >> 3
    line = jnp.where(c == 0, z, y)
    along = jnp.where(c == 0, y, z)
    line1 = jnp.where(c1 == 0, z1, y1)
    along1 = jnp.where(c1 == 0, y1, z1)
    same = ((c1 == c) & (line1 == line)).astype(f32)
    sooner = same * (along1 < along).astype(f32)
    band = ((i >> 3) == (j >> 3)).astype(f32)
    band_below = ((j >> 3) < (i >> 3)).astype(f32)
    in_line = dot(start, same)
    sooner_in_line = dot(start, sooner)
    rank0 = sooner_in_line.sum(0, keepdims=True) + dot(below, start)
    rank1 = dot(band_below, in_line) + dot(band, sooner_in_line) + dot(below * band, start)
    back = (jnp.where(c == 0, my_z, my_y) - line) & 3
    piece = jnp.where(c == my_core, 0, 4) + back
    slot0 = piece.astype(f32) * GROUP_CAP + jnp.where(c == 0, rank0, rank1)
    slot0 = jnp.where(start > 0, slot0, float(ZERO))
    in_tiles = jnp.where(c == 0, start.sum(0, keepdims=True), dot(band, in_line))
    in_group = in_line.sum(0, keepdims=True)
    fit = jnp.where(in_tiles.max(0, keepdims=True).max(1, keepdims=True) <= LINE_CAP, 1, 0)
    fit = fit * jnp.where(in_group.max(1, keepdims=True) <= GROUP_CAP, 1, 0)

    mine = jnp.where(j == my_column, 1.0, 0.0)
    tile = mine * jnp.where((i >> 3) == row, 1.0, 0.0)
    outs = pattern[1:5] + [pattern[5] * mine, pattern[6] * tile]
    out_slot = []
    read_slot = []
    for t, base in enumerate((S_BASE, X_BASE, S_BASE, 0, S_BASE)):
        rank = dot(below, outs[t]).sum(1, keepdims=True) + dot(outs[t], above)
        out_slot.append(rank + float(base))
        read_slot.append(jnp.where(outs[t] > 0, out_slot[t], float(ZERO)))
        if t < 4:
            total = outs[t].sum(1, keepdims=True).sum(0, keepdims=True)
            fit = fit * jnp.where(total <= CAP, 1, 0)
    out_slot.append((TILE + i - 8 * row).astype(f32))
    left = [slot0, slot0, read_slot[1], read_slot[1], read_slot[3], read_slot[3]]
    right = [slot0, read_slot[0], read_slot[1], read_slot[2], read_slot[3], read_slot[4]]

    blank = ZERO + ZERO * 65536
    low_limits = [limit for limit, _ in CLASSES[1:]] + [-1]
    count_classes = len(CLASSES)
    ent_ref[:, pl.ds(flat_size, ROWS - flat_size)] = jnp.full((STEPS * TERMS, ROWS - flat_size), blank, i32)
    ox_ref[:, pl.ds(flat_size, ROWS - flat_size)] = jnp.full((8, ROWS - flat_size), DUMMY + ZERO * 65536, i32)
    member_ref[...] = jnp.zeros(member_ref.shape, f32)
    lives = []
    for t in range(STEPS):
        terms = dot(pattern[t - t % 2], pattern[t]) * pattern[t + 1]
        most = terms.max(1, keepdims=True).max(0, keepdims=True)
        fit = fit * jnp.where(most <= TERMS, 1, 0)

        wide_left = exact(left[t], of_row, ((0,), (0,))).astype(i32)
        wide_right = exact(right[t], of_col, ((1,), (0,))).astype(i32)
        live = flat(outs[t])
        lives.append(live)
        on = jnp.where((wide_left != ZERO) & (wide_right != ZERO), live, 0.0)
        place = jnp.where(on > 0, dot(below, on).astype(i32), TERMS)
        word = wide_left + wide_right * 65536 - blank
        for s in range(TERMS):
            found = jnp.where(place == s, word, 0).sum(0, keepdims=True)
            ent_ref[pl.ds(t * TERMS + s, 1), pl.ds(0, flat_size)] = found + blank
        slot = flat(out_slot[t]).astype(i32)
        old = flat(left[t]).astype(i32) if t % 2 else jnp.full((1, flat_size), ZERO, i32)
        ox_ref[pl.ds(t, 1), pl.ds(0, flat_size)] = slot + old * 65536
        count = on.sum(0, keepdims=True)
        for index, ((limit, _), low) in enumerate(zip(CLASSES, low_limits)):
            inside = (live > 0) & (count > low) & (count <= limit)
            member_ref[pl.ds(t * count_classes + index, 1), :] = jnp.where(inside, 1.0, 0.0)

    member = member_ref[...]
    earlier = iota((flat_size, flat_size), 0) < iota((flat_size, flat_size), 1)
    rank = dot(member, jnp.where(earlier, 1.0, 0.0))
    total = member.sum(1, keepdims=True)
    o_row = iota((8, flat_size), 1)
    o_part = iota((8, flat_size), 0)
    number = jnp.where(o_part == 0, o_row >> 5, jnp.where(o_part == 1, o_row & 31, jnp.where(o_part == 2, 1, 0)))
    lane = iota((1, 128), 1)
    for t in range(STEPS):
        position = jnp.zeros((1, flat_size), f32)
        ahead = jnp.zeros((1, 1), f32)
        end = jnp.zeros((1, 1), i32)
        body = jnp.zeros((1, 128), i32)
        for index, (_, width) in enumerate(CLASSES):
            at = t * count_classes + index
            position = position + member[at : at + 1] * (rank[at : at + 1] + ahead)
            ahead = ahead + total[at : at + 1]
            left_over = jnp.maximum(ahead.astype(i32) - end + (width - 1), 0)
            bodies = (left_over * -(-65536 // width)) >> 16
            body = jnp.where(lane == 2 * index, end, jnp.where(lane == 2 * index + 1, bodies, body))
            end = end + bodies * width
        body_ref[pl.ds(t, 1), :] = body
        position = jnp.where(lives[t] > 0, position, float(POSITIONS)).astype(i32)
        match = jnp.where(iota((POSITIONS, flat_size), 0) == position, 1.0, 0.0).astype(bf16)
        found = lax.dot_general(
            number.astype(f32).astype(bf16), match, (((1,), (1,)), ((), ())), preferred_element_type=f32
        )
        entry = found[0:1] * float(NB) + found[1:2]
        ord_ref[pl.ds(t, 1), :] = jnp.where(found[2:3] > 0, entry, float(flat_size)).astype(i32)
    body_ref[pl.ds(STEPS, 1), :] = jnp.broadcast_to(fit, (1, 128))


def lists(patterns):
    return pl.pallas_call(
        lists_kernel,
        out_shape=[
            jax.ShapeDtypeStruct((STEPS * TERMS, ROWS), jnp.int32),
            jax.ShapeDtypeStruct((8, ROWS), jnp.int32),
            jax.ShapeDtypeStruct((8, POSITIONS), jnp.int32),
            jax.ShapeDtypeStruct((8, 128), jnp.int32),
        ],
        in_specs=[pl.BlockSpec(memory_space=pltpu.VMEM)],
        out_specs=[pl.BlockSpec(memory_space=pltpu.VMEM)] * 4,
        scratch_shapes=[pltpu.VMEM((STEPS * len(CLASSES) + 2, NB * NB), jnp.float32)],
        compiler_params=pltpu.CompilerParams(vmem_limit_bytes=24 * 2**20),
        name="build_lists",
    )(patterns)


def my_place():
    row, col, depth = (lax.axis_index(a) for a in AXES)
    return row, col * 4 + depth, (col % 2, col // 2, depth)


def picked(mask, value, slots):
    place = jnp.where(mask > 0, ranks(mask[None])[0], slots)
    hit = place[None, :] == lax.iota(jnp.int32, slots)[:, None]
    return jnp.where(hit, value[None, :], 0).sum(-1)


def picks(pattern):
    x, _, (core, z, y) = my_place()
    by_place = pattern.reshape(4, 8, 4, 2, 4)
    lines0 = lax.dynamic_index_in_dim(by_place[:, :, :, 0], z, 2, keepdims=False).transpose(2, 0, 1)
    lines1 = lax.dynamic_index_in_dim(by_place[:, :, :, 1], y, 3, keepdims=False).transpose(0, 2, 1)
    lines = jnp.where(core == 0, lines0, lines1).reshape(4, 32)
    at1, at2 = jnp.where(core == 0, x, z), jnp.where(core == 0, y, x)
    e = lax.iota(jnp.int32, 32)
    line = lax.dynamic_index_in_dim(lines, at2, 0, keepdims=False)
    of_line = picked(line, ((at1 - e // 8) & 3) * 8 + e % 8, LINE_CAP)
    back = (at2 - lax.iota(jnp.int32, 4)) & 3
    value = back[:, None] * LINE_CAP + jnp.minimum(ranks(lines), LINE_CAP - 1)
    of_group = picked(lines.reshape(4 * 32), value.reshape(4 * 32), GROUP_CAP)
    return of_line, of_group


def hops(axes, shift):
    pairs = []
    for x in range(4):
        for z in range(4):
            for c in range(2):
                for y in range(4):
                    to = {"x": x, "y": y, "z": z}
                    to[axes[c]] = (to[axes[c]] + shift) % 4
                    pairs.append((((x * 4 + z) * 2 + c) * 4 + y, ((to["x"] * 4 + to["z"]) * 2 + c) * 4 + to["y"]))
    return pairs


def send(mine, axes, shift):
    return lax.ppermute(mine, AXES, hops(axes, shift))


def gather(mine, axes):
    far = {shift: send(mine, axes, shift) for shift in (1, 3, 2)}
    return [mine, far[1], far[2], far[3]]


def gather_halves(a, b, axes):
    a1, b3 = send(a, axes, 1), send(b, axes, 3)
    b1, a3 = send(b, axes, 1), send(a, axes, 3)
    a2, b2 = send(a1, axes, 1), send(b3, axes, 3)
    return [a, b, a1, b1, a2, b2, a3, b3]


def sparse_path(ent, ox, entry, body, pieces):
    smem = pl.BlockSpec(memory_space=pltpu.SMEM)
    out = pl.pallas_call(
        product_kernel,
        out_shape=jax.ShapeDtypeStruct((8, BLOCK, BLOCK), jnp.bfloat16),
        in_specs=[smem] * 4 + [pl.BlockSpec(memory_space=pl.ANY)] * 16,
        out_specs=pl.BlockSpec(memory_space=pl.ANY),
        scratch_shapes=[pltpu.VMEM((SLOTS, BLOCK, BLOCK), jnp.bfloat16), pltpu.SemaphoreType.DMA(())],
        compiler_params=pltpu.CompilerParams(vmem_limit_bytes=56 * 2**20),
        name="block_products",
    )(ent, ox, entry, body, *pieces)
    return out.reshape(8 * BLOCK, BLOCK)


def tile_mask(pattern, row_first, col_first, tile_rows, tile_cols):
    blocks = pattern.shape[0]
    slab = lax.dynamic_slice_in_dim(pattern, row_first // BLOCK, tile_rows // BLOCK, 0).astype(jnp.float32)
    col_block = (col_first + lax.iota(jnp.int32, tile_cols)) // BLOCK
    onehot = (col_block[None, :] == lax.iota(jnp.int32, blocks)[:, None]).astype(jnp.float32)
    coarse = jnp.dot(slab, onehot)
    spread_rows = jnp.broadcast_to(coarse[:, None, :], (tile_rows // BLOCK, BLOCK, tile_cols))
    return spread_rows.reshape(tile_rows, tile_cols)


def dense_path(x_in, patterns):
    tile_rows, tile_width = x_in.shape
    row_first = lax.axis_index("row") * tile_rows
    col_first = (lax.axis_index("col") * lax.axis_size("depth") + lax.axis_index("depth")) * tile_width
    masks = [tile_mask(patterns[p], row_first, col_first, tile_rows, tile_width) for p in range(2 * ITERS + 1)]
    matrix = (x_in * masks[0]).astype(jnp.bfloat16)
    for iteration in range(ITERS):
        panel = lax.all_gather(matrix, ("col", "depth"), axis=1, tiled=True)

        def product(right):
            column = lax.all_gather(right, "row", axis=0, tiled=True)
            return jnp.dot(panel, column, preferred_element_type=jnp.float32)

        squared = (masks[2 * iteration + 1] * product(matrix)).astype(jnp.bfloat16)
        update = 1.5 * matrix.astype(jnp.float32) - 0.5 * product(squared)
        matrix = (masks[2 * iteration + 2] * update).astype(jnp.bfloat16)
    return matrix


def on_device(x_in, patterns):
    of_line, of_group = picks(patterns[0])
    (line,) = pack(of_line, gather(x_in.reshape(8, BLOCK, BLOCK), "xz"), 1)
    a, b = pack(of_group, gather(line, "yx"), 2)
    pieces = gather_halves(a, b, "zy")
    pieces[2], patterns = lax.optimization_barrier((pieces[2], patterns))
    tables = lists(patterns)
    tables, pieces[4] = lax.optimization_barrier((tables, pieces[4]))
    pieces += [lax.ppermute(piece, "col", [(c, c ^ 1) for c in range(8)]) for piece in pieces]
    return lax.cond(
        tables[3][STEPS, 0] > 0,
        lambda: sparse_path(*tables, pieces),
        lambda: dense_path(x_in, patterns),
    )


def solution(mesh):
    placed = (P("row", ("col", "depth")), P())
    return jax.shard_map(
        on_device, mesh=mesh, in_specs=placed, out_specs=P("row", ("col", "depth")), check_vma=False
    )
```

```python
import functools

import jax
import jax.numpy as jnp
from jax import lax
from jax.experimental import pallas as pl
from jax.experimental.pallas import tpu as pltpu
from jax.sharding import PartitionSpec as P

BLOCK = 128
ITERS = 3
NB = 32
AXES = ("row", "col", "depth")

LINE_CAP = 19
GROUP_CAP = 50
HALF = GROUP_CAP // 2
CAP = 400
ZERO = 8 * GROUP_CAP
DUMMY = ZERO + 1
TILE = DUMMY + 1
S_BASE = TILE + 8
X_BASE = S_BASE + CAP
SLOTS = X_BASE + CAP
TERMS = 16
POSITIONS = 512
ROWS = 1152
CLASSES = ((16, 2), (8, 8), (6, 10), (5, 12), (4, 16), (3, 20), (2, 32), (1, 32), (0, 16))
STEPS = 2 * ITERS


def pack_kernel(pick_ref, *refs):
    sources, outs, blocks, sem = refs[:4], refs[4:-2], refs[-2], refs[-1]
    length = sources[0].shape[0]
    for index, source in enumerate(sources):
        pltpu.make_async_copy(source, blocks.at[pl.ds(index * length, length)], sem).start()
    pltpu.make_async_copy(blocks, blocks, sem).wait()
    first = 0
    for out_ref in outs:
        for p in range(out_ref.shape[0]):
            out_ref[p] = blocks[pick_ref[first + p]]
        first += out_ref.shape[0]


def pack(pick, sources, parts):
    return pl.pallas_call(
        pack_kernel,
        out_shape=[jax.ShapeDtypeStruct((pick.shape[0] // parts, BLOCK, BLOCK), jnp.bfloat16)] * parts,
        in_specs=[pl.BlockSpec(memory_space=pltpu.SMEM)] + [pl.BlockSpec(memory_space=pl.ANY)] * 4,
        out_specs=[pl.BlockSpec(memory_space=pltpu.VMEM)] * parts,
        scratch_shapes=[
            pltpu.VMEM((4 * sources[0].shape[0], BLOCK, BLOCK), jnp.bfloat16),
            pltpu.SemaphoreType.DMA(()),
        ],
        compiler_params=pltpu.CompilerParams(vmem_limit_bytes=16 * 2**20),
        name="pack_blocks",
    )(pick, *sources)


def product_kernel(*refs):
    tables, pieces, out_ref, blocks, sem = refs[:4], refs[4:20], refs[20], refs[21], refs[22]
    ent_ref, ox_ref, ord_ref, body_ref = refs[23:27]
    table_sem = refs[27]
    copies = [
        pltpu.make_async_copy(table, kept, table_sem.at[index])
        for index, (table, kept) in enumerate(zip(tables, refs[23:27]))
    ]
    for copy in copies:
        copy.start()
    for index, piece in enumerate(pieces):
        pltpu.make_async_copy(piece, blocks.at[pl.ds(index * HALF, HALF)], sem).start()
    blocks[ZERO] = jnp.zeros((BLOCK, BLOCK), blocks.dtype)
    for b in range(8):
        blocks[TILE + b] = jnp.zeros((BLOCK, BLOCK), blocks.dtype)
    whole = blocks.at[pl.ds(0, ZERO)]
    pltpu.make_async_copy(whole, whole, sem).wait()
    for copy in copies:
        copy.wait()

    def load(slot):
        return blocks[slot]

    def step(t, carry):
        is_update = (t & 1) == 1
        keep = jnp.where(is_update, 1.5, 0.0).astype(jnp.float32)
        scale = jnp.where(is_update, -0.5, 1.0).astype(jnp.float32)
        for index, (terms, width) in enumerate(CLASSES):
            first = body_ref[t, index * 2]
            count = body_ref[t, index * 2 + 1]

            def body(it, carry, terms=terms, width=width, first=first):
                results = []
                for u in range(width):
                    entry = ord_ref[t, first + it * width + u]
                    words = [ent_ref[t * TERMS + q, entry] for q in range(terms)]
                    lefts = [load(w & 0xFFFF) for w in words]
                    rights = [load(w >> 16) for w in words]
                    total = jnp.zeros((BLOCK, BLOCK), jnp.float32)
                    if terms == 1:
                        total = jnp.dot(lefts[0], rights[0], preferred_element_type=jnp.float32)
                    elif terms > 1:
                        left = jnp.concatenate(lefts, axis=1)
                        right = jnp.concatenate(rights, axis=0)
                        total = jnp.dot(left, right, preferred_element_type=jnp.float32)
                    ox = ox_ref[t, entry]
                    old = load(ox >> 16).astype(jnp.float32)
                    results.append((ox & 0xFFFF, (keep * old + scale * total).astype(jnp.bfloat16)))
                for slot, value in results:
                    blocks[slot] = value
                return carry

            lax.fori_loop(0, count, body, 0)
        return carry

    lax.fori_loop(0, STEPS, step, 0)
    copy = pltpu.make_async_copy(blocks.at[pl.ds(TILE, 8)], out_ref, sem)
    copy.start()
    copy.wait()


def ranks(mask):
    n = mask.shape[-1]
    before = (lax.iota(jnp.int32, n)[:, None] < lax.iota(jnp.int32, n)[None, :]).astype(jnp.bfloat16)
    flat = mask.reshape(-1, n).astype(jnp.bfloat16)
    return jnp.dot(flat, before, preferred_element_type=jnp.float32).astype(jnp.int32).reshape(mask.shape)


def lists_kernel(pattern_ref, ent_ref, ox_ref, ord_ref, body_ref, member_ref):
    f32, bf16, i32 = jnp.float32, jnp.bfloat16, jnp.int32
    row, col, my_y = (lax.axis_index(a) for a in AXES)
    my_column, my_core, my_z = col * 4 + my_y, col & 1, col >> 1
    flat_size = NB * NB

    def iota(shape, axis):
        return lax.broadcasted_iota(i32, shape, axis)

    def dot(a, b):
        return jnp.dot(a.astype(bf16), b.astype(bf16), preferred_element_type=f32)

    def exact(a, b, contract):
        return lax.dot_general(a, b, (contract, ((), ())), precision=lax.Precision.HIGHEST, preferred_element_type=f32)

    i, j = iota((NB, NB), 0), iota((NB, NB), 1)
    below, above = (j < i).astype(f32), (i < j).astype(f32)
    o = iota((NB, flat_size), 1)
    of_row = ((o >> 5) == iota((NB, flat_size), 0)).astype(f32)
    of_col = ((o & 31) == iota((NB, flat_size), 0)).astype(f32)

    def flat(v):
        return (of_row * exact(v, of_col, ((1,), (0,)))).sum(0, keepdims=True)

    pattern = [pattern_ref[t].astype(f32) for t in range(2 * ITERS + 1)]
    start = pattern[0]

    y, c, z = j & 3, (j >> 2) & 1, j >> 3
    y1, c1, z1 = i & 3, (i >> 2) & 1, i >> 3
    line = jnp.where(c == 0, z, y)
    along = jnp.where(c == 0, y, z)
    line1 = jnp.where(c1 == 0, z1, y1)
    along1 = jnp.where(c1 == 0, y1, z1)
    same = ((c1 == c) & (line1 == line)).astype(f32)
    sooner = same * (along1 < along).astype(f32)
    band = ((i >> 3) == (j >> 3)).astype(f32)
    band_below = ((j >> 3) < (i >> 3)).astype(f32)
    in_line = dot(start, same)
    sooner_in_line = dot(start, sooner)
    rank0 = sooner_in_line.sum(0, keepdims=True) + dot(below, start)
    rank1 = dot(band_below, in_line) + dot(band, sooner_in_line) + dot(below * band, start)
    back = (jnp.where(c == 0, my_z, my_y) - line) & 3
    piece = jnp.where(c == my_core, 0, 4) + back
    slot0 = piece.astype(f32) * GROUP_CAP + jnp.where(c == 0, rank0, rank1)
    slot0 = jnp.where(start > 0, slot0, float(ZERO))
    in_tiles = jnp.where(c == 0, start.sum(0, keepdims=True), dot(band, in_line))
    in_group = in_line.sum(0, keepdims=True)
    fit = jnp.where(in_tiles.max(0, keepdims=True).max(1, keepdims=True) <= LINE_CAP, 1, 0)
    fit = fit * jnp.where(in_group.max(1, keepdims=True) <= GROUP_CAP, 1, 0)

    mine = jnp.where(j == my_column, 1.0, 0.0)
    tile = mine * jnp.where((i >> 3) == row, 1.0, 0.0)
    outs = pattern[1:5] + [pattern[5] * mine, pattern[6] * tile]
    out_slot = []
    read_slot = []
    for t, base in enumerate((S_BASE, X_BASE, S_BASE, 0, S_BASE)):
        rank = dot(below, outs[t]).sum(1, keepdims=True) + dot(outs[t], above)
        out_slot.append(rank + float(base))
        read_slot.append(jnp.where(outs[t] > 0, out_slot[t], float(ZERO)))
        if t < 4:
            total = outs[t].sum(1, keepdims=True).sum(0, keepdims=True)
            fit = fit * jnp.where(total <= CAP, 1, 0)
    out_slot.append((TILE + i - 8 * row).astype(f32))
    left = [slot0, slot0, read_slot[1], read_slot[1], read_slot[3], read_slot[3]]
    right = [slot0, read_slot[0], read_slot[1], read_slot[2], read_slot[3], read_slot[4]]

    blank = ZERO + ZERO * 65536
    low_limits = [limit for limit, _ in CLASSES[1:]] + [-1]
    count_classes = len(CLASSES)
    ent_ref[:, pl.ds(flat_size, ROWS - flat_size)] = jnp.full((STEPS * TERMS, ROWS - flat_size), blank, i32)
    ox_ref[:, pl.ds(flat_size, ROWS - flat_size)] = jnp.full((8, ROWS - flat_size), DUMMY + ZERO * 65536, i32)
    member_ref[...] = jnp.zeros(member_ref.shape, f32)
    lives = []
    for t in range(STEPS):
        terms = dot(pattern[t - t % 2], pattern[t]) * pattern[t + 1]
        most = terms.max(1, keepdims=True).max(0, keepdims=True)
        fit = fit * jnp.where(most <= TERMS, 1, 0)

        wide_left = exact(left[t], of_row, ((0,), (0,))).astype(i32)
        wide_right = exact(right[t], of_col, ((1,), (0,))).astype(i32)
        live = flat(outs[t])
        lives.append(live)
        on = jnp.where((wide_left != ZERO) & (wide_right != ZERO), live, 0.0)
        place = jnp.where(on > 0, dot(below, on).astype(i32), TERMS)
        word = wide_left + wide_right * 65536 - blank
        for s in range(TERMS):
            found = jnp.where(place == s, word, 0).sum(0, keepdims=True)
            ent_ref[pl.ds(t * TERMS + s, 1), pl.ds(0, flat_size)] = found + blank
        slot = flat(out_slot[t]).astype(i32)
        old = flat(left[t]).astype(i32) if t % 2 else jnp.full((1, flat_size), ZERO, i32)
        ox_ref[pl.ds(t, 1), pl.ds(0, flat_size)] = slot + old * 65536
        count = on.sum(0, keepdims=True)
        for index, ((limit, _), low) in enumerate(zip(CLASSES, low_limits)):
            inside = (live > 0) & (count > low) & (count <= limit)
            member_ref[pl.ds(t * count_classes + index, 1), :] = jnp.where(inside, 1.0, 0.0)

    member = member_ref[...]
    earlier = iota((flat_size, flat_size), 0) < iota((flat_size, flat_size), 1)
    rank = dot(member, jnp.where(earlier, 1.0, 0.0))
    total = member.sum(1, keepdims=True)
    o_row = iota((8, flat_size), 1)
    o_part = iota((8, flat_size), 0)
    number = jnp.where(o_part == 0, o_row >> 5, jnp.where(o_part == 1, o_row & 31, jnp.where(o_part == 2, 1, 0)))
    lane = iota((1, 128), 1)
    for t in range(STEPS):
        position = jnp.zeros((1, flat_size), f32)
        ahead = jnp.zeros((1, 1), f32)
        end = jnp.zeros((1, 1), i32)
        body = jnp.zeros((1, 128), i32)
        for index, (_, width) in enumerate(CLASSES):
            at = t * count_classes + index
            position = position + member[at : at + 1] * (rank[at : at + 1] + ahead)
            ahead = ahead + total[at : at + 1]
            left_over = jnp.maximum(ahead.astype(i32) - end + (width - 1), 0)
            bodies = (left_over * -(-65536 // width)) >> 16
            body = jnp.where(lane == 2 * index, end, jnp.where(lane == 2 * index + 1, bodies, body))
            end = end + bodies * width
        body_ref[pl.ds(t, 1), :] = body
        position = jnp.where(lives[t] > 0, position, float(POSITIONS)).astype(i32)
        match = jnp.where(iota((POSITIONS, flat_size), 0) == position, 1.0, 0.0).astype(bf16)
        found = lax.dot_general(
            number.astype(f32).astype(bf16), match, (((1,), (1,)), ((), ())), preferred_element_type=f32
        )
        entry = found[0:1] * float(NB) + found[1:2]
        ord_ref[pl.ds(t, 1), :] = jnp.where(found[2:3] > 0, entry, float(flat_size)).astype(i32)
    body_ref[pl.ds(STEPS, 1), :] = jnp.broadcast_to(fit, (1, 128))


def lists(patterns):
    return pl.pallas_call(
        lists_kernel,
        out_shape=[
            jax.ShapeDtypeStruct((STEPS * TERMS, ROWS), jnp.int32),
            jax.ShapeDtypeStruct((8, ROWS), jnp.int32),
            jax.ShapeDtypeStruct((8, POSITIONS), jnp.int32),
            jax.ShapeDtypeStruct((8, 128), jnp.int32),
        ],
        in_specs=[pl.BlockSpec(memory_space=pltpu.VMEM)],
        out_specs=[pl.BlockSpec(memory_space=pltpu.VMEM)] * 4,
        scratch_shapes=[pltpu.VMEM((STEPS * len(CLASSES) + 2, NB * NB), jnp.float32)],
        compiler_params=pltpu.CompilerParams(vmem_limit_bytes=24 * 2**20),
        name="build_lists",
    )(patterns)


def my_place():
    row, col, depth = (lax.axis_index(a) for a in AXES)
    return row, col * 4 + depth, (col % 2, col // 2, depth)


def picked(mask, value, slots):
    place = jnp.where(mask > 0, ranks(mask[None])[0], slots)
    hit = place[None, :] == lax.iota(jnp.int32, slots)[:, None]
    return jnp.where(hit, value[None, :], 0).sum(-1)


def picks(pattern):
    x, _, (core, z, y) = my_place()
    by_place = pattern.reshape(4, 8, 4, 2, 4)
    lines0 = lax.dynamic_index_in_dim(by_place[:, :, :, 0], z, 2, keepdims=False).transpose(2, 0, 1)
    lines1 = lax.dynamic_index_in_dim(by_place[:, :, :, 1], y, 3, keepdims=False).transpose(0, 2, 1)
    lines = jnp.where(core == 0, lines0, lines1).reshape(4, 32)
    at1, at2 = jnp.where(core == 0, x, z), jnp.where(core == 0, y, x)
    e = lax.iota(jnp.int32, 32)
    line = lax.dynamic_index_in_dim(lines, at2, 0, keepdims=False)
    of_line = picked(line, ((at1 - e // 8) & 3) * 8 + e % 8, LINE_CAP)
    back = (at2 - lax.iota(jnp.int32, 4)) & 3
    value = back[:, None] * LINE_CAP + jnp.minimum(ranks(lines), LINE_CAP - 1)
    of_group = picked(lines.reshape(4 * 32), value.reshape(4 * 32), GROUP_CAP)
    return of_line, of_group


def hops(axes, shift):
    pairs = []
    for x in range(4):
        for z in range(4):
            for c in range(2):
                for y in range(4):
                    to = {"x": x, "y": y, "z": z}
                    to[axes[c]] = (to[axes[c]] + shift) % 4
                    pairs.append((((x * 4 + z) * 2 + c) * 4 + y, ((to["x"] * 4 + to["z"]) * 2 + c) * 4 + to["y"]))
    return pairs


def send(mine, axes, shift):
    return lax.ppermute(mine, AXES, hops(axes, shift))


def gather(mine, axes):
    far = {shift: send(mine, axes, shift) for shift in (1, 3, 2)}
    return [mine, far[1], far[2], far[3]]


def gather_halves(a, b, axes):
    a1, b3 = send(a, axes, 1), send(b, axes, 3)
    b1, a3 = send(b, axes, 1), send(a, axes, 3)
    a2, b2 = send(a1, axes, 1), send(b3, axes, 3)
    return [a, b, a1, b1, a2, b2, a3, b3]


def sparse_path(ent, ox, entry, body, pieces):
    out = pl.pallas_call(
        product_kernel,
        out_shape=jax.ShapeDtypeStruct((8, BLOCK, BLOCK), jnp.bfloat16),
        in_specs=[pl.BlockSpec(memory_space=pl.ANY)] * 20,
        out_specs=pl.BlockSpec(memory_space=pl.ANY),
        scratch_shapes=[pltpu.VMEM((SLOTS, BLOCK, BLOCK), jnp.bfloat16), pltpu.SemaphoreType.DMA(())]
        + [pltpu.SMEM(table.shape, jnp.int32) for table in (ent, ox, entry, body)]
        + [pltpu.SemaphoreType.DMA((4,))],
        compiler_params=pltpu.CompilerParams(vmem_limit_bytes=56 * 2**20),
        name="block_products",
    )(ent, ox, entry, body, *pieces)
    return out.reshape(8 * BLOCK, BLOCK)


def tile_mask(pattern, row_first, col_first, tile_rows, tile_cols):
    blocks = pattern.shape[0]
    slab = lax.dynamic_slice_in_dim(pattern, row_first // BLOCK, tile_rows // BLOCK, 0).astype(jnp.float32)
    col_block = (col_first + lax.iota(jnp.int32, tile_cols)) // BLOCK
    onehot = (col_block[None, :] == lax.iota(jnp.int32, blocks)[:, None]).astype(jnp.float32)
    coarse = jnp.dot(slab, onehot)
    spread_rows = jnp.broadcast_to(coarse[:, None, :], (tile_rows // BLOCK, BLOCK, tile_cols))
    return spread_rows.reshape(tile_rows, tile_cols)


def dense_path(x_in, patterns):
    tile_rows, tile_width = x_in.shape
    row_first = lax.axis_index("row") * tile_rows
    col_first = (lax.axis_index("col") * lax.axis_size("depth") + lax.axis_index("depth")) * tile_width
    masks = [tile_mask(patterns[p], row_first, col_first, tile_rows, tile_width) for p in range(2 * ITERS + 1)]
    matrix = (x_in * masks[0]).astype(jnp.bfloat16)
    for iteration in range(ITERS):
        panel = lax.all_gather(matrix, ("col", "depth"), axis=1, tiled=True)

        def product(right):
            column = lax.all_gather(right, "row", axis=0, tiled=True)
            return jnp.dot(panel, column, preferred_element_type=jnp.float32)

        squared = (masks[2 * iteration + 1] * product(matrix)).astype(jnp.bfloat16)
        update = 1.5 * matrix.astype(jnp.float32) - 0.5 * product(squared)
        matrix = (masks[2 * iteration + 2] * update).astype(jnp.bfloat16)
    return matrix


def on_device(x_in, patterns):
    of_line, of_group = picks(patterns[0])
    (line,) = pack(of_line, gather(x_in.reshape(8, BLOCK, BLOCK), "xz"), 1)
    lines = gather(line, "yx")
    lines[1], late = lax.optimization_barrier((lines[1], patterns))
    tables, of_group = lax.optimization_barrier((lists(late), of_group))
    a, b = pack(of_group, lines, 2)
    pieces = gather_halves(a, b, "zy")
    pieces += [lax.ppermute(piece, "col", [(c, c ^ 1) for c in range(8)]) for piece in pieces]
    return lax.cond(
        tables[3][STEPS, 0] > 0,
        lambda: sparse_path(*tables, pieces),
        lambda: dense_path(x_in, patterns),
    )


def solution(mesh):
    placed = (P("row", ("col", "depth")), P())
    return jax.shard_map(
        on_device, mesh=mesh, in_specs=placed, out_specs=P("row", ("col", "depth")), check_vma=False
    )
```

```python
import functools

import jax
import jax.numpy as jnp
from jax import lax
from jax.experimental import pallas as pl
from jax.experimental.pallas import tpu as pltpu
from jax.sharding import PartitionSpec as P

BLOCK = 128
ITERS = 3
NB = 32
AXES = ("row", "col", "depth")

SIZES = ((14, 40), (16, 44), (20, 52))
LINE_CAP, GROUP_CAP = SIZES[-1]
CAP = 400
ZERO = 8 * GROUP_CAP
DUMMY = ZERO + 1
TILE = DUMMY + 1
S_BASE = TILE + 8
X_BASE = S_BASE + CAP
SLOTS = X_BASE + CAP
TERMS = 16
POSITIONS = 512
ROWS = 1152
CLASSES = ((16, 2), (8, 8), (6, 10), (5, 12), (4, 16), (3, 20), (2, 32), (1, 32), (0, 16))
STEPS = 2 * ITERS


def pack_kernel(stride, pick_ref, *refs):
    sources, outs, blocks, sem = refs[:4], refs[4:-2], refs[-2], refs[-1]
    length = sources[0].shape[0]
    for index, source in enumerate(sources):
        pltpu.make_async_copy(source, blocks.at[pl.ds(index * stride, length)], sem).start()
    whole = blocks.at[pl.ds(0, 4 * length)]
    pltpu.make_async_copy(whole, whole, sem).wait()
    first = 0
    for out_ref in outs:
        for p in range(out_ref.shape[0]):
            out_ref[p] = blocks[pick_ref[first + p]]
        first += out_ref.shape[0]


def pack(pick, sources, stride, lengths):
    return pl.pallas_call(
        functools.partial(pack_kernel, stride),
        out_shape=[jax.ShapeDtypeStruct((length, BLOCK, BLOCK), jnp.bfloat16) for length in lengths],
        in_specs=[pl.BlockSpec(memory_space=pltpu.SMEM)] + [pl.BlockSpec(memory_space=pl.ANY)] * 4,
        out_specs=[pl.BlockSpec(memory_space=pltpu.VMEM)] * len(lengths),
        scratch_shapes=[pltpu.VMEM((4 * stride, BLOCK, BLOCK), jnp.bfloat16), pltpu.SemaphoreType.DMA(())],
        compiler_params=pltpu.CompilerParams(vmem_limit_bytes=16 * 2**20),
        name="pack_blocks",
    )(pick, *sources)


def product_kernel(*refs):
    tables, pieces, out_ref, blocks, sem = refs[:4], refs[4:20], refs[20], refs[21], refs[22]
    ent_ref, ox_ref, ord_ref, body_ref = refs[23:27]
    table_sem = refs[27]
    copies = [
        pltpu.make_async_copy(table, kept, table_sem.at[index])
        for index, (table, kept) in enumerate(zip(tables, refs[23:27]))
    ]
    for copy in copies:
        copy.start()
    half = pieces[0].shape[0]
    for index, piece in enumerate(pieces):
        first = index // 2 * GROUP_CAP + index % 2 * half
        pltpu.make_async_copy(piece, blocks.at[pl.ds(first, half)], sem).start()
    blocks[ZERO] = jnp.zeros((BLOCK, BLOCK), blocks.dtype)
    for b in range(8):
        blocks[TILE + b] = jnp.zeros((BLOCK, BLOCK), blocks.dtype)
    whole = blocks.at[pl.ds(0, len(pieces) * half)]
    pltpu.make_async_copy(whole, whole, sem).wait()
    for copy in copies:
        copy.wait()

    def load(slot):
        return blocks[slot]

    def step(t, carry):
        is_update = (t & 1) == 1
        keep = jnp.where(is_update, 1.5, 0.0).astype(jnp.float32)
        scale = jnp.where(is_update, -0.5, 1.0).astype(jnp.float32)
        for index, (terms, width) in enumerate(CLASSES):
            first = body_ref[t, index * 2]
            count = body_ref[t, index * 2 + 1]

            def body(it, carry, terms=terms, width=width, first=first):
                results = []
                for u in range(width):
                    place = first + it * width + u
                    entry = ord_ref[t * 16 + (place >> 5), place & 31]
                    words = [ent_ref[t * TERMS + q, entry] for q in range(terms)]
                    lefts = [load(w & 0xFFFF) for w in words]
                    rights = [load(w >> 16) for w in words]
                    total = jnp.zeros((BLOCK, BLOCK), jnp.float32)
                    if terms == 1:
                        total = jnp.dot(lefts[0], rights[0], preferred_element_type=jnp.float32)
                    elif terms > 1:
                        left = jnp.concatenate(lefts, axis=1)
                        right = jnp.concatenate(rights, axis=0)
                        total = jnp.dot(left, right, preferred_element_type=jnp.float32)
                    ox = ox_ref[t, entry]
                    old = load(ox >> 16).astype(jnp.float32)
                    results.append((ox & 0xFFFF, (keep * old + scale * total).astype(jnp.bfloat16)))
                for slot, value in results:
                    blocks[slot] = value
                return carry

            lax.fori_loop(0, count, body, 0)
        return carry

    lax.fori_loop(0, STEPS, step, 0)
    copy = pltpu.make_async_copy(blocks.at[pl.ds(TILE, 8)], out_ref, sem)
    copy.start()
    copy.wait()


def ranks(mask):
    n = mask.shape[-1]
    before = (lax.iota(jnp.int32, n)[:, None] < lax.iota(jnp.int32, n)[None, :]).astype(jnp.bfloat16)
    flat = mask.reshape(-1, n).astype(jnp.bfloat16)
    return jnp.dot(flat, before, preferred_element_type=jnp.float32).astype(jnp.int32).reshape(mask.shape)


def lists_kernel(pattern_ref, ent_ref, ox_ref, ord_ref, body_ref, member_ref):
    f32, bf16, i32 = jnp.float32, jnp.bfloat16, jnp.int32
    row, col, my_y = (lax.axis_index(a) for a in AXES)
    my_column, my_core, my_z = col * 4 + my_y, col & 1, col >> 1
    flat_size = NB * NB

    def iota(shape, axis):
        return lax.broadcasted_iota(i32, shape, axis)

    def dot(a, b):
        return jnp.dot(a.astype(bf16), b.astype(bf16), preferred_element_type=f32)

    def exact(a, b, contract):
        return lax.dot_general(a, b, (contract, ((), ())), precision=lax.Precision.HIGHEST, preferred_element_type=f32)

    i, j = iota((NB, NB), 0), iota((NB, NB), 1)
    below, above = (j < i).astype(f32), (i < j).astype(f32)
    o = iota((NB, flat_size), 1)
    of_row = ((o >> 5) == iota((NB, flat_size), 0)).astype(f32)
    of_col = ((o & 31) == iota((NB, flat_size), 0)).astype(f32)

    def flat(v):
        return (of_row * exact(v, of_col, ((1,), (0,)))).sum(0, keepdims=True)

    pattern = [pattern_ref[t].astype(f32) for t in range(2 * ITERS + 1)]
    start = pattern[0]

    y, c, z = j & 3, (j >> 2) & 1, j >> 3
    y1, c1, z1 = i & 3, (i >> 2) & 1, i >> 3
    line = jnp.where(c == 0, z, y)
    along = jnp.where(c == 0, y, z)
    line1 = jnp.where(c1 == 0, z1, y1)
    along1 = jnp.where(c1 == 0, y1, z1)
    same = ((c1 == c) & (line1 == line)).astype(f32)
    sooner = same * (along1 < along).astype(f32)
    band = ((i >> 3) == (j >> 3)).astype(f32)
    band_below = ((j >> 3) < (i >> 3)).astype(f32)
    in_line = dot(start, same)
    sooner_in_line = dot(start, sooner)
    rank0 = sooner_in_line.sum(0, keepdims=True) + dot(below, start)
    rank1 = dot(band_below, in_line) + dot(band, sooner_in_line) + dot(below * band, start)
    back = (jnp.where(c == 0, my_z, my_y) - line) & 3
    piece = jnp.where(c == my_core, 0, 4) + back
    slot0 = piece.astype(f32) * GROUP_CAP + jnp.where(c == 0, rank0, rank1)
    slot0 = jnp.where(start > 0, slot0, float(ZERO))
    in_tiles = jnp.where(c == 0, start.sum(0, keepdims=True), dot(band, in_line))
    in_group = in_line.sum(0, keepdims=True)
    most_in_line = in_tiles.max(0, keepdims=True).max(1, keepdims=True)
    most_in_group = in_group.max(1, keepdims=True)
    fit = jnp.ones((1, 1), i32)

    mine = jnp.where(j == my_column, 1.0, 0.0)
    tile = mine * jnp.where((i >> 3) == row, 1.0, 0.0)
    outs = pattern[1:5] + [pattern[5] * mine, pattern[6] * tile]
    out_slot = []
    read_slot = []
    for t, base in enumerate((S_BASE, X_BASE, S_BASE, 0, S_BASE)):
        rank = dot(below, outs[t]).sum(1, keepdims=True) + dot(outs[t], above)
        out_slot.append(rank + float(base))
        read_slot.append(jnp.where(outs[t] > 0, out_slot[t], float(ZERO)))
        if t < 4:
            total = outs[t].sum(1, keepdims=True).sum(0, keepdims=True)
            fit = fit * jnp.where(total <= CAP, 1, 0)
    out_slot.append((TILE + i - 8 * row).astype(f32))
    left = [slot0, slot0, read_slot[1], read_slot[1], read_slot[3], read_slot[3]]
    right = [slot0, read_slot[0], read_slot[1], read_slot[2], read_slot[3], read_slot[4]]

    blank = ZERO + ZERO * 65536
    low_limits = [limit for limit, _ in CLASSES[1:]] + [-1]
    count_classes = len(CLASSES)
    ent_ref[:, pl.ds(flat_size, ROWS - flat_size)] = jnp.full((STEPS * TERMS, ROWS - flat_size), blank, i32)
    ox_ref[:, pl.ds(flat_size, ROWS - flat_size)] = jnp.full((8, ROWS - flat_size), DUMMY + ZERO * 65536, i32)
    member_ref[...] = jnp.zeros(member_ref.shape, f32)
    lives = []
    for t in range(STEPS):
        terms = dot(pattern[t - t % 2], pattern[t]) * pattern[t + 1]
        most = terms.max(1, keepdims=True).max(0, keepdims=True)
        fit = fit * jnp.where(most <= TERMS, 1, 0)

        wide_left = exact(left[t], of_row, ((0,), (0,))).astype(i32)
        wide_right = exact(right[t], of_col, ((1,), (0,))).astype(i32)
        live = flat(outs[t])
        lives.append(live)
        on = jnp.where((wide_left != ZERO) & (wide_right != ZERO), live, 0.0)
        place = jnp.where(on > 0, dot(below, on).astype(i32), TERMS)
        word = wide_left + wide_right * 65536 - blank
        for s in range(TERMS):
            found = jnp.where(place == s, word, 0).sum(0, keepdims=True)
            ent_ref[pl.ds(t * TERMS + s, 1), pl.ds(0, flat_size)] = found + blank
        slot = flat(out_slot[t]).astype(i32)
        old = flat(left[t]).astype(i32) if t % 2 else jnp.full((1, flat_size), ZERO, i32)
        ox_ref[pl.ds(t, 1), pl.ds(0, flat_size)] = slot + old * 65536
        count = on.sum(0, keepdims=True)
        for index, ((limit, _), low) in enumerate(zip(CLASSES, low_limits)):
            inside = (live > 0) & (count > low) & (count <= limit)
            member_ref[pl.ds(t * count_classes + index, 1), :] = jnp.where(inside, 1.0, 0.0)

    member = member_ref[...]
    earlier = (iota((BLOCK, BLOCK), 0) < iota((BLOCK, BLOCK), 1)).astype(f32)
    rank = []
    total = jnp.zeros((member.shape[0], 1), f32)
    for chunk in range(flat_size // BLOCK):
        part = member[:, chunk * BLOCK : (chunk + 1) * BLOCK]
        rank.append(dot(part, earlier) + total)
        total = total + part.sum(1, keepdims=True)
    rank = jnp.concatenate(rank, axis=1)
    o_wide = iota((16, flat_size), 1)
    number = jnp.concatenate([o_wide >> 5, o_wide & 31, jnp.ones((16, flat_size), i32)], axis=0).astype(f32)
    high = jnp.concatenate([iota((16, flat_size), 0)] * 3, axis=0)
    low = iota((32, flat_size), 0)
    lane = iota((1, 128), 1)
    for t in range(STEPS):
        position = jnp.zeros((1, flat_size), f32)
        ahead = jnp.zeros((1, 1), f32)
        end = jnp.zeros((1, 1), i32)
        body = jnp.zeros((1, 128), i32)
        for index, (_, width) in enumerate(CLASSES):
            at = t * count_classes + index
            position = position + member[at : at + 1] * (rank[at : at + 1] + ahead)
            ahead = ahead + total[at : at + 1]
            left_over = jnp.maximum(ahead.astype(i32) - end + (width - 1), 0)
            bodies = (left_over * -(-65536 // width)) >> 16
            body = jnp.where(lane == 2 * index, end, jnp.where(lane == 2 * index + 1, bodies, body))
            end = end + bodies * width
        body_ref[pl.ds(t, 1), :] = body
        position = jnp.where(lives[t] > 0, position, float(POSITIONS)).astype(i32)
        by_high = jnp.where(high == (position >> 5), number, 0.0)
        by_low = jnp.where(low == (position & 31), 1.0, 0.0)
        found = lax.dot_general(
            by_high.astype(bf16), by_low.astype(bf16), (((1,), (1,)), ((), ())), preferred_element_type=f32
        )
        entry = jnp.where(found[32:48] > 0, found[0:16] * float(NB) + found[16:32], float(flat_size))
        ord_ref[pl.ds(t * 16, 16), pl.ds(0, 32)] = entry.astype(i32)
    choice = jnp.zeros((1, 1), i32)
    for line_cap, group_cap in SIZES:
        inside = (most_in_line <= line_cap) & (most_in_group <= group_cap)
        choice = choice + 1 - fit * jnp.where(inside, 1, 0)
    body_ref[pl.ds(STEPS, 1), :] = jnp.broadcast_to(choice, (1, 128))


def lists(patterns):
    return pl.pallas_call(
        lists_kernel,
        out_shape=[
            jax.ShapeDtypeStruct((STEPS * TERMS, ROWS), jnp.int32),
            jax.ShapeDtypeStruct((8, ROWS), jnp.int32),
            jax.ShapeDtypeStruct((STEPS * 16, 128), jnp.int32),
            jax.ShapeDtypeStruct((8, 128), jnp.int32),
        ],
        in_specs=[pl.BlockSpec(memory_space=pltpu.VMEM)],
        out_specs=[pl.BlockSpec(memory_space=pltpu.VMEM)] * 4,
        scratch_shapes=[pltpu.VMEM((STEPS * len(CLASSES) + 2, NB * NB), jnp.float32)],
        compiler_params=pltpu.CompilerParams(vmem_limit_bytes=24 * 2**20),
        name="build_lists",
    )(patterns)


def my_place():
    row, col, depth = (lax.axis_index(a) for a in AXES)
    return row, col * 4 + depth, (col % 2, col // 2, depth)


def picked(mask, value, slots):
    place = jnp.where(mask > 0, ranks(mask[None])[0], slots)
    hit = place[None, :] == lax.iota(jnp.int32, slots)[:, None]
    return jnp.where(hit, value[None, :], 0).sum(-1)


def picks(pattern):
    x, _, (core, z, y) = my_place()
    by_place = pattern.reshape(4, 8, 4, 2, 4)
    lines0 = lax.dynamic_index_in_dim(by_place[:, :, :, 0], z, 2, keepdims=False).transpose(2, 0, 1)
    lines1 = lax.dynamic_index_in_dim(by_place[:, :, :, 1], y, 3, keepdims=False).transpose(0, 2, 1)
    lines = jnp.where(core == 0, lines0, lines1).reshape(4, 32)
    at1, at2 = jnp.where(core == 0, x, z), jnp.where(core == 0, y, x)
    e = lax.iota(jnp.int32, 32)
    line = lax.dynamic_index_in_dim(lines, at2, 0, keepdims=False)
    of_line = picked(line, ((at1 - e // 8) & 3) * 8 + e % 8, LINE_CAP)
    back = (at2 - lax.iota(jnp.int32, 4)) & 3
    value = back[:, None] * LINE_CAP + jnp.minimum(ranks(lines), LINE_CAP - 1)
    of_group = picked(lines.reshape(4 * 32), value.reshape(4 * 32), GROUP_CAP)
    return of_line, of_group


def hops(axes, shift):
    pairs = []
    for x in range(4):
        for z in range(4):
            for c in range(2):
                for y in range(4):
                    to = {"x": x, "y": y, "z": z}
                    to[axes[c]] = (to[axes[c]] + shift) % 4
                    pairs.append((((x * 4 + z) * 2 + c) * 4 + y, ((to["x"] * 4 + to["z"]) * 2 + c) * 4 + to["y"]))
    return pairs


def send(mine, axes, shift):
    return lax.ppermute(mine, AXES, hops(axes, shift))


def gather(mine, axes):
    far = {shift: send(mine, axes, shift) for shift in (1, 3, 2)}
    return [mine, far[1], far[2], far[3]]


def gather_halves(a, b, axes):
    a1, b3 = send(a, axes, 1), send(b, axes, 3)
    b1, a3 = send(b, axes, 1), send(a, axes, 3)
    a2, b2 = send(a1, axes, 1), send(b3, axes, 3)
    return [a, b, a1, b1, a2, b2, a3, b3]


def sparse_path(ent, ox, entry, body, pieces):
    out = pl.pallas_call(
        product_kernel,
        out_shape=jax.ShapeDtypeStruct((8, BLOCK, BLOCK), jnp.bfloat16),
        in_specs=[pl.BlockSpec(memory_space=pl.ANY)] * 20,
        out_specs=pl.BlockSpec(memory_space=pl.ANY),
        scratch_shapes=[pltpu.VMEM((SLOTS, BLOCK, BLOCK), jnp.bfloat16), pltpu.SemaphoreType.DMA(())]
        + [pltpu.SMEM(table.shape, jnp.int32) for table in (ent, ox, entry, body)]
        + [pltpu.SemaphoreType.DMA((4,))],
        compiler_params=pltpu.CompilerParams(vmem_limit_bytes=56 * 2**20),
        name="block_products",
    )(ent, ox, entry, body, *pieces)
    return out.reshape(8 * BLOCK, BLOCK)


def tile_mask(pattern, row_first, col_first, tile_rows, tile_cols):
    blocks = pattern.shape[0]
    slab = lax.dynamic_slice_in_dim(pattern, row_first // BLOCK, tile_rows // BLOCK, 0).astype(jnp.float32)
    col_block = (col_first + lax.iota(jnp.int32, tile_cols)) // BLOCK
    onehot = (col_block[None, :] == lax.iota(jnp.int32, blocks)[:, None]).astype(jnp.float32)
    coarse = jnp.dot(slab, onehot)
    spread_rows = jnp.broadcast_to(coarse[:, None, :], (tile_rows // BLOCK, BLOCK, tile_cols))
    return spread_rows.reshape(tile_rows, tile_cols)


def dense_path(x_in, patterns):
    tile_rows, tile_width = x_in.shape
    row_first = lax.axis_index("row") * tile_rows
    col_first = (lax.axis_index("col") * lax.axis_size("depth") + lax.axis_index("depth")) * tile_width
    masks = [tile_mask(patterns[p], row_first, col_first, tile_rows, tile_width) for p in range(2 * ITERS + 1)]
    matrix = (x_in * masks[0]).astype(jnp.bfloat16)
    for iteration in range(ITERS):
        panel = lax.all_gather(matrix, ("col", "depth"), axis=1, tiled=True)

        def product(right):
            column = lax.all_gather(right, "row", axis=0, tiled=True)
            return jnp.dot(panel, column, preferred_element_type=jnp.float32)

        squared = (masks[2 * iteration + 1] * product(matrix)).astype(jnp.bfloat16)
        update = 1.5 * matrix.astype(jnp.float32) - 0.5 * product(squared)
        matrix = (masks[2 * iteration + 2] * update).astype(jnp.bfloat16)
    return matrix


def on_device(x_in, patterns):
    of_line, of_group = picks(patterns[0])
    tiles = gather(x_in.reshape(8, BLOCK, BLOCK), "xz")
    tables = lists(patterns)

    def path(line_cap, group_cap):
        (line,) = pack(of_line, tiles, 8, (line_cap,))
        a, b = pack(of_group, gather(line, "yx"), LINE_CAP, (group_cap // 2, group_cap // 2))
        pieces = gather_halves(a, b, "zy")
        pieces += [lax.ppermute(piece, "col", [(c, c ^ 1) for c in range(8)]) for piece in pieces]
        return sparse_path(*tables, pieces)

    paths = [functools.partial(path, *sizes) for sizes in SIZES]
    return lax.switch(tables[3][STEPS, 0], paths + [lambda: dense_path(x_in, patterns)])


def solution(mesh):
    placed = (P("row", ("col", "depth")), P())
    return jax.shard_map(
        on_device, mesh=mesh, in_specs=placed, out_specs=P("row", ("col", "depth")), check_vma=False
    )
```

```python
import functools

import jax
import jax.numpy as jnp
from jax import lax
from jax.experimental import pallas as pl
from jax.experimental.pallas import tpu as pltpu
from jax.sharding import PartitionSpec as P

BLOCK = 128
ITERS = 3
NB = 32
AXES = ("row", "col", "depth")

SIZES = ((15, 42), (20, 52))
LINE_CAP, GROUP_CAP = SIZES[-1]
CAP = 400
ZERO = 8 * GROUP_CAP
DUMMY = ZERO + 1
TILE = DUMMY + 1
S_BASE = TILE + 8
X_BASE = S_BASE + CAP
SLOTS = X_BASE + CAP
TERMS = 16
POSITIONS = 512
ROWS = 1152
CLASSES = ((16, 2), (8, 8), (6, 10), (5, 12), (4, 16), (3, 20), (2, 32), (1, 32), (0, 16))
STEPS = 2 * ITERS


def pack_kernel(stride, pick_ref, *refs):
    sources, outs, blocks, sem = refs[:4], refs[4:-2], refs[-2], refs[-1]
    length = sources[0].shape[0]
    for index, source in enumerate(sources):
        pltpu.make_async_copy(source, blocks.at[pl.ds(index * stride, length)], sem).start()
    whole = blocks.at[pl.ds(0, 4 * length)]
    pltpu.make_async_copy(whole, whole, sem).wait()
    first = 0
    for out_ref in outs:
        for p in range(out_ref.shape[0]):
            out_ref[p] = blocks[pick_ref[first + p]]
        first += out_ref.shape[0]


def pack(pick, sources, stride, lengths):
    return pl.pallas_call(
        functools.partial(pack_kernel, stride),
        out_shape=[jax.ShapeDtypeStruct((length, BLOCK, BLOCK), jnp.bfloat16) for length in lengths],
        in_specs=[pl.BlockSpec(memory_space=pltpu.SMEM)] + [pl.BlockSpec(memory_space=pl.ANY)] * 4,
        out_specs=[pl.BlockSpec(memory_space=pltpu.VMEM)] * len(lengths),
        scratch_shapes=[pltpu.VMEM((4 * stride, BLOCK, BLOCK), jnp.bfloat16), pltpu.SemaphoreType.DMA(())],
        compiler_params=pltpu.CompilerParams(vmem_limit_bytes=16 * 2**20),
        name="pack_blocks",
    )(pick, *sources)


def product_kernel(*refs):
    tables, pieces, out_ref, blocks, sem = refs[:4], refs[4:20], refs[20], refs[21], refs[22]
    ent_ref, ox_ref, ord_ref, body_ref = refs[23:27]
    table_sem = refs[27]
    copies = [
        pltpu.make_async_copy(table, kept, table_sem.at[STEPS + index])
        for index, (table, kept) in enumerate(zip(tables[1:], refs[24:27]))
    ]

    def ent_copy(t):
        rows = pl.ds(t * TERMS, TERMS)
        return pltpu.make_async_copy(tables[0].at[rows], ent_ref.at[rows], table_sem.at[t])

    for copy in copies + [ent_copy(t) for t in range(STEPS)]:
        copy.start()
    half = pieces[0].shape[0]
    for index, piece in enumerate(pieces):
        first = index // 2 * GROUP_CAP + index % 2 * half
        pltpu.make_async_copy(piece, blocks.at[pl.ds(first, half)], sem).start()
    blocks[ZERO] = jnp.zeros((BLOCK, BLOCK), blocks.dtype)
    for b in range(8):
        blocks[TILE + b] = jnp.zeros((BLOCK, BLOCK), blocks.dtype)
    whole = blocks.at[pl.ds(0, len(pieces) * half)]
    pltpu.make_async_copy(whole, whole, sem).wait()
    for copy in copies:
        copy.wait()

    def load(slot):
        return blocks[slot]

    def step(t, carry):
        ent_copy(t).wait()
        is_update = (t & 1) == 1
        keep = jnp.where(is_update, 1.5, 0.0).astype(jnp.float32)
        scale = jnp.where(is_update, -0.5, 1.0).astype(jnp.float32)
        for index, (terms, width) in enumerate(CLASSES):
            first = body_ref[t, index * 2]
            count = body_ref[t, index * 2 + 1]

            def body(it, carry, terms=terms, width=width, first=first):
                results = []
                for u in range(width):
                    place = first + it * width + u
                    entry = ord_ref[t * 16 + (place >> 5), place & 31]
                    words = [ent_ref[t * TERMS + q, entry] for q in range(terms)]
                    lefts = [load(w & 0xFFFF) for w in words]
                    rights = [load(w >> 16) for w in words]
                    total = jnp.zeros((BLOCK, BLOCK), jnp.float32)
                    if terms == 1:
                        total = jnp.dot(lefts[0], rights[0], preferred_element_type=jnp.float32)
                    elif terms > 1:
                        left = jnp.concatenate(lefts, axis=1)
                        right = jnp.concatenate(rights, axis=0)
                        total = jnp.dot(left, right, preferred_element_type=jnp.float32)
                    ox = ox_ref[t, entry]
                    old = load(ox >> 16).astype(jnp.float32)
                    results.append((ox & 0xFFFF, (keep * old + scale * total).astype(jnp.bfloat16)))
                for slot, value in results:
                    blocks[slot] = value
                return carry

            lax.fori_loop(0, count, body, 0)
        return carry

    lax.fori_loop(0, STEPS, step, 0)
    copy = pltpu.make_async_copy(blocks.at[pl.ds(TILE, 8)], out_ref, sem)
    copy.start()
    copy.wait()


def ranks(mask):
    n = mask.shape[-1]
    before = (lax.iota(jnp.int32, n)[:, None] < lax.iota(jnp.int32, n)[None, :]).astype(jnp.bfloat16)
    flat = mask.reshape(-1, n).astype(jnp.bfloat16)
    return jnp.dot(flat, before, preferred_element_type=jnp.float32).astype(jnp.int32).reshape(mask.shape)


def lists_kernel(pattern_ref, ent_ref, ox_ref, ord_ref, body_ref, member_ref):
    f32, bf16, i32 = jnp.float32, jnp.bfloat16, jnp.int32
    row, col, my_y = (lax.axis_index(a) for a in AXES)
    my_column, my_core, my_z = col * 4 + my_y, col & 1, col >> 1
    flat_size = NB * NB

    def iota(shape, axis):
        return lax.broadcasted_iota(i32, shape, axis)

    def dot(a, b):
        return jnp.dot(a.astype(bf16), b.astype(bf16), preferred_element_type=f32)

    def split(v, axis):
        whole = v.astype(i32)
        return jnp.concatenate([(whole >> 4).astype(f32), (whole & 15).astype(f32)], axis=axis).astype(bf16)

    def join(v):
        return v[:NB] * 16.0 + v[NB:]

    i, j = iota((NB, NB), 0), iota((NB, NB), 1)
    below, above = (j < i).astype(f32), (i < j).astype(f32)
    o = iota((NB, flat_size), 1)
    of_row = ((o >> 5) == iota((NB, flat_size), 0)).astype(f32)
    of_col = ((o & 31) == iota((NB, flat_size), 0)).astype(f32)

    of_row16, of_col16 = of_row.astype(bf16), of_col.astype(bf16)

    def by_row(v):
        parts = lax.dot_general(split(v, 1), of_row16, (((0,), (0,)), ((), ())), preferred_element_type=f32)
        return join(parts)

    def by_col(v):
        return join(jnp.dot(split(v, 0), of_col16, preferred_element_type=f32))

    def flat(v):
        return (of_row * by_col(v)).sum(0, keepdims=True)

    def flat_mask(v):
        return (of_row * dot(v, of_col16)).sum(0, keepdims=True)

    pattern = [pattern_ref[t].astype(f32) for t in range(2 * ITERS + 1)]
    start = pattern[0]

    y, c, z = j & 3, (j >> 2) & 1, j >> 3
    y1, c1, z1 = i & 3, (i >> 2) & 1, i >> 3
    line = jnp.where(c == 0, z, y)
    along = jnp.where(c == 0, y, z)
    line1 = jnp.where(c1 == 0, z1, y1)
    along1 = jnp.where(c1 == 0, y1, z1)
    same = ((c1 == c) & (line1 == line)).astype(f32)
    sooner = same * (along1 < along).astype(f32)
    band = ((i >> 3) == (j >> 3)).astype(f32)
    band_below = ((j >> 3) < (i >> 3)).astype(f32)
    in_line = dot(start, same)
    sooner_in_line = dot(start, sooner)
    rank0 = sooner_in_line.sum(0, keepdims=True) + dot(below, start)
    rank1 = dot(band_below, in_line) + dot(band, sooner_in_line) + dot(below * band, start)
    back = (jnp.where(c == 0, my_z, my_y) - line) & 3
    piece = jnp.where(c == my_core, 0, 4) + back
    slot0 = piece.astype(f32) * GROUP_CAP + jnp.where(c == 0, rank0, rank1)
    slot0 = jnp.where(start > 0, slot0, float(ZERO))
    in_tiles = jnp.where(c == 0, start.sum(0, keepdims=True), dot(band, in_line))
    in_group = in_line.sum(0, keepdims=True)
    most_in_line = in_tiles.max(0, keepdims=True).max(1, keepdims=True)
    most_in_group = in_group.max(1, keepdims=True)
    fit = jnp.ones((1, 1), i32)

    mine = jnp.where(j == my_column, 1.0, 0.0)
    tile = mine * jnp.where((i >> 3) == row, 1.0, 0.0)
    outs = pattern[1:5] + [pattern[5] * mine, pattern[6] * tile]
    out_slot = []
    read_slot = []
    for t, base in enumerate((S_BASE, X_BASE, S_BASE, 0, S_BASE)):
        rank = dot(below, outs[t]).sum(1, keepdims=True) + dot(outs[t], above)
        out_slot.append(rank + float(base))
        read_slot.append(jnp.where(outs[t] > 0, out_slot[t], float(ZERO)))
        if t < 4:
            total = outs[t].sum(1, keepdims=True).sum(0, keepdims=True)
            fit = fit * jnp.where(total <= CAP, 1, 0)
    out_slot.append((TILE + (i & 7)).astype(f32))
    left = [slot0, slot0, read_slot[1], read_slot[1], read_slot[3], read_slot[3]]
    right = [slot0, read_slot[0], read_slot[1], read_slot[2], read_slot[3], read_slot[4]]

    blank = ZERO + ZERO * 65536
    low_limits = [limit for limit, _ in CLASSES[1:]] + [-1]
    count_classes = len(CLASSES)
    ent_ref[:, pl.ds(flat_size, ROWS - flat_size)] = jnp.full((STEPS * TERMS, ROWS - flat_size), blank, i32)
    ox_ref[:, pl.ds(flat_size, ROWS - flat_size)] = jnp.full((8, ROWS - flat_size), DUMMY + ZERO * 65536, i32)
    member_ref[...] = jnp.zeros(member_ref.shape, f32)
    lives = []
    for t in range(STEPS):
        terms = dot(pattern[t - t % 2], pattern[t]) * pattern[t + 1]
        most = terms.max(1, keepdims=True).max(0, keepdims=True)
        fit = fit * jnp.where(most <= TERMS, 1, 0)

        wide_left = by_row(left[t]).astype(i32)
        wide_right = by_col(right[t]).astype(i32)
        live = flat_mask(outs[t])
        lives.append(live)
        on = jnp.where((wide_left != ZERO) & (wide_right != ZERO), live, 0.0)
        place = jnp.where(on > 0, dot(below, on).astype(i32), TERMS)
        word = wide_left + wide_right * 65536 - blank
        for s in range(TERMS):
            found = jnp.where(place == s, word, 0).sum(0, keepdims=True)
            ent_ref[pl.ds(t * TERMS + s, 1), pl.ds(0, flat_size)] = found + blank
        slot = flat(out_slot[t]).astype(i32)
        old = flat(left[t]).astype(i32) if t % 2 else jnp.full((1, flat_size), ZERO, i32)
        ox_ref[pl.ds(t, 1), pl.ds(0, flat_size)] = slot + old * 65536
        count = on.sum(0, keepdims=True)
        for index, ((limit, _), low) in enumerate(zip(CLASSES, low_limits)):
            inside = (live > 0) & (count > low) & (count <= limit)
            member_ref[pl.ds(t * count_classes + index, 1), :] = jnp.where(inside, 1.0, 0.0)

    member = member_ref[...]
    earlier = (iota((BLOCK, BLOCK), 0) < iota((BLOCK, BLOCK), 1)).astype(f32)
    rank = []
    total = jnp.zeros((member.shape[0], 1), f32)
    for chunk in range(flat_size // BLOCK):
        part = member[:, chunk * BLOCK : (chunk + 1) * BLOCK]
        rank.append(dot(part, earlier) + total)
        total = total + part.sum(1, keepdims=True)
    rank = jnp.concatenate(rank, axis=1)
    o_wide = iota((16, flat_size), 1)
    number = jnp.concatenate([o_wide >> 5, o_wide & 31, jnp.ones((16, flat_size), i32)], axis=0).astype(f32)
    high = jnp.concatenate([iota((16, flat_size), 0)] * 3, axis=0)
    low = iota((32, flat_size), 0)
    lane = iota((1, 128), 1)
    for t in range(STEPS):
        position = jnp.zeros((1, flat_size), f32)
        ahead = jnp.zeros((1, 1), f32)
        end = jnp.zeros((1, 1), i32)
        body = jnp.zeros((1, 128), i32)
        for index, (_, width) in enumerate(CLASSES):
            at = t * count_classes + index
            position = position + member[at : at + 1] * (rank[at : at + 1] + ahead)
            ahead = ahead + total[at : at + 1]
            left_over = jnp.maximum(ahead.astype(i32) - end + (width - 1), 0)
            bodies = (left_over * -(-65536 // width)) >> 16
            body = jnp.where(lane == 2 * index, end, jnp.where(lane == 2 * index + 1, bodies, body))
            end = end + bodies * width
        body_ref[pl.ds(t, 1), :] = body
        position = jnp.where(lives[t] > 0, position, float(POSITIONS)).astype(i32)
        by_high = jnp.where(high == (position >> 5), number, 0.0)
        by_low = jnp.where(low == (position & 31), 1.0, 0.0)
        found = lax.dot_general(
            by_high.astype(bf16), by_low.astype(bf16), (((1,), (1,)), ((), ())), preferred_element_type=f32
        )
        entry = jnp.where(found[32:48] > 0, found[0:16] * float(NB) + found[16:32], float(flat_size))
        ord_ref[pl.ds(t * 16, 16), pl.ds(0, 32)] = entry.astype(i32)
    choice = jnp.zeros((1, 1), i32)
    for line_cap, group_cap in SIZES:
        inside = (most_in_line <= line_cap) & (most_in_group <= group_cap)
        choice = choice + 1 - fit * jnp.where(inside, 1, 0)
    body_ref[pl.ds(STEPS, 1), :] = jnp.broadcast_to(choice, (1, 128))


def lists(patterns):
    return pl.pallas_call(
        lists_kernel,
        out_shape=[
            jax.ShapeDtypeStruct((STEPS * TERMS, ROWS), jnp.int32),
            jax.ShapeDtypeStruct((8, ROWS), jnp.int32),
            jax.ShapeDtypeStruct((STEPS * 16, 128), jnp.int32),
            jax.ShapeDtypeStruct((8, 128), jnp.int32),
        ],
        in_specs=[pl.BlockSpec(memory_space=pltpu.VMEM)],
        out_specs=[pl.BlockSpec(memory_space=pltpu.VMEM)] * 4,
        scratch_shapes=[pltpu.VMEM((STEPS * len(CLASSES) + 2, NB * NB), jnp.float32)],
        compiler_params=pltpu.CompilerParams(vmem_limit_bytes=24 * 2**20),
        name="build_lists",
    )(patterns)


def my_place():
    row, col, depth = (lax.axis_index(a) for a in AXES)
    return row, col * 4 + depth, (col % 2, col // 2, depth)


def picked(mask, value, slots):
    place = jnp.where(mask > 0, ranks(mask[None])[0], slots)
    hit = place[None, :] == lax.iota(jnp.int32, slots)[:, None]
    return jnp.where(hit, value[None, :], 0).sum(-1)


def picks(pattern):
    x, _, (core, z, y) = my_place()
    by_place = pattern.reshape(4, 8, 4, 2, 4)
    lines0 = lax.dynamic_index_in_dim(by_place[:, :, :, 0], z, 2, keepdims=False).transpose(2, 0, 1)
    lines1 = lax.dynamic_index_in_dim(by_place[:, :, :, 1], y, 3, keepdims=False).transpose(0, 2, 1)
    lines = jnp.where(core == 0, lines0, lines1).reshape(4, 32)
    at1, at2 = jnp.where(core == 0, x, z), jnp.where(core == 0, y, x)
    e = lax.iota(jnp.int32, 32)
    line = lax.dynamic_index_in_dim(lines, at2, 0, keepdims=False)
    of_line = picked(line, ((at1 - e // 8) & 3) * 8 + e % 8, LINE_CAP)
    back = (at2 - lax.iota(jnp.int32, 4)) & 3
    value = back[:, None] * LINE_CAP + jnp.minimum(ranks(lines), LINE_CAP - 1)
    of_group = picked(lines.reshape(4 * 32), value.reshape(4 * 32), GROUP_CAP)
    return of_line, of_group


def hops(axes, shift):
    pairs = []
    for x in range(4):
        for z in range(4):
            for c in range(2):
                for y in range(4):
                    to = {"x": x, "y": y, "z": z}
                    to[axes[c]] = (to[axes[c]] + shift) % 4
                    pairs.append((((x * 4 + z) * 2 + c) * 4 + y, ((to["x"] * 4 + to["z"]) * 2 + c) * 4 + to["y"]))
    return pairs


def send(mine, axes, shift):
    return lax.ppermute(mine, AXES, hops(axes, shift))


def gather(mine, axes):
    far = {shift: send(mine, axes, shift) for shift in (1, 3, 2)}
    return [mine, far[1], far[2], far[3]]


def gather_halves(a, b, axes):
    a1, b3 = send(a, axes, 1), send(b, axes, 3)
    b1, a3 = send(b, axes, 1), send(a, axes, 3)
    a2, b2 = send(a1, axes, 1), send(b3, axes, 3)
    return [a, b, a1, b1, a2, b2, a3, b3]


def sparse_path(ent, ox, entry, body, pieces):
    out = pl.pallas_call(
        product_kernel,
        out_shape=jax.ShapeDtypeStruct((8, BLOCK, BLOCK), jnp.bfloat16),
        in_specs=[pl.BlockSpec(memory_space=pl.ANY)] * 20,
        out_specs=pl.BlockSpec(memory_space=pl.ANY),
        scratch_shapes=[pltpu.VMEM((SLOTS, BLOCK, BLOCK), jnp.bfloat16), pltpu.SemaphoreType.DMA(())]
        + [pltpu.SMEM(table.shape, jnp.int32) for table in (ent, ox, entry, body)]
        + [pltpu.SemaphoreType.DMA((STEPS + 3,))],
        compiler_params=pltpu.CompilerParams(vmem_limit_bytes=56 * 2**20),
        name="block_products",
    )(ent, ox, entry, body, *pieces)
    return out.reshape(8 * BLOCK, BLOCK)


def tile_mask(pattern, row_first, col_first, tile_rows, tile_cols):
    blocks = pattern.shape[0]
    slab = lax.dynamic_slice_in_dim(pattern, row_first // BLOCK, tile_rows // BLOCK, 0).astype(jnp.float32)
    col_block = (col_first + lax.iota(jnp.int32, tile_cols)) // BLOCK
    onehot = (col_block[None, :] == lax.iota(jnp.int32, blocks)[:, None]).astype(jnp.float32)
    coarse = jnp.dot(slab, onehot)
    spread_rows = jnp.broadcast_to(coarse[:, None, :], (tile_rows // BLOCK, BLOCK, tile_cols))
    return spread_rows.reshape(tile_rows, tile_cols)


def dense_path(x_in, patterns):
    tile_rows, tile_width = x_in.shape
    row_first = lax.axis_index("row") * tile_rows
    col_first = (lax.axis_index("col") * lax.axis_size("depth") + lax.axis_index("depth")) * tile_width

    def mask(index):
        pattern = lax.dynamic_index_in_dim(patterns, index, 0, keepdims=False)
        return tile_mask(pattern, row_first, col_first, tile_rows, tile_width)

    def product(panel, right):
        column = lax.all_gather(right, "row", axis=0, tiled=True)
        return jnp.dot(panel, column, preferred_element_type=jnp.float32)

    def step(iteration, matrix):
        panel = lax.all_gather(matrix, ("col", "depth"), axis=1, tiled=True)
        squared = (mask(2 * iteration + 1) * product(panel, matrix)).astype(jnp.bfloat16)
        update = 1.5 * matrix.astype(jnp.float32) - 0.5 * product(panel, squared)
        return (mask(2 * iteration + 2) * update).astype(jnp.bfloat16)

    return lax.fori_loop(0, ITERS, step, (x_in * mask(0)).astype(jnp.bfloat16))


def on_device(x_in, patterns):
    of_line, of_group = picks(patterns[0])
    tiles = gather(x_in.reshape(8, BLOCK, BLOCK), "xz")
    tables = lists(patterns)

    def path(line_cap, group_cap):
        (line,) = pack(of_line, tiles, 8, (line_cap,))
        a, b = pack(of_group, gather(line, "yx"), LINE_CAP, (group_cap // 2, group_cap // 2))
        pieces = gather_halves(a, b, "zy")
        pieces += [lax.ppermute(piece, "col", [(c, c ^ 1) for c in range(8)]) for piece in pieces]
        return sparse_path(*tables, pieces)

    paths = [functools.partial(path, *sizes) for sizes in SIZES]
    return lax.switch(tables[3][STEPS, 0], paths + [lambda: dense_path(x_in, patterns)])


def solution(mesh):
    placed = (P("row", ("col", "depth")), P())
    return jax.shard_map(
        on_device, mesh=mesh, in_specs=placed, out_specs=P("row", ("col", "depth")), check_vma=False
    )
```

```python
import functools

import jax
import jax.numpy as jnp
from jax import lax
from jax.experimental import pallas as pl
from jax.experimental.pallas import tpu as pltpu
from jax.sharding import PartitionSpec as P

BLOCK = 128
ITERS = 3
NB = 32
AXES = ("row", "col", "depth")

SIZES = ((15, 42), (20, 52))
LINE_CAP, GROUP_CAP = SIZES[-1]
CAP = 400
ZERO = 8 * GROUP_CAP
DUMMY = ZERO + 1
TILE = DUMMY + 1
S_BASE = TILE + 8
X_BASE = S_BASE + CAP
SLOTS = X_BASE + CAP
TERMS = 16
POSITIONS = 512
ROWS = 1152
CLASSES = ((16, 2), (9, 4), (7, 8), (6, 8), (5, 16), (4, 24), (3, 32), (2, 32), (1, 32), (0, 32))
STEPS = 2 * ITERS


def pack_kernel(stride, pick_ref, *refs):
    sources, outs, blocks, sem = refs[:4], refs[4:-2], refs[-2], refs[-1]
    length = sources[0].shape[0]
    for index, source in enumerate(sources):
        pltpu.make_async_copy(source, blocks.at[pl.ds(index * stride, length)], sem).start()
    whole = blocks.at[pl.ds(0, 4 * length)]
    pltpu.make_async_copy(whole, whole, sem).wait()
    first = 0
    for out_ref in outs:
        for p in range(out_ref.shape[0]):
            out_ref[p] = blocks[pick_ref[first + p]]
        first += out_ref.shape[0]


def pack(pick, sources, stride, lengths):
    return pl.pallas_call(
        functools.partial(pack_kernel, stride),
        out_shape=[jax.ShapeDtypeStruct((length, BLOCK, BLOCK), jnp.bfloat16) for length in lengths],
        in_specs=[pl.BlockSpec(memory_space=pltpu.SMEM)] + [pl.BlockSpec(memory_space=pl.ANY)] * 4,
        out_specs=[pl.BlockSpec(memory_space=pltpu.VMEM)] * len(lengths),
        scratch_shapes=[pltpu.VMEM((4 * stride, BLOCK, BLOCK), jnp.bfloat16), pltpu.SemaphoreType.DMA(())],
        compiler_params=pltpu.CompilerParams(vmem_limit_bytes=16 * 2**20),
        name="pack_blocks",
    )(pick, *sources)


def product_kernel(*refs):
    tables, pieces, out_ref, blocks, sem = refs[:4], refs[4:20], refs[20], refs[21], refs[22]
    ent_ref, ox_ref, ord_ref, body_ref = refs[23:27]
    table_sem = refs[27]
    copies = [
        pltpu.make_async_copy(table, kept, table_sem.at[STEPS + index])
        for index, (table, kept) in enumerate(zip(tables[1:], refs[24:27]))
    ]

    def ent_copy(t):
        rows = pl.ds(t * TERMS, TERMS)
        return pltpu.make_async_copy(tables[0].at[rows], ent_ref.at[rows], table_sem.at[t])

    for copy in copies + [ent_copy(t) for t in range(STEPS)]:
        copy.start()
    half = pieces[0].shape[0]
    for index, piece in enumerate(pieces):
        first = index // 2 * GROUP_CAP + index % 2 * half
        pltpu.make_async_copy(piece, blocks.at[pl.ds(first, half)], sem).start()
    blocks[ZERO] = jnp.zeros((BLOCK, BLOCK), blocks.dtype)
    for b in range(8):
        blocks[TILE + b] = jnp.zeros((BLOCK, BLOCK), blocks.dtype)
    whole = blocks.at[pl.ds(0, len(pieces) * half)]
    pltpu.make_async_copy(whole, whole, sem).wait()
    for copy in copies:
        copy.wait()

    def load(slot):
        return blocks[slot]

    def step(t, carry):
        ent_copy(t).wait()
        is_update = (t & 1) == 1
        keep = jnp.where(is_update, 1.5, 0.0).astype(jnp.float32)
        scale = jnp.where(is_update, -0.5, 1.0).astype(jnp.float32)
        for index, (terms, width) in enumerate(CLASSES):
            first = body_ref[t, index * 2]
            count = body_ref[t, index * 2 + 1]

            def body(it, carry, terms=terms, width=width, first=first):
                results = []
                for u in range(width):
                    place = first + it * width + u
                    entry = ord_ref[t * 16 + (place >> 5), place & 31]
                    words = [ent_ref[t * TERMS + q, entry] for q in range(terms)]
                    lefts = [load(w & 0xFFFF) for w in words]
                    rights = [load(w >> 16) for w in words]
                    total = jnp.zeros((BLOCK, BLOCK), jnp.float32)
                    if terms == 1:
                        total = jnp.dot(lefts[0], rights[0], preferred_element_type=jnp.float32)
                    elif terms > 1:
                        left = jnp.concatenate(lefts, axis=1)
                        right = jnp.concatenate(rights, axis=0)
                        total = jnp.dot(left, right, preferred_element_type=jnp.float32)
                    ox = ox_ref[t, entry]
                    old = load(ox >> 16).astype(jnp.float32)
                    results.append((ox & 0xFFFF, (keep * old + scale * total).astype(jnp.bfloat16)))
                for slot, value in results:
                    blocks[slot] = value
                return carry

            lax.fori_loop(0, count, body, 0)
        return carry

    lax.fori_loop(0, STEPS, step, 0)
    copy = pltpu.make_async_copy(blocks.at[pl.ds(TILE, 8)], out_ref, sem)
    copy.start()
    copy.wait()


def ranks(mask):
    n = mask.shape[-1]
    before = (lax.iota(jnp.int32, n)[:, None] < lax.iota(jnp.int32, n)[None, :]).astype(jnp.bfloat16)
    flat = mask.reshape(-1, n).astype(jnp.bfloat16)
    return jnp.dot(flat, before, preferred_element_type=jnp.float32).astype(jnp.int32).reshape(mask.shape)


def lists_kernel(pattern_ref, ent_ref, ox_ref, ord_ref, body_ref, choice_ref, member_ref):
    f32, bf16, i32 = jnp.float32, jnp.bfloat16, jnp.int32
    row, col, my_y = (lax.axis_index(a) for a in AXES)
    my_column, my_core, my_z = col * 4 + my_y, col & 1, col >> 1
    flat_size = NB * NB

    def iota(shape, axis):
        return lax.broadcasted_iota(i32, shape, axis)

    def dot(a, b):
        return jnp.dot(a.astype(bf16), b.astype(bf16), preferred_element_type=f32)

    def split(v, axis):
        whole = v.astype(i32)
        return jnp.concatenate([(whole >> 4).astype(f32), (whole & 15).astype(f32)], axis=axis).astype(bf16)

    def join(v):
        return v[:NB] * 16.0 + v[NB:]

    i, j = iota((NB, NB), 0), iota((NB, NB), 1)
    below, above = (j < i).astype(f32), (i < j).astype(f32)
    o = iota((NB, flat_size), 1)
    of_row = ((o >> 5) == iota((NB, flat_size), 0)).astype(f32)
    of_col = ((o & 31) == iota((NB, flat_size), 0)).astype(f32)

    of_row16, of_col16 = of_row.astype(bf16), of_col.astype(bf16)

    def by_row(v):
        parts = lax.dot_general(split(v, 1), of_row16, (((0,), (0,)), ((), ())), preferred_element_type=f32)
        return join(parts)

    def by_col(v):
        return join(jnp.dot(split(v, 0), of_col16, preferred_element_type=f32))

    def flat(v):
        return (of_row * by_col(v)).sum(0, keepdims=True)

    def flat_mask(v):
        return (of_row * dot(v, of_col16)).sum(0, keepdims=True)

    pattern = [pattern_ref[t].astype(f32) for t in range(2 * ITERS + 1)]
    start = pattern[0]

    y, c, z = j & 3, (j >> 2) & 1, j >> 3
    y1, c1, z1 = i & 3, (i >> 2) & 1, i >> 3
    line = jnp.where(c == 0, z, y)
    along = jnp.where(c == 0, y, z)
    line1 = jnp.where(c1 == 0, z1, y1)
    along1 = jnp.where(c1 == 0, y1, z1)
    same = ((c1 == c) & (line1 == line)).astype(f32)
    sooner = same * (along1 < along).astype(f32)
    band = ((i >> 3) == (j >> 3)).astype(f32)
    band_below = ((j >> 3) < (i >> 3)).astype(f32)
    in_line = dot(start, same)
    sooner_in_line = dot(start, sooner)
    rank0 = sooner_in_line.sum(0, keepdims=True) + dot(below, start)
    rank1 = dot(band_below, in_line) + dot(band, sooner_in_line) + dot(below * band, start)
    back = (jnp.where(c == 0, my_z, my_y) - line) & 3
    piece = jnp.where(c == my_core, 0, 4) + back
    slot0 = piece.astype(f32) * GROUP_CAP + jnp.where(c == 0, rank0, rank1)
    slot0 = jnp.where(start > 0, slot0, float(ZERO))
    in_tiles = jnp.where(c == 0, start.sum(0, keepdims=True), dot(band, in_line))
    in_group = in_line.sum(0, keepdims=True)
    most_in_line = in_tiles.max(0, keepdims=True).max(1, keepdims=True)
    most_in_group = in_group.max(1, keepdims=True)
    fit = jnp.ones((1, 1), i32)

    mine = jnp.where(j == my_column, 1.0, 0.0)
    tile = mine * jnp.where((i >> 3) == row, 1.0, 0.0)
    outs = pattern[1:5] + [pattern[5] * mine, pattern[6] * tile]
    out_slot = []
    read_slot = []
    for t, base in enumerate((S_BASE, X_BASE, S_BASE, 0, S_BASE)):
        rank = dot(below, outs[t]).sum(1, keepdims=True) + dot(outs[t], above)
        out_slot.append(rank + float(base))
        read_slot.append(jnp.where(outs[t] > 0, out_slot[t], float(ZERO)))
        if t < 4:
            total = outs[t].sum(1, keepdims=True).sum(0, keepdims=True)
            fit = fit * jnp.where(total <= CAP, 1, 0)
    out_slot.append((TILE + (i & 7)).astype(f32))
    left = [slot0, slot0, read_slot[1], read_slot[1], read_slot[3], read_slot[3]]
    right = [slot0, read_slot[0], read_slot[1], read_slot[2], read_slot[3], read_slot[4]]

    blank = ZERO + ZERO * 65536
    low_limits = [limit for limit, _ in CLASSES[1:]] + [-1]
    count_classes = len(CLASSES)
    ent_ref[:, pl.ds(flat_size, ROWS - flat_size)] = jnp.full((STEPS * TERMS, ROWS - flat_size), blank, i32)
    ox_ref[:, pl.ds(flat_size, ROWS - flat_size)] = jnp.full((8, ROWS - flat_size), DUMMY + ZERO * 65536, i32)
    member_ref[...] = jnp.zeros(member_ref.shape, f32)
    lives = []
    for t in range(STEPS):
        terms = dot(pattern[t - t % 2], pattern[t]) * pattern[t + 1]
        most = terms.max(1, keepdims=True).max(0, keepdims=True)
        fit = fit * jnp.where(most <= TERMS, 1, 0)

        wide_left = by_row(left[t]).astype(i32)
        wide_right = by_col(right[t]).astype(i32)
        live = flat_mask(outs[t])
        lives.append(live)
        on = jnp.where((wide_left != ZERO) & (wide_right != ZERO), live, 0.0)
        place = jnp.where(on > 0, dot(below, on).astype(i32), TERMS)
        word = wide_left + wide_right * 65536 - blank
        for s in range(TERMS):
            found = jnp.where(place == s, word, 0).sum(0, keepdims=True)
            ent_ref[pl.ds(t * TERMS + s, 1), pl.ds(0, flat_size)] = found + blank
        slot = flat(out_slot[t]).astype(i32)
        old = flat(left[t]).astype(i32) if t % 2 else jnp.full((1, flat_size), ZERO, i32)
        ox_ref[pl.ds(t, 1), pl.ds(0, flat_size)] = slot + old * 65536
        count = on.sum(0, keepdims=True)
        for index, ((limit, _), low) in enumerate(zip(CLASSES, low_limits)):
            inside = (live > 0) & (count > low) & (count <= limit)
            member_ref[pl.ds(t * count_classes + index, 1), :] = jnp.where(inside, 1.0, 0.0)

    member = member_ref[...]
    earlier = (iota((BLOCK, BLOCK), 0) < iota((BLOCK, BLOCK), 1)).astype(f32)
    rank = []
    total = jnp.zeros((member.shape[0], 1), f32)
    for chunk in range(flat_size // BLOCK):
        part = member[:, chunk * BLOCK : (chunk + 1) * BLOCK]
        rank.append(dot(part, earlier) + total)
        total = total + part.sum(1, keepdims=True)
    rank = jnp.concatenate(rank, axis=1)
    o_wide = iota((16, flat_size), 1)
    number = jnp.concatenate([o_wide >> 5, o_wide & 31, jnp.ones((16, flat_size), i32)], axis=0).astype(f32)
    high = jnp.concatenate([iota((16, flat_size), 0)] * 3, axis=0)
    low = iota((32, flat_size), 0)
    lane = iota((1, 128), 1)
    for t in range(STEPS):
        position = jnp.zeros((1, flat_size), f32)
        ahead = jnp.zeros((1, 1), f32)
        end = jnp.zeros((1, 1), i32)
        body = jnp.zeros((1, 128), i32)
        for index, (_, width) in enumerate(CLASSES):
            at = t * count_classes + index
            position = position + member[at : at + 1] * (rank[at : at + 1] + ahead)
            ahead = ahead + total[at : at + 1]
            left_over = jnp.maximum(ahead.astype(i32) - end + (width - 1), 0)
            bodies = (left_over * -(-65536 // width)) >> 16
            body = jnp.where(lane == 2 * index, end, jnp.where(lane == 2 * index + 1, bodies, body))
            end = end + bodies * width
        body_ref[pl.ds(t, 1), :] = body
        position = jnp.where(lives[t] > 0, position, float(POSITIONS)).astype(i32)
        by_high = jnp.where(high == (position >> 5), number, 0.0)
        by_low = jnp.where(low == (position & 31), 1.0, 0.0)
        found = lax.dot_general(
            by_high.astype(bf16), by_low.astype(bf16), (((1,), (1,)), ((), ())), preferred_element_type=f32
        )
        entry = jnp.where(found[32:48] > 0, found[0:16] * float(NB) + found[16:32], float(flat_size))
        ord_ref[pl.ds(t * 16, 16), pl.ds(0, 32)] = entry.astype(i32)
    choice = jnp.zeros((1, 1), i32)
    for line_cap, group_cap in SIZES:
        inside = (most_in_line <= line_cap) & (most_in_group <= group_cap)
        choice = choice + 1 - fit * jnp.where(inside, 1, 0)
    choice_ref[0] = jnp.max(choice)


def lists(patterns):
    return pl.pallas_call(
        lists_kernel,
        out_shape=[
            jax.ShapeDtypeStruct((STEPS * TERMS, ROWS), jnp.int32),
            jax.ShapeDtypeStruct((8, ROWS), jnp.int32),
            jax.ShapeDtypeStruct((STEPS * 16, 128), jnp.int32),
            jax.ShapeDtypeStruct((8, 128), jnp.int32),
            jax.ShapeDtypeStruct((1,), jnp.int32),
        ],
        in_specs=[pl.BlockSpec(memory_space=pltpu.VMEM)],
        out_specs=[pl.BlockSpec(memory_space=pltpu.VMEM)] * 4 + [pl.BlockSpec(memory_space=pltpu.SMEM)],
        scratch_shapes=[pltpu.VMEM((-(-STEPS * len(CLASSES) // 8) * 8, NB * NB), jnp.float32)],
        compiler_params=pltpu.CompilerParams(vmem_limit_bytes=24 * 2**20),
        name="build_lists",
    )(patterns)


def my_place():
    row, col, depth = (lax.axis_index(a) for a in AXES)
    return row, col * 4 + depth, (col % 2, col // 2, depth)


def picked(mask, value, slots):
    place = jnp.where(mask > 0, ranks(mask[None])[0], slots)
    hit = place[None, :] == lax.iota(jnp.int32, slots)[:, None]
    return jnp.where(hit, value[None, :], 0).sum(-1)


def picks(pattern):
    x, _, (core, z, y) = my_place()
    by_place = pattern.reshape(4, 8, 4, 2, 4)
    lines0 = lax.dynamic_index_in_dim(by_place[:, :, :, 0], z, 2, keepdims=False).transpose(2, 0, 1)
    lines1 = lax.dynamic_index_in_dim(by_place[:, :, :, 1], y, 3, keepdims=False).transpose(0, 2, 1)
    lines = jnp.where(core == 0, lines0, lines1).reshape(4, 32)
    at1, at2 = jnp.where(core == 0, x, z), jnp.where(core == 0, y, x)
    e = lax.iota(jnp.int32, 32)
    line = lax.dynamic_index_in_dim(lines, at2, 0, keepdims=False)
    of_line = picked(line, ((at1 - e // 8) & 3) * 8 + e % 8, LINE_CAP)
    back = (at2 - lax.iota(jnp.int32, 4)) & 3
    value = back[:, None] * LINE_CAP + jnp.minimum(ranks(lines), LINE_CAP - 1)
    of_group = picked(lines.reshape(4 * 32), value.reshape(4 * 32), GROUP_CAP)
    return of_line, of_group


def hops(axes, shift):
    pairs = []
    for x in range(4):
        for z in range(4):
            for c in range(2):
                for y in range(4):
                    to = {"x": x, "y": y, "z": z}
                    to[axes[c]] = (to[axes[c]] + shift) % 4
                    pairs.append((((x * 4 + z) * 2 + c) * 4 + y, ((to["x"] * 4 + to["z"]) * 2 + c) * 4 + to["y"]))
    return pairs


def send(mine, axes, shift):
    return lax.ppermute(mine, AXES, hops(axes, shift))


def gather(mine, axes):
    far = {shift: send(mine, axes, shift) for shift in (1, 3, 2)}
    return [mine, far[1], far[2], far[3]]


def gather_halves(a, b, axes):
    a1, b3 = send(a, axes, 1), send(b, axes, 3)
    late_a, a1 = lax.optimization_barrier((a, a1))
    b1, a3 = send(b, axes, 1), send(late_a, axes, 3)
    a2, b2 = send(a1, axes, 1), send(b3, axes, 3)
    return [a, b, a1, b1, a2, b2, a3, b3]


def sparse_path(ent, ox, entry, body, pieces):
    out = pl.pallas_call(
        product_kernel,
        out_shape=jax.ShapeDtypeStruct((8, BLOCK, BLOCK), jnp.bfloat16),
        in_specs=[pl.BlockSpec(memory_space=pl.ANY)] * 20,
        out_specs=pl.BlockSpec(memory_space=pl.ANY),
        scratch_shapes=[pltpu.VMEM((SLOTS, BLOCK, BLOCK), jnp.bfloat16), pltpu.SemaphoreType.DMA(())]
        + [pltpu.SMEM(table.shape, jnp.int32) for table in (ent, ox, entry, body)]
        + [pltpu.SemaphoreType.DMA((STEPS + 3,))],
        compiler_params=pltpu.CompilerParams(vmem_limit_bytes=56 * 2**20),
        name="block_products",
    )(ent, ox, entry, body, *pieces)
    return out.reshape(8 * BLOCK, BLOCK)


def tile_mask(pattern, row_first, col_first, tile_rows, tile_cols):
    blocks = pattern.shape[0]
    slab = lax.dynamic_slice_in_dim(pattern, row_first // BLOCK, tile_rows // BLOCK, 0).astype(jnp.float32)
    col_block = (col_first + lax.iota(jnp.int32, tile_cols)) // BLOCK
    onehot = (col_block[None, :] == lax.iota(jnp.int32, blocks)[:, None]).astype(jnp.float32)
    coarse = jnp.dot(slab, onehot)
    spread_rows = jnp.broadcast_to(coarse[:, None, :], (tile_rows // BLOCK, BLOCK, tile_cols))
    return spread_rows.reshape(tile_rows, tile_cols)


def dense_path(x_in, patterns):
    tile_rows, tile_width = x_in.shape
    row_first = lax.axis_index("row") * tile_rows
    col_first = (lax.axis_index("col") * lax.axis_size("depth") + lax.axis_index("depth")) * tile_width

    def mask(index):
        pattern = lax.dynamic_index_in_dim(patterns, index, 0, keepdims=False)
        return tile_mask(pattern, row_first, col_first, tile_rows, tile_width)

    def product(panel, right):
        column = lax.all_gather(right, "row", axis=0, tiled=True)
        return jnp.dot(panel, column, preferred_element_type=jnp.float32)

    def step(iteration, matrix):
        panel = lax.all_gather(matrix, ("col", "depth"), axis=1, tiled=True)
        squared = (mask(2 * iteration + 1) * product(panel, matrix)).astype(jnp.bfloat16)
        update = 1.5 * matrix.astype(jnp.float32) - 0.5 * product(panel, squared)
        return (mask(2 * iteration + 2) * update).astype(jnp.bfloat16)

    return lax.fori_loop(0, ITERS, step, (x_in * mask(0)).astype(jnp.bfloat16))


def on_device(x_in, patterns):
    of_line, _ = picks(patterns[0])
    tiles = gather(x_in.reshape(8, BLOCK, BLOCK), "xz")
    *tables, choice = lists(patterns)

    def path(line_cap, group_cap):
        (line,) = pack(of_line, tiles, 8, (line_cap,))
        lines = gather(line, "yx")
        lines[1], late = lax.optimization_barrier((lines[1], patterns[0]))
        _, of_group = picks(late)
        a, b = pack(of_group, lines, LINE_CAP, (group_cap // 2, group_cap // 2))
        pieces = gather_halves(a, b, "zy")
        pieces += [lax.ppermute(piece, "col", [(c, c ^ 1) for c in range(8)]) for piece in pieces]
        return sparse_path(*tables, pieces)

    paths = [functools.partial(path, *sizes) for sizes in SIZES]
    return lax.switch(choice[0], paths + [lambda: dense_path(x_in, patterns)])


def solution(mesh):
    placed = (P("row", ("col", "depth")), P())
    return jax.shard_map(
        on_device, mesh=mesh, in_specs=placed, out_specs=P("row", ("col", "depth")), check_vma=False
    )
```

```python
import functools

import jax
import jax.numpy as jnp
from jax import lax
from jax.experimental import pallas as pl
from jax.experimental.pallas import tpu as pltpu
from jax.sharding import PartitionSpec as P

BLOCK = 128
ITERS = 3
NB = 32
AXES = ("row", "col", "depth")

SIZES = ((15, 42), (20, 52))
LINE_CAP, GROUP_CAP = SIZES[-1]
CAP = 400
ZERO = 8 * GROUP_CAP
DUMMY = ZERO + 1
TILE = DUMMY + 1
S_BASE = TILE + 8
X_BASE = S_BASE + CAP
SLOTS = X_BASE + CAP
TERMS = 16
POSITIONS = 512
ROWS = 1152
CLASSES = ((16, 2), (9, 4), (7, 8), (6, 8), (5, 16), (4, 24), (3, 32), (2, 32), (1, 32), (0, 32))
STEPS = 2 * ITERS


def pack_kernel(stride, pick_ref, *refs):
    sources, outs, blocks, sem = refs[:4], refs[4:-2], refs[-2], refs[-1]
    length = sources[0].shape[0]
    for index, source in enumerate(sources):
        pltpu.make_async_copy(source, blocks.at[pl.ds(index * stride, length)], sem).start()
    whole = blocks.at[pl.ds(0, 4 * length)]
    pltpu.make_async_copy(whole, whole, sem).wait()
    first = 0
    for out_ref in outs:
        for p in range(out_ref.shape[0]):
            out_ref[p] = blocks[pick_ref[first + p]]
        first += out_ref.shape[0]


def pack(pick, sources, stride, lengths):
    return pl.pallas_call(
        functools.partial(pack_kernel, stride),
        out_shape=[jax.ShapeDtypeStruct((length, BLOCK, BLOCK), jnp.bfloat16) for length in lengths],
        in_specs=[pl.BlockSpec(memory_space=pltpu.SMEM)] + [pl.BlockSpec(memory_space=pl.ANY)] * 4,
        out_specs=[pl.BlockSpec(memory_space=pltpu.VMEM)] * len(lengths),
        scratch_shapes=[pltpu.VMEM((4 * stride, BLOCK, BLOCK), jnp.bfloat16), pltpu.SemaphoreType.DMA(())],
        compiler_params=pltpu.CompilerParams(vmem_limit_bytes=16 * 2**20),
        name="pack_blocks",
    )(pick, *sources)


def product_kernel(*refs):
    tables, pieces, out_ref, blocks, sem = refs[:4], refs[4:20], refs[20], refs[21], refs[22]
    ent_ref, ox_ref, ord_ref, body_ref = refs[23:27]
    table_sem = refs[27]
    copies = [
        pltpu.make_async_copy(table, kept, table_sem.at[STEPS + index])
        for index, (table, kept) in enumerate(zip(tables[1:], refs[24:27]))
    ]

    def ent_copy(t):
        rows = pl.ds(t * TERMS, TERMS)
        return pltpu.make_async_copy(tables[0].at[rows], ent_ref.at[rows], table_sem.at[t])

    half = pieces[0].shape[0]
    for index, piece in enumerate(pieces):
        first = index // 2 * GROUP_CAP + index % 2 * half
        pltpu.make_async_copy(piece, blocks.at[pl.ds(first, half)], sem).start()
    for copy in copies + [ent_copy(t) for t in range(STEPS)]:
        copy.start()
    blocks[ZERO] = jnp.zeros((BLOCK, BLOCK), blocks.dtype)
    for b in range(8):
        blocks[TILE + b] = jnp.zeros((BLOCK, BLOCK), blocks.dtype)
    whole = blocks.at[pl.ds(0, len(pieces) * half)]
    pltpu.make_async_copy(whole, whole, sem).wait()
    for copy in copies:
        copy.wait()

    def load(slot):
        return blocks[slot]

    def step(t, carry):
        ent_copy(t).wait()
        is_update = (t & 1) == 1
        keep = jnp.where(is_update, 1.5, 0.0).astype(jnp.float32)
        scale = jnp.where(is_update, -0.5, 1.0).astype(jnp.float32)
        for index, (terms, width) in enumerate(CLASSES):
            first = body_ref[t, index * 2]
            count = body_ref[t, index * 2 + 1]

            def body(it, carry, terms=terms, width=width, first=first):
                results = []
                for u in range(width):
                    place = first + it * width + u
                    entry = ord_ref[t * 16 + (place >> 5), place & 31]
                    words = [ent_ref[t * TERMS + q, entry] for q in range(terms)]
                    lefts = [load(w & 0xFFFF) for w in words]
                    rights = [load(w >> 16) for w in words]
                    total = jnp.zeros((BLOCK, BLOCK), jnp.float32)
                    if terms == 1:
                        total = jnp.dot(lefts[0], rights[0], preferred_element_type=jnp.float32)
                    elif terms > 1:
                        left = jnp.concatenate(lefts, axis=1)
                        right = jnp.concatenate(rights, axis=0)
                        total = jnp.dot(left, right, preferred_element_type=jnp.float32)
                    ox = ox_ref[t, entry]
                    old = load(ox >> 16).astype(jnp.float32)
                    results.append((ox & 0xFFFF, (keep * old + scale * total).astype(jnp.bfloat16)))
                for slot, value in results:
                    blocks[slot] = value
                return carry

            lax.fori_loop(0, count, body, 0)
        return carry

    lax.fori_loop(0, STEPS, step, 0)
    copy = pltpu.make_async_copy(blocks.at[pl.ds(TILE, 8)], out_ref, sem)
    copy.start()
    copy.wait()


def ranks(mask):
    n = mask.shape[-1]
    before = (lax.iota(jnp.int32, n)[:, None] < lax.iota(jnp.int32, n)[None, :]).astype(jnp.bfloat16)
    flat = mask.reshape(-1, n).astype(jnp.bfloat16)
    return jnp.dot(flat, before, preferred_element_type=jnp.float32).astype(jnp.int32).reshape(mask.shape)


def lists_kernel(pattern_ref, ent_ref, ox_ref, ord_ref, body_ref, choice_ref, member_ref):
    f32, bf16, i32 = jnp.float32, jnp.bfloat16, jnp.int32
    row, col, my_y = (lax.axis_index(a) for a in AXES)
    my_column, my_core, my_z = col * 4 + my_y, col & 1, col >> 1
    flat_size = NB * NB

    def iota(shape, axis):
        return lax.broadcasted_iota(i32, shape, axis)

    def dot(a, b):
        return jnp.dot(a.astype(bf16), b.astype(bf16), preferred_element_type=f32)

    def split(v, axis):
        whole = v.astype(i32)
        return jnp.concatenate([(whole >> 4).astype(f32), (whole & 15).astype(f32)], axis=axis).astype(bf16)

    def join(v):
        return v[:NB] * 16.0 + v[NB:]

    i, j = iota((NB, NB), 0), iota((NB, NB), 1)
    below, above = (j < i).astype(f32), (i < j).astype(f32)
    o = iota((NB, flat_size), 1)
    of_row = ((o >> 5) == iota((NB, flat_size), 0)).astype(f32)
    of_col = ((o & 31) == iota((NB, flat_size), 0)).astype(f32)

    of_row16, of_col16 = of_row.astype(bf16), of_col.astype(bf16)

    def by_row(v):
        parts = lax.dot_general(split(v, 1), of_row16, (((0,), (0,)), ((), ())), preferred_element_type=f32)
        return join(parts)

    def by_col(v):
        return join(jnp.dot(split(v, 0), of_col16, preferred_element_type=f32))

    def flat(v):
        return (of_row * by_col(v)).sum(0, keepdims=True)

    def flat_mask(v):
        return (of_row * dot(v, of_col16)).sum(0, keepdims=True)

    pattern = [pattern_ref[t].astype(f32) for t in range(2 * ITERS + 1)]
    start = pattern[0]

    y, c, z = j & 3, (j >> 2) & 1, j >> 3
    y1, c1, z1 = i & 3, (i >> 2) & 1, i >> 3
    line = jnp.where(c == 0, z, y)
    along = jnp.where(c == 0, y, z)
    line1 = jnp.where(c1 == 0, z1, y1)
    along1 = jnp.where(c1 == 0, y1, z1)
    same = ((c1 == c) & (line1 == line)).astype(f32)
    sooner = same * (along1 < along).astype(f32)
    band = ((i >> 3) == (j >> 3)).astype(f32)
    band_below = ((j >> 3) < (i >> 3)).astype(f32)
    in_line = dot(start, same)
    sooner_in_line = dot(start, sooner)
    rank0 = sooner_in_line.sum(0, keepdims=True) + dot(below, start)
    rank1 = dot(band_below, in_line) + dot(band, sooner_in_line) + dot(below * band, start)
    back = (jnp.where(c == 0, my_z, my_y) - line) & 3
    piece = jnp.where(c == my_core, 0, 4) + back
    slot0 = piece.astype(f32) * GROUP_CAP + jnp.where(c == 0, rank0, rank1)
    slot0 = jnp.where(start > 0, slot0, float(ZERO))
    in_tiles = jnp.where(c == 0, start.sum(0, keepdims=True), dot(band, in_line))
    in_group = in_line.sum(0, keepdims=True)
    most_in_line = in_tiles.max(0, keepdims=True).max(1, keepdims=True)
    most_in_group = in_group.max(1, keepdims=True)
    fit = jnp.ones((1, 1), i32)

    mine = jnp.where(j == my_column, 1.0, 0.0)
    tile = mine * jnp.where((i >> 3) == row, 1.0, 0.0)
    outs = pattern[1:5] + [pattern[5] * mine, pattern[6] * tile]
    out_slot = []
    read_slot = []
    for t, base in enumerate((S_BASE, X_BASE, S_BASE, 0, S_BASE)):
        rank = dot(below, outs[t]).sum(1, keepdims=True) + dot(outs[t], above)
        out_slot.append(rank + float(base))
        read_slot.append(jnp.where(outs[t] > 0, out_slot[t], float(ZERO)))
        if t < 4:
            total = outs[t].sum(1, keepdims=True).sum(0, keepdims=True)
            fit = fit * jnp.where(total <= CAP, 1, 0)
    out_slot.append((TILE + (i & 7)).astype(f32))
    left = [slot0, slot0, read_slot[1], read_slot[1], read_slot[3], read_slot[3]]
    right = [slot0, read_slot[0], read_slot[1], read_slot[2], read_slot[3], read_slot[4]]

    blank = ZERO + ZERO * 65536
    low_limits = [limit for limit, _ in CLASSES[1:]] + [-1]
    count_classes = len(CLASSES)
    ent_ref[:, pl.ds(flat_size, ROWS - flat_size)] = jnp.full((STEPS * TERMS, ROWS - flat_size), blank, i32)
    ox_ref[:, pl.ds(flat_size, ROWS - flat_size)] = jnp.full((8, ROWS - flat_size), DUMMY + ZERO * 65536, i32)
    member_ref[...] = jnp.zeros(member_ref.shape, f32)
    lives = []
    for t in range(STEPS):
        terms = dot(pattern[t - t % 2], pattern[t]) * pattern[t + 1]
        most = terms.max(1, keepdims=True).max(0, keepdims=True)
        fit = fit * jnp.where(most <= TERMS, 1, 0)

        wide_left = by_row(left[t]).astype(i32)
        wide_right = by_col(right[t]).astype(i32)
        live = flat_mask(outs[t])
        lives.append(live)
        on = jnp.where((wide_left != ZERO) & (wide_right != ZERO), live, 0.0)
        place = jnp.where(on > 0, dot(below, on).astype(i32), TERMS)
        word = wide_left + wide_right * 65536 - blank
        for s in range(TERMS):
            found = jnp.where(place == s, word, 0).sum(0, keepdims=True)
            ent_ref[pl.ds(t * TERMS + s, 1), pl.ds(0, flat_size)] = found + blank
        slot = flat(out_slot[t]).astype(i32)
        old = flat(left[t]).astype(i32) if t % 2 else jnp.full((1, flat_size), ZERO, i32)
        ox_ref[pl.ds(t, 1), pl.ds(0, flat_size)] = slot + old * 65536
        count = on.sum(0, keepdims=True)
        for index, ((limit, _), low) in enumerate(zip(CLASSES, low_limits)):
            inside = (live > 0) & (count > low) & (count <= limit)
            member_ref[pl.ds(t * count_classes + index, 1), :] = jnp.where(inside, 1.0, 0.0)

    member = member_ref[...]
    earlier = (iota((BLOCK, BLOCK), 0) < iota((BLOCK, BLOCK), 1)).astype(f32)
    rank = []
    total = jnp.zeros((member.shape[0], 1), f32)
    for chunk in range(flat_size // BLOCK):
        part = member[:, chunk * BLOCK : (chunk + 1) * BLOCK]
        rank.append(dot(part, earlier) + total)
        total = total + part.sum(1, keepdims=True)
    rank = jnp.concatenate(rank, axis=1)
    o_wide = iota((16, flat_size), 1)
    number = jnp.concatenate([o_wide >> 5, o_wide & 31, jnp.ones((16, flat_size), i32)], axis=0).astype(f32)
    high = jnp.concatenate([iota((16, flat_size), 0)] * 3, axis=0)
    low = iota((32, flat_size), 0)
    lane = iota((1, 128), 1)
    for t in range(STEPS):
        position = jnp.zeros((1, flat_size), f32)
        ahead = jnp.zeros((1, 1), f32)
        end = jnp.zeros((1, 1), i32)
        body = jnp.zeros((1, 128), i32)
        for index, (_, width) in enumerate(CLASSES):
            at = t * count_classes + index
            position = position + member[at : at + 1] * (rank[at : at + 1] + ahead)
            ahead = ahead + total[at : at + 1]
            left_over = jnp.maximum(ahead.astype(i32) - end + (width - 1), 0)
            bodies = (left_over * -(-65536 // width)) >> 16
            body = jnp.where(lane == 2 * index, end, jnp.where(lane == 2 * index + 1, bodies, body))
            end = end + bodies * width
        body_ref[pl.ds(t, 1), :] = body
        position = jnp.where(lives[t] > 0, position, float(POSITIONS)).astype(i32)
        by_high = jnp.where(high == (position >> 5), number, 0.0)
        by_low = jnp.where(low == (position & 31), 1.0, 0.0)
        found = lax.dot_general(
            by_high.astype(bf16), by_low.astype(bf16), (((1,), (1,)), ((), ())), preferred_element_type=f32
        )
        entry = jnp.where(found[32:48] > 0, found[0:16] * float(NB) + found[16:32], float(flat_size))
        ord_ref[pl.ds(t * 16, 16), pl.ds(0, 32)] = entry.astype(i32)
    choice = jnp.zeros((1, 1), i32)
    for line_cap, group_cap in SIZES:
        inside = (most_in_line <= line_cap) & (most_in_group <= group_cap)
        choice = choice + 1 - fit * jnp.where(inside, 1, 0)
    choice_ref[0] = jnp.max(choice)


def lists(patterns):
    return pl.pallas_call(
        lists_kernel,
        out_shape=[
            jax.ShapeDtypeStruct((STEPS * TERMS, ROWS), jnp.int32),
            jax.ShapeDtypeStruct((8, ROWS), jnp.int32),
            jax.ShapeDtypeStruct((STEPS * 16, 128), jnp.int32),
            jax.ShapeDtypeStruct((8, 128), jnp.int32),
            jax.ShapeDtypeStruct((1,), jnp.int32),
        ],
        in_specs=[pl.BlockSpec(memory_space=pltpu.VMEM)],
        out_specs=[pl.BlockSpec(memory_space=pltpu.VMEM)] * 4 + [pl.BlockSpec(memory_space=pltpu.SMEM)],
        scratch_shapes=[pltpu.VMEM((-(-STEPS * len(CLASSES) // 8) * 8, NB * NB), jnp.float32)],
        compiler_params=pltpu.CompilerParams(vmem_limit_bytes=24 * 2**20),
        name="build_lists",
    )(patterns)


def my_place():
    row, col, depth = (lax.axis_index(a) for a in AXES)
    return row, col * 4 + depth, (col % 2, col // 2, depth)


def picked(mask, value, slots):
    place = jnp.where(mask > 0, ranks(mask[None])[0], slots)
    hit = place[None, :] == lax.iota(jnp.int32, slots)[:, None]
    return jnp.where(hit, value[None, :], 0).sum(-1)


def picks(pattern):
    x, _, (core, z, y) = my_place()
    by_place = pattern.reshape(4, 8, 4, 2, 4)
    lines0 = lax.dynamic_index_in_dim(by_place[:, :, :, 0], z, 2, keepdims=False).transpose(2, 0, 1)
    lines1 = lax.dynamic_index_in_dim(by_place[:, :, :, 1], y, 3, keepdims=False).transpose(0, 2, 1)
    lines = jnp.where(core == 0, lines0, lines1).reshape(4, 32)
    at1, at2 = jnp.where(core == 0, x, z), jnp.where(core == 0, y, x)
    e = lax.iota(jnp.int32, 32)
    line = lax.dynamic_index_in_dim(lines, at2, 0, keepdims=False)
    of_line = picked(line, ((at1 - e // 8) & 3) * 8 + e % 8, LINE_CAP)
    back = (at2 - lax.iota(jnp.int32, 4)) & 3
    value = back[:, None] * LINE_CAP + jnp.minimum(ranks(lines), LINE_CAP - 1)
    of_group = picked(lines.reshape(4 * 32), value.reshape(4 * 32), GROUP_CAP)
    return of_line, of_group


def hops(axes, shift):
    pairs = []
    for x in range(4):
        for z in range(4):
            for c in range(2):
                for y in range(4):
                    to = {"x": x, "y": y, "z": z}
                    to[axes[c]] = (to[axes[c]] + shift) % 4
                    pairs.append((((x * 4 + z) * 2 + c) * 4 + y, ((to["x"] * 4 + to["z"]) * 2 + c) * 4 + to["y"]))
    return pairs


def send(mine, axes, shift):
    return lax.ppermute(mine, AXES, hops(axes, shift))


def gather(mine, axes):
    far = {shift: send(mine, axes, shift) for shift in (1, 3, 2)}
    return [mine, far[1], far[2], far[3]]


def gather_halves(a, b, axes):
    a1, b3 = send(a, axes, 1), send(b, axes, 3)
    late_a, a1 = lax.optimization_barrier((a, a1))
    b1, a3 = send(b, axes, 1), send(late_a, axes, 3)
    a2, b2 = send(a1, axes, 1), send(b3, axes, 3)
    return [a, b, a1, b1, a2, b2, a3, b3]


def sparse_path(ent, ox, entry, body, pieces):
    out = pl.pallas_call(
        product_kernel,
        out_shape=jax.ShapeDtypeStruct((8, BLOCK, BLOCK), jnp.bfloat16),
        in_specs=[pl.BlockSpec(memory_space=pl.ANY)] * 20,
        out_specs=pl.BlockSpec(memory_space=pl.ANY),
        scratch_shapes=[pltpu.VMEM((SLOTS, BLOCK, BLOCK), jnp.bfloat16), pltpu.SemaphoreType.DMA(())]
        + [pltpu.SMEM(table.shape, jnp.int32) for table in (ent, ox, entry, body)]
        + [pltpu.SemaphoreType.DMA((STEPS + 3,))],
        compiler_params=pltpu.CompilerParams(vmem_limit_bytes=44 * 2**20),
        name="block_products",
    )(ent, ox, entry, body, *pieces)
    return out.reshape(8 * BLOCK, BLOCK)


def tile_mask(pattern, row_first, col_first, tile_rows, tile_cols):
    blocks = pattern.shape[0]
    slab = lax.dynamic_slice_in_dim(pattern, row_first // BLOCK, tile_rows // BLOCK, 0).astype(jnp.float32)
    col_block = (col_first + lax.iota(jnp.int32, tile_cols)) // BLOCK
    onehot = (col_block[None, :] == lax.iota(jnp.int32, blocks)[:, None]).astype(jnp.float32)
    coarse = jnp.dot(slab, onehot)
    spread_rows = jnp.broadcast_to(coarse[:, None, :], (tile_rows // BLOCK, BLOCK, tile_cols))
    return spread_rows.reshape(tile_rows, tile_cols)


def dense_path(x_in, patterns):
    tile_rows, tile_width = x_in.shape
    row_first = lax.axis_index("row") * tile_rows
    col_first = (lax.axis_index("col") * lax.axis_size("depth") + lax.axis_index("depth")) * tile_width

    def mask(index):
        pattern = lax.dynamic_index_in_dim(patterns, index, 0, keepdims=False)
        return tile_mask(pattern, row_first, col_first, tile_rows, tile_width)

    def product(panel, right):
        column = lax.all_gather(right, "row", axis=0, tiled=True)
        return jnp.dot(panel, column, preferred_element_type=jnp.float32)

    def step(iteration, matrix):
        panel = lax.all_gather(matrix, ("col", "depth"), axis=1, tiled=True)
        squared = (mask(2 * iteration + 1) * product(panel, matrix)).astype(jnp.bfloat16)
        update = 1.5 * matrix.astype(jnp.float32) - 0.5 * product(panel, squared)
        return (mask(2 * iteration + 2) * update).astype(jnp.bfloat16)

    return lax.fori_loop(0, ITERS, step, (x_in * mask(0)).astype(jnp.bfloat16))


def on_device(x_in, patterns):
    of_line, _ = picks(patterns[0])
    tiles = gather(x_in.reshape(8, BLOCK, BLOCK), "xz")
    *tables, choice = lists(patterns)

    def path(line_cap, group_cap):
        (line,) = pack(of_line, tiles, 8, (line_cap,))
        lines = gather(line, "yx")
        lines[1], late = lax.optimization_barrier((lines[1], patterns[0]))
        _, of_group = picks(late)
        a, b = pack(of_group, lines, LINE_CAP, (group_cap // 2, group_cap // 2))
        pieces = gather_halves(a, b, "zy")
        pieces += [lax.ppermute(piece, "col", [(c, c ^ 1) for c in range(8)]) for piece in pieces]
        return sparse_path(*tables, pieces)

    paths = [functools.partial(path, *sizes) for sizes in SIZES]
    return lax.switch(choice[0], paths + [lambda: dense_path(x_in, patterns)])


def solution(mesh):
    placed = (P("row", ("col", "depth")), P())
    return jax.shard_map(
        on_device, mesh=mesh, in_specs=placed, out_specs=P("row", ("col", "depth")), check_vma=False
    )
```
